32 devices in a mesh: groups: 2 (over x), ctx: 8 (over z, y), exp: 2 (over core).
Axes of the slice: x: 2, y: 2, z: 4, core: 2. Of those that a mesh axis runs over, the one named last changes fastest.
Arguments:
- tokens: bfloat16 [4096, 2048], P(('groups', 'ctx', 'exp')), parts along dimension 0, may hold values from -6 to 152
- norm_gain: float32 [2048], replicated, may hold values from 0.1 to 1.9
- router_weight: float32 [2048, 8], replicated, may hold values from -0.125 to 5.1
- routes: int32 [4096, 2], P(('groups', 'ctx', 'exp')), parts along dimension 0, may hold values from 0 to 7, all different within a row; in each aligned block of 128 rows (0 to 127, 128 to 255, ...) at most 40 rows name the same one
- key_weight: bfloat16 [2048, 1024], replicated, may hold values from -0.125 to 0.125
- value_weight: bfloat16 [2048, 1024], replicated, may hold values from -0.125 to 0.125
- query_weight: bfloat16 [8, 2048, 1024], P('ctx'), may hold values from -0.125 to 0.125
- output_weight: bfloat16 [8, 1024, 2048], P('ctx'), may hold values from -3 to 3
Outputs:
- attention_out: bfloat16 [4096, 2048], P(('groups', 'ctx', 'exp')), parts along dimension 0
The draws below stay inside these ranges and needn't reach their ends.
There are 2 independent parts, one for each index of `groups`. The reference program is written for one: setup_inputs(seed, part) draws one part's arguments, and reference() takes and returns one part's arrays. A program takes and returns all parts, laid end to end along the dimension named above; an argument that names none is the same for every part. Nothing has to cross between parts.
Inputs may be any that keep to these rules, and one draw needn't show every extreme that they name: `routes`: each row names 2 different experts; among the 128 rows of one device no expert is named more than 40 times, a bound that some block reaches.
All inputs are finite; a program needn't handle non-finite values.
Results may differ from the reference program's by a relative error of at most 0.006.
The reference program's roundings to bfloat16 on the way count: a program that leaves them out, or rounds other values in their place, can miss the bound.
Values may be sent and summed in bfloat16 or wider, within the bound.
No kernel may reach another device: no remote copies, remote signals or barrier semaphores. Data moves between devices by JAX's collectives and lax.ppermute only.
A program may use at most 128 MiB of HBM per device.

```python
import math
import jax
import jax.numpy as jnp
import numpy as np
from jax import lax

D = 2048
HEADS = 8
HS = 128
EXPERTS = 8
TOPK = 2
TOK_DEV = 128
MOST = 40
LENGTH = 2048
QUARTERS = 1
HPD = 8


def drawn_weight(key, shape):
    return jnp.clip(jax.random.normal(key, shape, jnp.float32) * D ** (-0.5), -0.125, 0.125)


def draw_tokens(key, part):
    key = jax.random.fold_in(key, 11)
    drawn = jnp.clip(jax.random.normal(key, (LENGTH, D), jnp.float32), -6.0, 6.0)
    return drawn.astype(jnp.bfloat16)


def draw_router_weight(key, part):
    key = jax.random.fold_in(key, 31)
    drawn = drawn_weight(key, (D, EXPERTS))
    return drawn


def draw_key_weight(key, part):
    key = jax.random.fold_in(key, 23)
    drawn = drawn_weight(key, (D, HEADS * HS))
    return drawn.astype(jnp.bfloat16)


def draw_query_weight(key, part):
    key = jax.random.fold_in(key, 29)
    drawn = drawn_weight(key, (EXPERTS * QUARTERS, D, HPD * HS))
    return drawn.astype(jnp.bfloat16)


def shard_levels(own_key, shape, split, least, top_value):
    loudness, own = 1.0, jax.random.fold_in(own_key, 6)
    for axis_at, shards_of in split:
        steps = jnp.exp(jax.random.uniform(jax.random.fold_in(own, axis_at), (shards_of,), jnp.float32, least / len(split), top_value / len(split)))
        loudness = loudness * jnp.repeat(steps, shape[axis_at] // shards_of).reshape([-1 if axis == axis_at else 1 for axis in range(len(shape))])
    return loudness


def assign_block(rng, own, number, rows, count, top, most, lean):
    ranking = jax.random.permutation(rng, count)
    crowded, usual = portions_of(count, rows * top, most, lean, True), portions_of(count, rows * top, most, lean, False)
    places = jnp.arange(count)

    def named(sizes, rotation):
        used = int((sizes > 0).sum())
        fixed = max(1, used // 4)
        moved = fixed + (places - fixed + rotation * (used - fixed)) % max(1, count - fixed)
        return jnp.zeros((count,), jnp.int32).at[ranking[jnp.where(places < fixed, places, moved)]].set(jnp.asarray(sizes, jnp.int32))

    sizes = jnp.where(number % 4 == 0, named(crowded, number // 4), named(usual, number - number // 4 - 1))
    mixed = jax.random.permutation(jax.random.fold_in(own, 3), count)
    donor, receiver = mixed[0:count // 2 * 2:2], mixed[1:count // 2 * 2:2]
    slack = jnp.minimum(sizes[donor] - 1, most - sizes[receiver]) // 2
    slack = jnp.where((donor == ranking[0]) | (receiver == ranking[0]) | (sizes[receiver] == 0), 0, jnp.maximum(slack, 0))
    moved = jax.random.randint(jax.random.fold_in(own, 4), (count // 2,), 0, 1 << 20) % (slack + 1)
    sizes = sizes.at[donor].add(-moved).at[receiver].add(moved)
    labels = jnp.searchsorted(jnp.cumsum(sizes), jnp.arange(rows * top), side="right").astype(jnp.int32)
    grid = labels.reshape(top, rows).T
    grid = grid[jax.random.permutation(jax.random.fold_in(own, 1), rows)]
    rotation = jax.random.randint(jax.random.fold_in(own, 2), (rows, 1), 0, top)
    return jnp.take_along_axis(grid, (jnp.arange(top)[None, :] + rotation) % top, axis=1)


def portions_of(amount, total, reach, lean, full):
    weights = [(1 << 20) // math.isqrt(grade ** lean) + 1 for grade in range(1, amount + 1)]
    largest = reach if full else min(reach, max(-(-total // amount), total * weights[0] // sum(weights)))
    least = 1 if total - largest >= amount - 1 else 0
    holding, rest = [largest] + [least] * (amount - 1), total - largest - least * (amount - 1)
    while rest > 0:
        candidates = [i for i in range(1, amount) if holding[i] < largest] or [i for i in range(1, amount) if holding[i] < reach]
        pool, remaining = sum([weights[i] for i in candidates]), rest
        for i in candidates:
            addition = min(reach - holding[i], max(1, remaining * weights[i] // pool), rest)
            holding[i] = holding[i] + addition
            rest = rest - addition
    return np.array(holding)


def centred(rng, shape, deviation, most, cuts=(), kind=jnp.bfloat16):
    level = shard_levels(rng, shape, cuts, -0.22, 0.18) if cuts else 1.0
    entries = jax.random.normal(rng, shape, jnp.float32) * deviation * level
    return jnp.minimum(jnp.maximum(entries, -most), most).astype(kind)


def setup_inputs(seed: int = 0, part: int = 0) -> dict:
    seeds = jax.random.split(jax.random.key(seed), 9)
    own_keys = jax.random.split(jax.random.fold_in(seeds[8], part), 9)
    tokens = draw_tokens(jax.random.fold_in(jax.random.fold_in(seeds[8], part), 71), part)
    norm_gain = jnp.clip(1.0 + 0.18 * jax.random.normal(seeds[1], (D,), jnp.float32), 0.1, 1.9)
    router_weight = draw_router_weight(jax.random.fold_in(seeds[8], 71), part)
    routes_keys = jax.random.split(jax.random.fold_in(own_keys[3], 1), LENGTH // TOK_DEV)
    routes_turns = jax.random.permutation(jax.random.fold_in(own_keys[3], 3), LENGTH // TOK_DEV)
    routes = jax.vmap(lambda own, number: assign_block(jax.random.fold_in(own_keys[3], 2), own, number, TOK_DEV, EXPERTS, TOPK, MOST, 2))(routes_keys, routes_turns).reshape((LENGTH, TOPK))
    key_weight = draw_key_weight(jax.random.fold_in(seeds[8], 71), part)
    value_weight = centred(seeds[5], (D, HEADS * HS), D ** -0.5, 0.125)
    query_weight = draw_query_weight(jax.random.fold_in(seeds[8], 71), part)
    output_weight = centred(seeds[7], (EXPERTS * QUARTERS, HPD * HS, D), 0.5, 3.0, ((0, 8),))
    return {"tokens": tokens, "norm_gain": norm_gain, "router_weight": router_weight, "routes": routes, "key_weight": key_weight, "value_weight": value_weight, "query_weight": query_weight, "output_weight": output_weight}


def norm_rows(tokens, norm_gain):
    floats = tokens.astype(jnp.float32)
    factor = lax.rsqrt(lax.optimization_barrier(jnp.mean(floats * floats, axis=1, keepdims=True)) + 1e-06)
    return (floats * factor * norm_gain).astype(jnp.bfloat16)

def split_blocks(row_count):
    pieces = max(1, row_count // 512)
    while row_count % pieces != 0:
        pieces = pieces - 1
    return pieces

def attend_block(queries, positions, key_rows, value_rows, head_count, head_size):
    key_index = jnp.arange(key_rows.shape[0], dtype=jnp.int32)
    allowed = key_index[None, :] <= positions[:, None]
    outputs = []
    for head_id in range(head_count):
        start_col = head_id * head_size
        query_part = queries[:, start_col:start_col + head_size]
        key_part = key_rows[:, start_col:start_col + head_size]
        scores = lax.dot_general(query_part, key_part, (((1,), (1,)), ((), ())), preferred_element_type=jnp.float32)
        scores = jnp.where(allowed, scores * (1.0 / math.sqrt(head_size)), -1e+30)
        peak_val = lax.optimization_barrier(jnp.max(scores, axis=1, keepdims=True))
        raised = jnp.exp(scores - peak_val)
        weights = (raised / lax.optimization_barrier(jnp.sum(raised, axis=1, keepdims=True))).astype(jnp.bfloat16)
        value_part = value_rows[:, start_col:start_col + head_size]
        outputs.append(jnp.dot(weights, value_part, preferred_element_type=jnp.float32).astype(jnp.bfloat16))
    return jnp.concatenate(outputs, axis=1)

def reference(tokens, norm_gain, router_weight, routes, key_weight, value_weight, query_weight, output_weight):
    quarter_count = query_weight.shape[0] // EXPERTS
    head_width = query_weight.shape[2]
    normed = norm_rows(tokens, norm_gain)
    logits = jnp.dot(normed.astype(jnp.float32), router_weight, precision=lax.Precision.HIGHEST)
    gating = jax.nn.softmax(jnp.take_along_axis(logits, routes, axis=1), axis=1)
    key_rows = jnp.dot(normed, key_weight, preferred_element_type=jnp.float32).astype(jnp.bfloat16)
    value_rows = jnp.dot(normed, value_weight, preferred_element_type=jnp.float32).astype(jnp.bfloat16)
    pair_total = LENGTH * TOPK
    pair_cap = LENGTH // TOK_DEV * MOST
    flat_expert = routes.reshape(pair_total)
    pair_token = jnp.arange(pair_total, dtype=jnp.int32) // TOPK
    queries = jnp.zeros((pair_total, HEADS * HS), jnp.bfloat16)
    members = []
    for expert_id in range(EXPERTS):
        found = jnp.nonzero(flat_expert == expert_id, size=pair_cap, fill_value=pair_total)[0].astype(jnp.int32)
        members.append(found)
        source = normed[jnp.minimum(found // TOPK, LENGTH - 1)]
        weight_cols = jnp.concatenate([query_weight[expert_id * quarter_count + quarter_id] for quarter_id in range(quarter_count)], axis=1)
        projected = jnp.dot(source, weight_cols, preferred_element_type=jnp.float32).astype(jnp.bfloat16)
        queries = queries.at[found].set(projected, mode='drop')
    block_total = split_blocks(pair_total)

    def run_block(packed):
        return attend_block(packed[0], packed[1], key_rows, value_rows, HEADS, HS)
    attended = lax.map(run_block, (queries.reshape(block_total, -1, HEADS * HS), pair_token.reshape(block_total, -1)))
    attended = attended.reshape(pair_total, HEADS * HS)
    pair_out = jnp.zeros((pair_total, D), jnp.float32)
    for expert_id in range(EXPERTS):
        found = members[expert_id]
        rows_in = attended[jnp.minimum(found, pair_total - 1)]
        part_sum = jnp.zeros((pair_cap, D), jnp.float32)
        for quarter_id in range(quarter_count):
            block_cols = rows_in[:, quarter_id * head_width:(quarter_id + 1) * head_width]
            piece = jnp.dot(block_cols, output_weight[expert_id * quarter_count + quarter_id], preferred_element_type=jnp.float32).astype(jnp.bfloat16)
            part_sum = part_sum + lax.optimization_barrier(piece).astype(jnp.float32)
        pair_out = pair_out.at[found].set(part_sum, mode='drop')
    weighted = pair_out * gating.reshape(pair_total)[:, None]
    return lax.optimization_barrier(jnp.sum(weighted.reshape(LENGTH, TOPK, D), axis=1)).astype(jnp.bfloat16)
```

```python
import functools
import math

import jax
import jax.numpy as jnp
from jax import lax
from jax.experimental import pallas as pl
from jax.experimental.pallas import tpu as pltpu
from jax.sharding import PartitionSpec as P

HS = 128
EXPERTS = 8
TOPK = 2
MOST = 40
MASKED = -1e30


def norm_rows(tokens, norm_gain):
    floats = tokens.astype(jnp.float32)
    factor = lax.rsqrt(jnp.mean(floats * floats, axis=1, keepdims=True) + 1e-06)
    return (floats * factor * norm_gain).astype(jnp.bfloat16)


def ring_order(count):
    return list(range(0, count, 2)) + list(range(1, count, 2))[::-1]


def attend_kernel(tile, span, pos_ref, q_ref, k_ref, v_ref, out_ref):
    scale = 1.0 / math.sqrt(HS)
    for i in range(q_ref.shape[0] // tile):
        rows = pl.ds(i * tile, tile)
        reach = (i + 1) * span
        scores = lax.dot_general(
            q_ref[rows, :],
            k_ref[pl.ds(0, reach), :],
            (((1,), (1,)), ((), ())),
            preferred_element_type=jnp.float32,
        )
        scores = scores * scale
        last = scores[:, reach - span :]
        key_index = lax.broadcasted_iota(jnp.int32, last.shape, 1) + (reach - span)
        last = jnp.where(key_index <= pos_ref[rows, :], last, MASKED)
        if i > 0:
            scores = jnp.concatenate([scores[:, : reach - span], last], axis=1)
        else:
            scores = last
        peak = jnp.max(scores, axis=1, keepdims=True)
        raised = jnp.exp(scores - peak)
        total = jnp.sum(raised, axis=1, keepdims=True)
        weights = (raised * (1.0 / total)).astype(jnp.bfloat16)
        out_ref[rows, :] = jnp.dot(
            weights, v_ref[pl.ds(0, reach), :], preferred_element_type=jnp.float32
        ).astype(jnp.bfloat16)


def attend(queries, positions, keys, values, tile, span):
    row_count, width = queries.shape
    length = keys.shape[0]
    heads = width // HS
    body = functools.partial(attend_kernel, tile, span)
    return pl.pallas_call(
        body,
        grid=(heads,),
        in_specs=[
            pl.BlockSpec((row_count, 1), lambda h: (0, 0)),
            pl.BlockSpec((row_count, HS), lambda h: (0, h)),
            pl.BlockSpec((length, HS), lambda h: (0, h)),
            pl.BlockSpec((length, HS), lambda h: (0, h)),
        ],
        out_specs=pl.BlockSpec((row_count, HS), lambda h: (0, h)),
        out_shape=jax.ShapeDtypeStruct((row_count, width), jnp.bfloat16),
        compiler_params=pltpu.CompilerParams(vmem_limit_bytes=48 * 1024 * 1024),
        cost_estimate=pl.CostEstimate(
            flops=2 * row_count * length * width,
            bytes_accessed=4 * length * width,
            transcendentals=row_count * length * heads // 2,
        ),
        name="attend",
    )(positions, queries, keys, values)


def per_device(
    tokens, norm_gain, router_weight, routes, key_weight, value_weight, query_weight, output_weight
):
    tok_count, model_width = tokens.shape
    ctx_count = lax.axis_size("ctx")
    exp_count = lax.axis_size("exp")
    quarter_count = ctx_count // EXPERTS
    head_width = query_weight.shape[2]
    ctx_index = lax.axis_index("ctx")
    exp_index = lax.axis_index("exp")
    order = ring_order(ctx_count)
    order_table = jnp.array(order, jnp.int32)
    place_table = jnp.array([order.index(c) for c in range(ctx_count)], jnp.int32)
    place = place_table[ctx_index]
    forward = [(order[p], order[(p + 1) % ctx_count]) for p in range(ctx_count)]
    backward = [(b, a) for a, b in forward]
    sibling = [(e, (e + 1) % exp_count) for e in range(exp_count)]
    query_slab = query_weight[0]
    output_slab = output_weight[0]
    if quarter_count > 1:
        first = (ctx_index % quarter_count) * head_width
        key_weight = lax.dynamic_slice_in_dim(key_weight, first, head_width, axis=1)
        value_weight = lax.dynamic_slice_in_dim(value_weight, first, head_width, axis=1)

    normed = norm_rows(tokens, norm_gain)
    half = tok_count // 2

    pair_count = tok_count * TOPK
    slot_total = EXPERTS * MOST
    flat_expert = routes.reshape(pair_count)
    onehot = (flat_expert[:, None] == jnp.arange(EXPERTS, dtype=jnp.int32)[None, :]).astype(
        jnp.int32
    )
    slot_rank = jnp.sum((jnp.cumsum(onehot, axis=0) - 1) * onehot, axis=1)
    slot_index = flat_expert * MOST + slot_rank
    chosen_mask = slot_index[None, :] == jnp.arange(slot_total, dtype=jnp.int32)[:, None]
    pair_token = jnp.arange(pair_count, dtype=jnp.int32) // TOPK
    slot_token = jnp.max(jnp.where(chosen_mask, pair_token[None, :], -1), axis=1)
    send_token = jnp.repeat(slot_token.reshape(EXPERTS, MOST), quarter_count, axis=0)
    got_token = lax.all_to_all(send_token, "ctx", split_axis=0, concat_axis=0, tiled=True)

    def project(rows):
        keys = jnp.dot(rows, key_weight, preferred_element_type=jnp.float32)
        values = jnp.dot(rows, value_weight, preferred_element_type=jnp.float32)
        return jnp.stack([keys.astype(jnp.bfloat16), values.astype(jnp.bfloat16)], axis=0)

    all_rows = jnp.zeros((ctx_count, tok_count, model_width), jnp.bfloat16)
    all_panels = jnp.zeros((2, ctx_count, exp_count, tok_count, head_width), jnp.bfloat16)
    panels = []

    def place_blocks(blocks, owners):
        nonlocal all_rows, all_panels
        rows = jnp.concatenate(blocks, axis=0)
        own = project(rows)
        others = lax.ppermute(own, "exp", sibling)
        for b, owner in enumerate(owners):
            part = slice(b * tok_count, (b + 1) * tok_count)
            all_rows = lax.dynamic_update_slice(
                all_rows, rows[part][None], (owner, 0, 0)
            )
            all_panels = lax.dynamic_update_slice(
                all_panels, own[:, None, None, part], (0, owner, exp_index, 0, 0)
            )
            all_panels = lax.dynamic_update_slice(
                all_panels, others[:, None, None, part], (0, owner, 1 - exp_index, 0, 0)
            )

    place_blocks([normed], [ctx_index])
    ahead = [normed[:half], normed[half:]]
    behind = [normed[:half], normed[half:]]
    steps = ctx_count // 2
    for step in range(1, steps + 1):
        if step < steps:
            ahead = [lax.ppermute(part, "ctx", forward) for part in ahead]
            behind = [lax.ppermute(part, "ctx", backward) for part in behind]
            owners = [
                order_table[(place - step) % ctx_count],
                order_table[(place + step) % ctx_count],
            ]
            place_blocks(ahead + behind, owners)
        else:
            one = lax.ppermute(ahead[0], "ctx", forward)
            two = lax.ppermute(behind[1], "ctx", backward)
            place_blocks([one, two], [order_table[(place + step) % ctx_count]])

    select = (
        got_token[:, :, None] == jnp.arange(tok_count, dtype=jnp.int32)[None, None, :]
    ).astype(jnp.bfloat16)
    slot_rows = lax.dot_general(
        select, all_rows, (((2,), (1,)), ((0,), (0,))), preferred_element_type=jnp.float32
    ).astype(jnp.bfloat16)
    row_count = ctx_count * MOST
    slot_rows = slot_rows.reshape(row_count, model_width)
    queries = jnp.dot(slot_rows, query_slab, preferred_element_type=jnp.float32).astype(
        jnp.bfloat16
    )
    source = jnp.arange(ctx_count, dtype=jnp.int32)[:, None] * exp_count + exp_index
    positions = (jnp.maximum(got_token, 0) + source * tok_count).reshape(row_count, 1)
    length = ctx_count * exp_count * tok_count
    attended = attend(
        queries,
        positions,
        all_panels[0].reshape(length, head_width),
        all_panels[1].reshape(length, head_width),
        2 * MOST,
        2 * exp_count * tok_count,
    )
    pieces = jnp.dot(attended, output_slab, preferred_element_type=jnp.float32).astype(
        jnp.bfloat16
    )
    returned = lax.all_to_all(
        pieces.reshape(ctx_count, MOST, model_width), "ctx", split_axis=0, concat_axis=0, tiled=True
    )

    logits = jnp.dot(normed.astype(jnp.float32), router_weight, precision=lax.Precision.HIGHEST)
    gating = jax.nn.softmax(jnp.take_along_axis(logits, routes, axis=1), axis=1)
    summed = (
        returned.astype(jnp.float32).reshape(EXPERTS, quarter_count, MOST, model_width).sum(axis=1)
    )
    summed = summed.reshape(slot_total, model_width)
    gate_flat = gating.reshape(pair_count)
    combine_mat = (
        jnp.where(chosen_mask, gate_flat[None, :], 0.0)
        .reshape(slot_total, tok_count, TOPK)
        .sum(axis=2)
    )
    combined = lax.dot_general(
        combine_mat, summed, (((0,), (0,)), ((), ())), precision=lax.Precision.HIGHEST
    )
    return combined.astype(jnp.bfloat16)


def solution(mesh):
    in_specs = (
        P(("groups", "ctx", "exp"), None),
        P(),
        P(),
        P(("groups", "ctx", "exp"), None),
        P(),
        P(),
        P("ctx", None, None),
        P("ctx", None, None),
    )
    out_specs = P(("groups", "ctx", "exp"), None)
    return jax.shard_map(
        per_device, mesh=mesh, in_specs=in_specs, out_specs=out_specs, check_vma=False
    )
```

```python
import functools
import math

import jax
import jax.numpy as jnp
from jax import lax
from jax.experimental import pallas as pl
from jax.experimental.pallas import tpu as pltpu
from jax.sharding import PartitionSpec as P

HS = 128
EXPERTS = 8
TOPK = 2
MOST = 40
SLOTS = 48
MASKED = -1e30
VMEM = 48 * 1024 * 1024


def ring_rank(place, count):
    place = lax.rem(place + 2 * count, count)
    return jnp.where(place < count // 2, 2 * place, 2 * (count - 1 - place) + 1)


def ring_place(rank, count):
    return jnp.where(rank % 2 == 0, rank // 2, count - 1 - rank // 2)


def ring_owner(offset):
    count = lax.axis_size("ctx")
    return ring_rank(ring_place(lax.axis_index("ctx"), count) + offset, count)


def norm_kernel(tokens_ref, gain_ref, out_ref):
    floats = tokens_ref[...].astype(jnp.float32)
    factor = lax.rsqrt(jnp.mean(floats * floats, axis=1, keepdims=True) + 1e-06)
    out_ref[...] = (floats * factor * gain_ref[...]).astype(jnp.bfloat16)


def norm_rows(tokens, norm_gain):
    return pl.pallas_call(
        norm_kernel,
        out_shape=jax.ShapeDtypeStruct(tokens.shape, jnp.bfloat16),
        name="norm_rows",
    )(tokens, norm_gain.reshape(1, -1))


def project_kernel(offsets, count, token_ref, *refs):
    blocks = refs[:count]
    key_ref, value_ref, query_ref, panel_ref, out_ref, picked = refs[count:]
    rows = jnp.concatenate([block[...] for block in blocks], axis=0)
    tok_count = rows.shape[0] // len(offsets)

    @pl.when(pl.program_id(0) == 0)
    def _():
        for g, offset in enumerate(offsets):
            wanted = token_ref[ring_owner(offset)]
            lane = lax.broadcasted_iota(jnp.int32, (SLOTS, tok_count), 1)
            select = (lane == wanted).astype(jnp.bfloat16)
            picked[pl.ds(g * SLOTS, SLOTS), :] = jnp.dot(
                select,
                rows[g * tok_count : (g + 1) * tok_count],
                preferred_element_type=jnp.float32,
            ).astype(jnp.bfloat16)

    panel_ref[0] = jnp.dot(
        rows, key_ref[...], preferred_element_type=jnp.float32
    ).astype(jnp.bfloat16)
    panel_ref[1] = jnp.dot(
        rows, value_ref[...], preferred_element_type=jnp.float32
    ).astype(jnp.bfloat16)
    queries = jnp.dot(picked[...], query_ref[...], preferred_element_type=jnp.float32)
    for g in range(len(offsets)):
        out_ref[g] = queries[g * SLOTS : (g + 1) * SLOTS].astype(jnp.bfloat16)


def project(blocks, offsets, slot_token, key_weight, value_weight, query_slab):
    row_count = sum(block.shape[0] for block in blocks)
    model_width, width = key_weight.shape
    step = min(width, 512)
    weight_spec = pl.BlockSpec((model_width, step), lambda n: (0, n))
    return pl.pallas_call(
        functools.partial(project_kernel, offsets, len(blocks)),
        grid=(width // step,),
        in_specs=[pl.BlockSpec(slot_token.shape, lambda n: (0, 0, 0))]
        + [pl.BlockSpec(block.shape, lambda n: (0, 0)) for block in blocks]
        + [weight_spec] * 3,
        out_specs=[
            pl.BlockSpec((2, row_count, step), lambda n: (0, 0, n)),
            pl.BlockSpec((len(offsets), SLOTS, step), lambda n: (0, 0, n)),
        ],
        out_shape=[
            jax.ShapeDtypeStruct((2, row_count, width), jnp.bfloat16),
            jax.ShapeDtypeStruct((len(offsets), SLOTS, width), jnp.bfloat16),
        ],
        scratch_shapes=[pltpu.VMEM((len(offsets) * SLOTS, model_width), jnp.bfloat16)],
        compiler_params=pltpu.CompilerParams(vmem_limit_bytes=VMEM),
        name="project",
    )(slot_token, *blocks, key_weight, value_weight, query_slab)


def attend_kernel(plan, tok_count, pos_ref, *refs):
    count = len(plan)
    query_refs = refs[:count]
    own_refs = refs[count : 2 * count]
    other_refs = refs[2 * count : 3 * count]
    out_ref, queries, keys, values, scores, weights = refs[3 * count :]
    side = lax.axis_index("exp")
    exp_count = 2
    rate = math.log2(math.e) / math.sqrt(HS)
    tile = 2 * MOST
    span = 2 * exp_count * tok_count
    tiles = queries.shape[0] // 2
    group = min(tiles, 4)

    for offsets, query_ref, own_ref, other_ref in zip(plan, query_refs, own_refs, other_refs):
        for g, offset in enumerate(offsets):
            owner = ring_owner(offset)
            part = pl.ds(g * tok_count, tok_count)
            queries[owner] = query_ref[g].astype(jnp.float32)[:MOST]
            keys[owner * exp_count + side] = own_ref[0, part]
            values[owner * exp_count + side] = own_ref[1, part]
            keys[owner * exp_count + 1 - side] = other_ref[0, part]
            values[owner * exp_count + 1 - side] = other_ref[1, part]

    per_span = 2 * exp_count
    for lead in range(0, tiles, group):
        top = lead + group
        base = lead * tile
        held = queries[2 * lead : 2 * top].reshape(group * tile, HS).astype(jnp.bfloat16)
        for j in range(top):
            skip = max(0, j - lead) * tile
            key_part = keys[per_span * j : per_span * (j + 1)].reshape(span, HS)
            scores[pl.ds(skip, group * tile - skip), pl.ds(j * span, span)] = lax.dot_general(
                held[skip:], key_part, (((1,), (1,)), ((), ())), preferred_element_type=jnp.float32
            )
        for i in range(lead, top):
            reach = (i + 1) * span
            for sub in range(0, tile, 16):
                rows = pl.ds((i - lead) * tile + sub, 16)
                part = scores[rows, pl.ds(0, reach)]
                last = part[:, reach - span :]
                key_index = lax.broadcasted_iota(jnp.int32, last.shape, 1) + (reach - span)
                allowed = key_index <= pos_ref[pl.ds(i * tile + sub, 16), :]
                last = jnp.where(allowed, last, MASKED)
                if i > 0:
                    part = jnp.concatenate([part[:, : reach - span], last], axis=1)
                else:
                    part = last
                peak = jnp.max(part, axis=1, keepdims=True)
                raised = jnp.exp2((part - peak) * rate)
                total = jnp.sum(raised, axis=1, keepdims=True)
                weights[rows, pl.ds(0, reach)] = (raised * (1.0 / total)).astype(jnp.bfloat16)
        sums = [None] * group
        for j in range(top):
            skip = max(0, j - lead)
            value_part = values[per_span * j : per_span * (j + 1)].reshape(span, HS)
            product = jnp.dot(
                weights[pl.ds(skip * tile, (group - skip) * tile), pl.ds(j * span, span)],
                value_part,
                preferred_element_type=jnp.float32,
            )
            for i in range(skip, group):
                piece = product[(i - skip) * tile : (i - skip + 1) * tile]
                sums[i] = piece if sums[i] is None else sums[i] + piece
        for i in range(group):
            out_ref[pl.ds(base + i * tile, tile), :] = sums[i].astype(jnp.bfloat16)


def attend(plan, positions, queries, own, other):
    row_count = positions.shape[0]
    width = queries[0].shape[-1]
    heads = width // HS
    ctx_count = row_count // MOST
    tok_count = own[0].shape[1] // len(plan[0])
    length = ctx_count * 2 * tok_count
    group_rows = min(row_count, 8 * MOST)
    query_specs = [pl.BlockSpec((q.shape[0], SLOTS, HS), lambda h: (0, 0, h)) for q in queries]
    panel_specs = [pl.BlockSpec((2, p.shape[1], HS), lambda h: (0, 0, h)) for p in own]
    return pl.pallas_call(
        functools.partial(attend_kernel, plan, tok_count),
        grid=(heads,),
        in_specs=[pl.BlockSpec((row_count, 1), lambda h: (0, 0))]
        + query_specs
        + panel_specs
        + panel_specs,
        out_specs=pl.BlockSpec((row_count, HS), lambda h: (0, h)),
        out_shape=jax.ShapeDtypeStruct((row_count, width), jnp.bfloat16),
        scratch_shapes=[
            pltpu.VMEM((ctx_count, MOST, HS), jnp.float32),
            pltpu.VMEM((2 * ctx_count, tok_count, HS), jnp.bfloat16),
            pltpu.VMEM((2 * ctx_count, tok_count, HS), jnp.bfloat16),
            pltpu.VMEM((group_rows, length), jnp.float32),
            pltpu.VMEM((group_rows, length), jnp.bfloat16),
        ],
        compiler_params=pltpu.CompilerParams(vmem_limit_bytes=VMEM),
        name="attend",
    )(positions, *queries, *own, *other)


def per_device(
    tokens, norm_gain, router_weight, routes, key_weight, value_weight, query_weight, output_weight
):
    tok_count, model_width = tokens.shape
    ctx_count = lax.axis_size("ctx")
    exp_count = lax.axis_size("exp")
    quarter_count = ctx_count // EXPERTS
    head_width = query_weight.shape[2]
    ctx_index = lax.axis_index("ctx")
    exp_index = lax.axis_index("exp")
    ranks = list(range(0, ctx_count, 2)) + list(range(1, ctx_count, 2))[::-1]
    forward = [(ranks[p], ranks[(p + 1) % ctx_count]) for p in range(ctx_count)]
    backward = [(b, a) for a, b in forward]
    sibling = [(e, 1 - e) for e in range(exp_count)]
    query_slab = query_weight[0]
    output_slab = output_weight[0]
    if quarter_count > 1:
        first = (ctx_index % quarter_count) * head_width
        key_weight = lax.dynamic_slice_in_dim(key_weight, first, head_width, axis=1)
        value_weight = lax.dynamic_slice_in_dim(value_weight, first, head_width, axis=1)

    normed = norm_rows(tokens, norm_gain)
    half = tok_count // 2

    pair_count = tok_count * TOPK
    slot_total = EXPERTS * MOST
    flat_expert = routes.reshape(pair_count)
    onehot = (flat_expert[:, None] == jnp.arange(EXPERTS, dtype=jnp.int32)[None, :]).astype(
        jnp.int32
    )
    slot_rank = jnp.sum((jnp.cumsum(onehot, axis=0) - 1) * onehot, axis=1)
    slot_index = flat_expert * MOST + slot_rank
    chosen_mask = slot_index[None, :] == jnp.arange(slot_total, dtype=jnp.int32)[:, None]
    pair_token = jnp.arange(pair_count, dtype=jnp.int32) // TOPK
    slot_token = jnp.max(jnp.where(chosen_mask, pair_token[None, :], -1), axis=1)
    send_token = jnp.repeat(slot_token.reshape(EXPERTS, MOST), quarter_count, axis=0)
    got_token = lax.all_to_all(send_token, "ctx", split_axis=0, concat_axis=0, tiled=True)
    wanted = jnp.pad(got_token, ((0, 0), (0, SLOTS - MOST)), constant_values=-1)[:, :, None]
    source = jnp.arange(ctx_count, dtype=jnp.int32)[:, None] * exp_count + exp_index
    positions = (got_token + source * tok_count).reshape(ctx_count * MOST, 1)

    plan, queries, own, other = [], [], [], []

    def serve(blocks, offsets):
        panel, query = project(blocks, offsets, wanted, key_weight, value_weight, query_slab)
        plan.append(offsets)
        queries.append(query)
        own.append(panel)
        other.append(lax.ppermute(panel, "exp", sibling))

    serve([normed], [0])
    ahead = behind = normed
    steps = ctx_count // 2
    for step in range(1, steps):
        ahead = lax.ppermute(ahead, "ctx", forward)
        behind = lax.ppermute(behind, "ctx", backward)
        serve([ahead, behind], [-step, step])
    one = lax.ppermute(ahead[:half], "ctx", forward)
    two = lax.ppermute(behind[half:], "ctx", backward)
    serve([one, two], [steps])

    attended = attend(plan, positions, queries, own, other)
    pieces = jnp.dot(attended, output_slab, preferred_element_type=jnp.float32).astype(
        jnp.bfloat16
    )
    returned = lax.all_to_all(
        pieces.reshape(ctx_count, MOST, model_width), "ctx", split_axis=0, concat_axis=0, tiled=True
    )

    logits = jnp.dot(normed.astype(jnp.float32), router_weight, precision=lax.Precision.HIGHEST)
    gating = jax.nn.softmax(jnp.take_along_axis(logits, routes, axis=1), axis=1)
    summed = (
        returned.astype(jnp.float32).reshape(EXPERTS, quarter_count, MOST, model_width).sum(axis=1)
    )
    summed = summed.reshape(slot_total, model_width)
    gate_flat = gating.reshape(pair_count)
    combine_mat = (
        jnp.where(chosen_mask, gate_flat[None, :], 0.0)
        .reshape(slot_total, tok_count, TOPK)
        .sum(axis=2)
    )
    combined = lax.dot_general(
        combine_mat, summed, (((0,), (0,)), ((), ())), precision=lax.Precision.HIGHEST
    )
    return combined.astype(jnp.bfloat16)


def solution(mesh):
    in_specs = (
        P(("groups", "ctx", "exp"), None),
        P(),
        P(),
        P(("groups", "ctx", "exp"), None),
        P(),
        P(),
        P("ctx", None, None),
        P("ctx", None, None),
    )
    out_specs = P(("groups", "ctx", "exp"), None)
    return jax.shard_map(
        per_device, mesh=mesh, in_specs=in_specs, out_specs=out_specs, check_vma=False
    )
```

```python
import functools
import math

import jax
import jax.numpy as jnp
from jax import lax
from jax.experimental import pallas as pl
from jax.experimental.pallas import tpu as pltpu
from jax.sharding import PartitionSpec as P

HS = 128
EXPERTS = 8
MOST = 40
SLOTS = 48
MASKED = -1e30
LANES = 128
MIB = 1 << 20


def ring_rank(place, count):
    place = lax.rem(place + 2 * count, count)
    return jnp.where(place < count // 2, 2 * place, 2 * (count - 1 - place) + 1)


def ring_place(rank, count):
    return jnp.where(rank % 2 == 0, rank // 2, count - 1 - rank // 2)


def ring_owner(offset):
    count = lax.axis_size("ctx")
    return ring_rank(ring_place(lax.axis_index("ctx"), count) + offset, count)


def norm_kernel(tokens_ref, gain_ref, routes_ref, top_ref, bottom_ref):
    floats = tokens_ref[...].astype(jnp.float32)
    count, width = floats.shape
    factor = lax.rsqrt(jnp.mean(floats * floats, axis=1, keepdims=True) + 1e-06)
    normed = (floats * factor * gain_ref[...]).astype(jnp.bfloat16)
    expert = lax.broadcasted_iota(jnp.int32, (LANES, count), 0)
    named = (expert == routes_ref[0:1, :]) | (expert == routes_ref[1:2, :])
    before = lax.broadcasted_iota(jnp.int32, (count, count), 0) < lax.broadcasted_iota(
        jnp.int32, (count, count), 1
    )
    rank = jnp.dot(
        named.astype(jnp.bfloat16),
        before.astype(jnp.bfloat16),
        preferred_element_type=jnp.float32,
    )
    slots = jnp.where(named, rank, -1.0).T.astype(jnp.bfloat16)
    half = count // 2
    for ref, part in ((top_ref, slice(0, half)), (bottom_ref, slice(half, count))):
        ref[:, :width] = normed[part]
        ref[:, width:] = slots[part]


def norm_rows(tokens, norm_gain, routes):
    count, width = tokens.shape
    half = jax.ShapeDtypeStruct((count // 2, width + LANES), jnp.bfloat16)
    return pl.pallas_call(
        norm_kernel, out_shape=[half, half], name="norm_rows"
    )(tokens, norm_gain.reshape(1, -1), routes.T)


def project_kernel(offsets, count, experts, *refs):
    blocks = refs[:count]
    key_ref, value_ref, query_ref, panel_ref, out_ref, pos_ref, picked = refs[count:]
    width = key_ref.shape[0]
    rows = jnp.concatenate([block[:, :width] for block in blocks], axis=0)
    tok_count = rows.shape[0] // len(offsets)

    @pl.when(pl.program_id(0) == 0)
    def _():
        slots = jnp.concatenate([block[:, width:] for block in blocks], axis=0)
        slots = slots.astype(jnp.float32)
        expert = lax.axis_index("ctx") // (lax.axis_size("ctx") // experts)
        lane = lax.broadcasted_iota(jnp.int32, slots.shape, 1)
        slot = jnp.sum(jnp.where(lane == expert, slots, 0.0), axis=1, keepdims=True)
        select = (slot == lane.astype(jnp.float32)).astype(jnp.float32)
        number = lax.broadcasted_iota(jnp.int32, (tok_count, LANES), 0).astype(jnp.bfloat16)
        for g, offset in enumerate(offsets):
            part = slice(g * tok_count, (g + 1) * tok_count)
            chosen = select[part].T[:SLOTS].astype(jnp.bfloat16)
            picked[pl.ds(g * SLOTS, SLOTS), :] = jnp.dot(
                chosen, rows[part], preferred_element_type=jnp.float32
            ).astype(jnp.bfloat16)
            start = (ring_owner(offset) * lax.axis_size("exp") + lax.axis_index("exp")) * tok_count
            pos_ref[g] = jnp.dot(
                chosen, number, preferred_element_type=jnp.float32
            ) + start.astype(jnp.float32)

    panel_ref[0] = jnp.dot(
        rows, key_ref[...], preferred_element_type=jnp.float32
    ).astype(jnp.bfloat16)
    panel_ref[1] = jnp.dot(
        rows, value_ref[...], preferred_element_type=jnp.float32
    ).astype(jnp.bfloat16)
    queries = jnp.dot(picked[...], query_ref[...], preferred_element_type=jnp.float32)
    for g in range(len(offsets)):
        out_ref[g] = queries[g * SLOTS : (g + 1) * SLOTS].astype(jnp.bfloat16)


def project(blocks, offsets, key_weight, value_weight, query_slab):
    row_count = sum(block.shape[0] for block in blocks)
    model_width, width = key_weight.shape
    step = min(width, 256)
    owners = len(offsets)
    weight_spec = pl.BlockSpec((model_width, step), lambda n: (0, n))
    return pl.pallas_call(
        functools.partial(project_kernel, offsets, len(blocks), EXPERTS),
        grid=(width // step,),
        in_specs=[pl.BlockSpec(block.shape, lambda n: (0, 0)) for block in blocks]
        + [weight_spec] * 3,
        out_specs=[
            pl.BlockSpec((2, row_count, step), lambda n: (0, 0, n)),
            pl.BlockSpec((owners, SLOTS, step), lambda n: (0, 0, n)),
            pl.BlockSpec((owners, SLOTS, LANES), lambda n: (0, 0, 0)),
        ],
        out_shape=[
            jax.ShapeDtypeStruct((2, row_count, width), jnp.bfloat16),
            jax.ShapeDtypeStruct((owners, SLOTS, width), jnp.bfloat16),
            jax.ShapeDtypeStruct((owners, SLOTS, LANES), jnp.float32),
        ],
        scratch_shapes=[pltpu.VMEM((owners * SLOTS, model_width), jnp.bfloat16)],
        compiler_params=pltpu.CompilerParams(vmem_limit_bytes=20 * MIB),
        name="project",
    )(*blocks, key_weight, value_weight, query_slab)


def attend_kernel(plan, tok_count, heads, *refs):
    count = len(plan)
    query_refs, pos_refs, own_refs, other_refs = (
        refs[k * count : (k + 1) * count] for k in range(4)
    )
    out_ref, places, queries, keys, values, scores, weights = refs[4 * count :]
    side = lax.axis_index("exp")
    exp_count = 2
    rate = math.log2(math.e) / math.sqrt(HS)
    tile = 2 * MOST
    per_span = 2 * exp_count
    span = per_span * tok_count
    tiles = queries.shape[1] // 2
    group = min(tiles, 4)

    @pl.when(pl.program_id(0) == 0)
    def _():
        for offsets, pos_ref in zip(plan, pos_refs):
            for g, offset in enumerate(offsets):
                places[ring_owner(offset)] = pos_ref[g, :MOST]

    for offsets, query_ref, own_ref, other_ref in zip(plan, query_refs, own_refs, other_refs):
        for g, offset in enumerate(offsets):
            owner = ring_owner(offset)
            part = pl.ds(g * tok_count, tok_count)
            for h in range(heads):
                lanes = pl.ds(h * HS, HS)
                queries[h, owner] = query_ref[g, :, lanes].astype(jnp.float32)[:MOST]
                keys[h, owner * exp_count + side] = own_ref[0, part, lanes]
                values[h, owner * exp_count + side] = own_ref[1, part, lanes]
                keys[h, owner * exp_count + 1 - side] = other_ref[0, part, lanes]
                values[h, owner * exp_count + 1 - side] = other_ref[1, part, lanes]

    for lead in range(0, tiles, group):
        top = lead + group
        base = lead * tile
        for h in range(heads):
            held = queries[h, 2 * lead : 2 * top].reshape(group * tile, HS).astype(jnp.bfloat16)
            for j in range(top):
                skip = max(0, j - lead) * tile
                key_part = keys[h, per_span * j : per_span * (j + 1)].reshape(span, HS)
                scores[h, pl.ds(skip, group * tile - skip), pl.ds(j * span, span)] = (
                    lax.dot_general(
                        held[skip:],
                        key_part,
                        (((1,), (1,)), ((), ())),
                        preferred_element_type=jnp.float32,
                    )
                )
        for h in range(heads):
            for i in range(lead, top):
                reach = (i + 1) * span
                spots = places[2 * i : 2 * i + 2].reshape(tile, LANES)
                for sub in range(0, tile, 16):
                    rows = pl.ds((i - lead) * tile + sub, 16)
                    part = scores[h, rows, pl.ds(0, reach)]
                    last = part[:, reach - span :]
                    key_index = lax.broadcasted_iota(jnp.int32, last.shape, 1) + (reach - span)
                    spot = spots[sub : sub + 16, 0:1]
                    last = jnp.where(key_index.astype(jnp.float32) <= spot, last, MASKED)
                    if i > 0:
                        part = jnp.concatenate([part[:, : reach - span], last], axis=1)
                    else:
                        part = last
                    peak = jnp.max(part, axis=1, keepdims=True)
                    raised = jnp.exp2((part - peak) * rate)
                    total = jnp.sum(raised, axis=1, keepdims=True)
                    weights[h, rows, pl.ds(0, reach)] = (raised * (1.0 / total)).astype(
                        jnp.bfloat16
                    )
        for h in range(heads):
            sums = [None] * group
            for j in range(top):
                skip = max(0, j - lead)
                value_part = values[h, per_span * j : per_span * (j + 1)].reshape(span, HS)
                product = jnp.dot(
                    weights[h, pl.ds(skip * tile, (group - skip) * tile), pl.ds(j * span, span)],
                    value_part,
                    preferred_element_type=jnp.float32,
                )
                for i in range(skip, group):
                    piece = product[(i - skip) * tile : (i - skip + 1) * tile]
                    sums[i] = piece if sums[i] is None else sums[i] + piece
            for i in range(group):
                out_ref[pl.ds(base + i * tile, tile), pl.ds(h * HS, HS)] = sums[i].astype(
                    jnp.bfloat16
                )


def attend(plan, queries, positions, own, other):
    owners = sum(len(offsets) for offsets in plan)
    row_count = owners * MOST
    width = queries[0].shape[-1]
    heads = 2 if owners <= 8 else 1
    step = heads * HS
    tok_count = own[0].shape[1] // len(plan[0])
    length = owners * 2 * tok_count
    group_rows = min(row_count, 8 * MOST)
    query_specs = [pl.BlockSpec((q.shape[0], SLOTS, step), lambda h: (0, 0, h)) for q in queries]
    pos_specs = [pl.BlockSpec(p.shape, lambda h: (0, 0, 0)) for p in positions]
    panel_specs = [pl.BlockSpec((2, p.shape[1], step), lambda h: (0, 0, h)) for p in own]
    scratch = heads * (group_rows * length * 6 + length * HS * 4 + row_count * HS * 4)
    windows = 2 * (length * step * 4 + row_count * step * 4) + 4 * row_count * LANES * 4
    return pl.pallas_call(
        functools.partial(attend_kernel, plan, tok_count, heads),
        grid=(width // step,),
        in_specs=query_specs + pos_specs + panel_specs + panel_specs,
        out_specs=pl.BlockSpec((row_count, step), lambda h: (0, h)),
        out_shape=jax.ShapeDtypeStruct((row_count, width), jnp.bfloat16),
        scratch_shapes=[
            pltpu.VMEM((owners, MOST, LANES), jnp.float32),
            pltpu.VMEM((heads, owners, MOST, HS), jnp.float32),
            pltpu.VMEM((heads, 2 * owners, tok_count, HS), jnp.bfloat16),
            pltpu.VMEM((heads, 2 * owners, tok_count, HS), jnp.bfloat16),
            pltpu.VMEM((heads, group_rows, length), jnp.float32),
            pltpu.VMEM((heads, group_rows, length), jnp.bfloat16),
        ],
        compiler_params=pltpu.CompilerParams(vmem_limit_bytes=scratch + windows + 4 * MIB),
        name="attend",
    )(*queries, *positions, *own, *other)


def per_device(
    tokens, norm_gain, router_weight, routes, key_weight, value_weight, query_weight, output_weight
):
    tok_count, model_width = tokens.shape
    ctx_count = lax.axis_size("ctx")
    exp_count = lax.axis_size("exp")
    quarter_count = ctx_count // EXPERTS
    head_width = query_weight.shape[2]
    ranks = list(range(0, ctx_count, 2)) + list(range(1, ctx_count, 2))[::-1]
    forward = [(ranks[p], ranks[(p + 1) % ctx_count]) for p in range(ctx_count)]
    backward = [(b, a) for a, b in forward]
    sibling = [(e, 1 - e) for e in range(exp_count)]
    query_slab = query_weight[0]
    output_slab = output_weight[0]
    if quarter_count > 1:
        first = (lax.axis_index("ctx") % quarter_count) * head_width
        key_weight = lax.dynamic_slice_in_dim(key_weight, first, head_width, axis=1)
        value_weight = lax.dynamic_slice_in_dim(value_weight, first, head_width, axis=1)

    plan, queries, positions, own, other = [], [], [], [], []

    def serve(blocks, offsets):
        panel, query, position = project(blocks, offsets, key_weight, value_weight, query_slab)
        plan.append(offsets)
        queries.append(query)
        positions.append(position)
        own.append(panel)
        other.append(lax.ppermute(panel, "exp", sibling))

    halves = norm_rows(tokens, norm_gain, routes)
    serve(halves, [0])
    ahead, behind = list(halves), list(halves)
    steps = ctx_count // 2
    for step in range(1, steps):
        ahead = [lax.ppermute(part, "ctx", forward) for part in ahead]
        behind = [lax.ppermute(part, "ctx", backward) for part in behind[::-1]][::-1]
        serve(ahead + behind, [-step, step])
    one = lax.ppermute(ahead[0], "ctx", forward)
    two = lax.ppermute(behind[1], "ctx", backward)
    serve([one, two], [steps])

    attended = attend(plan, queries, positions, own, other)
    pieces = jnp.dot(attended, output_slab, preferred_element_type=jnp.float32).astype(
        jnp.bfloat16
    )
    returned = lax.all_to_all(
        pieces.reshape(ctx_count, MOST, model_width), "ctx", split_axis=0, concat_axis=0, tiled=True
    )

    message = jnp.concatenate(halves, axis=0)
    logits = jnp.dot(
        message[:, :model_width].astype(jnp.float32), router_weight, precision=lax.Precision.HIGHEST
    )
    slots = message[:, model_width : model_width + EXPERTS].astype(jnp.float32)
    gating = jax.nn.softmax(jnp.where(slots >= 0, logits, -jnp.inf), axis=1)
    slot_index = jnp.arange(MOST, dtype=jnp.float32)[None, None, :]
    combine_mat = jnp.where(slots[:, :, None] == slot_index, gating[:, :, None], 0.0)
    combine_mat = combine_mat.reshape(tok_count, EXPERTS * MOST)
    summed = (
        returned.astype(jnp.float32).reshape(EXPERTS, quarter_count, MOST, model_width).sum(axis=1)
    )
    summed = summed.reshape(EXPERTS * MOST, model_width)
    combined = jnp.dot(combine_mat, summed, precision=lax.Precision.HIGHEST)
    return combined.astype(jnp.bfloat16)


def solution(mesh):
    in_specs = (
        P(("groups", "ctx", "exp"), None),
        P(),
        P(),
        P(("groups", "ctx", "exp"), None),
        P(),
        P(),
        P("ctx", None, None),
        P("ctx", None, None),
    )
    out_specs = P(("groups", "ctx", "exp"), None)
    return jax.shard_map(
        per_device, mesh=mesh, in_specs=in_specs, out_specs=out_specs, check_vma=False
    )
```

```python
import functools
import math

import jax
import jax.numpy as jnp
from jax import lax
from jax.experimental import pallas as pl
from jax.experimental.pallas import tpu as pltpu
from jax.sharding import PartitionSpec as P

HS = 128
EXPERTS = 8
MOST = 40
SLOTS = 48
MASKED = -1e30
LANES = 128
MIB = 1 << 20


def ring_rank(place, count):
    place = lax.rem(place + 2 * count, count)
    return jnp.where(place < count // 2, 2 * place, 2 * (count - 1 - place) + 1)


def ring_place(rank, count):
    return jnp.where(rank % 2 == 0, rank // 2, count - 1 - rank // 2)


def ring_owner(offset):
    count = lax.axis_size("ctx")
    return ring_rank(ring_place(lax.axis_index("ctx"), count) + offset, count)


def norm_kernel(tokens_ref, gain_ref, routes_ref, top_ref, bottom_ref):
    floats = tokens_ref[...].astype(jnp.float32)
    count, width = floats.shape
    factor = lax.rsqrt(jnp.mean(floats * floats, axis=1, keepdims=True) + 1e-06)
    normed = (floats * factor * gain_ref[...]).astype(jnp.bfloat16)
    expert = lax.broadcasted_iota(jnp.int32, (LANES, count), 0)
    named = (expert == routes_ref[0:1, :]) | (expert == routes_ref[1:2, :])
    before = lax.broadcasted_iota(jnp.int32, (count, count), 0) < lax.broadcasted_iota(
        jnp.int32, (count, count), 1
    )
    rank = jnp.dot(
        named.astype(jnp.bfloat16),
        before.astype(jnp.bfloat16),
        preferred_element_type=jnp.float32,
    )
    slots = jnp.where(named, rank, -1.0).T.astype(jnp.bfloat16)
    half = count // 2
    for ref, part in ((top_ref, slice(0, half)), (bottom_ref, slice(half, count))):
        ref[:, :width] = normed[part]
        ref[:, width:] = slots[part]


def norm_rows(tokens, norm_gain, routes):
    count, width = tokens.shape
    half = jax.ShapeDtypeStruct((count // 2, width + LANES), jnp.bfloat16)
    return pl.pallas_call(
        norm_kernel, out_shape=[half, half], name="norm_rows"
    )(tokens, norm_gain.reshape(1, -1), routes.T)


def project_kernel(offsets, count, experts, *refs):
    blocks = refs[:count]
    key_ref, value_ref, query_ref, panel_ref, out_ref, pos_ref, picked = refs[count:]
    width = key_ref.shape[0]
    rows = jnp.concatenate([block[:, :width] for block in blocks], axis=0)
    tok_count = rows.shape[0] // len(offsets)

    @pl.when(pl.program_id(0) == 0)
    def _():
        slots = jnp.concatenate([block[:, width:] for block in blocks], axis=0)
        slots = slots.astype(jnp.float32)
        expert = lax.axis_index("ctx") // (lax.axis_size("ctx") // experts)
        lane = lax.broadcasted_iota(jnp.int32, slots.shape, 1)
        slot = jnp.sum(jnp.where(lane == expert, slots, 0.0), axis=1, keepdims=True)
        select = (slot == lane.astype(jnp.float32)).astype(jnp.float32)
        number = lax.broadcasted_iota(jnp.int32, (tok_count, LANES), 0).astype(jnp.bfloat16)
        for g, offset in enumerate(offsets):
            part = slice(g * tok_count, (g + 1) * tok_count)
            chosen = select[part].T[:SLOTS].astype(jnp.bfloat16)
            picked[pl.ds(g * SLOTS, SLOTS), :] = jnp.dot(
                chosen, rows[part], preferred_element_type=jnp.float32
            ).astype(jnp.bfloat16)
            start = (ring_owner(offset) * lax.axis_size("exp") + lax.axis_index("exp")) * tok_count
            pos_ref[g] = jnp.dot(
                chosen, number, preferred_element_type=jnp.float32
            ) + start.astype(jnp.float32)

    panel_ref[0] = jnp.dot(
        rows, key_ref[...], preferred_element_type=jnp.float32
    ).astype(jnp.bfloat16)
    panel_ref[1] = jnp.dot(
        rows, value_ref[...], preferred_element_type=jnp.float32
    ).astype(jnp.bfloat16)
    queries = jnp.dot(picked[...], query_ref[...], preferred_element_type=jnp.float32)
    for g in range(len(offsets)):
        out_ref[g] = queries[g * SLOTS : (g + 1) * SLOTS].astype(jnp.bfloat16)


def project(blocks, offsets, key_weight, value_weight, query_slab):
    row_count = sum(block.shape[0] for block in blocks)
    model_width, width = key_weight.shape
    step = min(width, 256)
    owners = len(offsets)
    weight_spec = pl.BlockSpec((model_width, step), lambda n: (0, n))
    return pl.pallas_call(
        functools.partial(project_kernel, offsets, len(blocks), EXPERTS),
        grid=(width // step,),
        in_specs=[pl.BlockSpec(block.shape, lambda n: (0, 0)) for block in blocks]
        + [weight_spec] * 3,
        out_specs=[
            pl.BlockSpec((2, row_count, step), lambda n: (0, 0, n)),
            pl.BlockSpec((owners, SLOTS, step), lambda n: (0, 0, n)),
            pl.BlockSpec((owners, SLOTS, LANES), lambda n: (0, 0, 0)),
        ],
        out_shape=[
            jax.ShapeDtypeStruct((2, row_count, width), jnp.bfloat16),
            jax.ShapeDtypeStruct((owners, SLOTS, width), jnp.bfloat16),
            jax.ShapeDtypeStruct((owners, SLOTS, LANES), jnp.float32),
        ],
        scratch_shapes=[pltpu.VMEM((owners * SLOTS, model_width), jnp.bfloat16)],
        compiler_params=pltpu.CompilerParams(vmem_limit_bytes=20 * MIB),
        name="project",
    )(*blocks, key_weight, value_weight, query_slab)


def attend_kernel(plan, tok_count, heads, *refs):
    count = len(plan)
    query_refs, pos_refs, own_refs, other_refs = (
        refs[k * count : (k + 1) * count] for k in range(4)
    )
    out_ref, places, queries, keys, values, scores, weights = refs[4 * count :]
    side = lax.axis_index("exp")
    exp_count = 2
    rate = math.log2(math.e) / math.sqrt(HS)
    tile = 2 * MOST
    per_span = 2 * exp_count
    span = per_span * tok_count
    tiles = queries.shape[1] // 2
    group = min(tiles, 4)

    @pl.when(pl.program_id(0) == 0)
    def _():
        for offsets, pos_ref in zip(plan, pos_refs):
            for g, offset in enumerate(offsets):
                places[ring_owner(offset)] = pos_ref[g, :MOST]

    for offsets, query_ref, own_ref, other_ref in zip(plan, query_refs, own_refs, other_refs):
        for g, offset in enumerate(offsets):
            owner = ring_owner(offset)
            part = pl.ds(g * tok_count, tok_count)
            for h in range(heads):
                lanes = pl.ds(h * HS, HS)
                queries[h, owner] = query_ref[g, :, lanes].astype(jnp.float32)[:MOST]
                keys[h, owner * exp_count + side] = own_ref[0, part, lanes]
                values[h, owner * exp_count + side] = own_ref[1, part, lanes]
                keys[h, owner * exp_count + 1 - side] = other_ref[0, part, lanes]
                values[h, owner * exp_count + 1 - side] = other_ref[1, part, lanes]

    for lead in range(0, tiles, group):
        top = lead + group
        base = lead * tile
        for h in range(heads):
            held = queries[h, 2 * lead : 2 * top].reshape(group * tile, HS).astype(jnp.bfloat16)
            for j in range(top):
                skip = max(0, j - lead) * tile
                key_part = keys[h, per_span * j : per_span * (j + 1)].reshape(span, HS)
                scores[h, pl.ds(skip, group * tile - skip), pl.ds(j * span, span)] = (
                    lax.dot_general(
                        held[skip:],
                        key_part,
                        (((1,), (1,)), ((), ())),
                        preferred_element_type=jnp.float32,
                    )
                )
        for h in range(heads):
            for i in range(lead, top):
                reach = (i + 1) * span
                spots = places[2 * i : 2 * i + 2].reshape(tile, LANES)
                for sub in range(0, tile, 16):
                    rows = pl.ds((i - lead) * tile + sub, 16)
                    part = scores[h, rows, pl.ds(0, reach)]
                    last = part[:, reach - span :]
                    key_index = lax.broadcasted_iota(jnp.int32, last.shape, 1) + (reach - span)
                    spot = spots[sub : sub + 16, 0:1]
                    last = jnp.where(key_index.astype(jnp.float32) <= spot, last, MASKED)
                    if i > 0:
                        part = jnp.concatenate([part[:, : reach - span], last], axis=1)
                    else:
                        part = last
                    peak = jnp.max(part, axis=1, keepdims=True)
                    raised = jnp.exp2((part - peak) * rate)
                    total = jnp.sum(raised, axis=1, keepdims=True)
                    weights[h, rows, pl.ds(0, reach)] = (raised * (1.0 / total)).astype(
                        jnp.bfloat16
                    )
        for h in range(heads):
            sums = [None] * group
            for j in range(top):
                skip = max(0, j - lead)
                value_part = values[h, per_span * j : per_span * (j + 1)].reshape(span, HS)
                product = jnp.dot(
                    weights[h, pl.ds(skip * tile, (group - skip) * tile), pl.ds(j * span, span)],
                    value_part,
                    preferred_element_type=jnp.float32,
                )
                for i in range(skip, group):
                    piece = product[(i - skip) * tile : (i - skip + 1) * tile]
                    sums[i] = piece if sums[i] is None else sums[i] + piece
            for i in range(group):
                out_ref[pl.ds(base + i * tile, tile), pl.ds(h * HS, HS)] = sums[i].astype(
                    jnp.bfloat16
                )


def attend(plan, queries, positions, own, other):
    owners = sum(len(offsets) for offsets in plan)
    row_count = owners * MOST
    width = queries[0].shape[-1]
    heads = 2 if owners <= 8 else 1
    step = heads * HS
    tok_count = own[0].shape[1] // len(plan[0])
    length = owners * 2 * tok_count
    group_rows = min(row_count, 8 * MOST)
    query_specs = [pl.BlockSpec((q.shape[0], SLOTS, step), lambda h: (0, 0, h)) for q in queries]
    pos_specs = [pl.BlockSpec(p.shape, lambda h: (0, 0, 0)) for p in positions]
    panel_specs = [pl.BlockSpec((2, p.shape[1], step), lambda h: (0, 0, h)) for p in own]
    scratch = heads * (group_rows * length * 6 + length * HS * 4 + row_count * HS * 4)
    windows = 2 * (length * step * 4 + row_count * step * 4) + 4 * row_count * LANES * 4
    return pl.pallas_call(
        functools.partial(attend_kernel, plan, tok_count, heads),
        grid=(width // step,),
        in_specs=query_specs + pos_specs + panel_specs + panel_specs,
        out_specs=pl.BlockSpec((row_count, step), lambda h: (0, h)),
        out_shape=jax.ShapeDtypeStruct((row_count, width), jnp.bfloat16),
        scratch_shapes=[
            pltpu.VMEM((owners, MOST, LANES), jnp.float32),
            pltpu.VMEM((heads, owners, MOST, HS), jnp.float32),
            pltpu.VMEM((heads, 2 * owners, tok_count, HS), jnp.bfloat16),
            pltpu.VMEM((heads, 2 * owners, tok_count, HS), jnp.bfloat16),
            pltpu.VMEM((heads, group_rows, length), jnp.float32),
            pltpu.VMEM((heads, group_rows, length), jnp.bfloat16),
        ],
        compiler_params=pltpu.CompilerParams(vmem_limit_bytes=scratch + windows + 4 * MIB),
        name="attend",
    )(*queries, *positions, *own, *other)


def per_device(
    tokens, norm_gain, router_weight, routes, key_weight, value_weight, query_weight, output_weight
):
    tok_count, model_width = tokens.shape
    ctx_count = lax.axis_size("ctx")
    exp_count = lax.axis_size("exp")
    quarter_count = ctx_count // EXPERTS
    head_width = query_weight.shape[2]
    ranks = list(range(0, ctx_count, 2)) + list(range(1, ctx_count, 2))[::-1]
    forward = [(ranks[p], ranks[(p + 1) % ctx_count]) for p in range(ctx_count)]
    backward = [(b, a) for a, b in forward]
    sibling = [(e, 1 - e) for e in range(exp_count)]
    query_slab = query_weight[0]
    output_slab = output_weight[0]
    if quarter_count > 1:
        first = (lax.axis_index("ctx") % quarter_count) * head_width
        key_weight = lax.dynamic_slice_in_dim(key_weight, first, head_width, axis=1)
        value_weight = lax.dynamic_slice_in_dim(value_weight, first, head_width, axis=1)

    plan, queries, positions, own, other = [], [], [], [], []

    def serve(blocks, offsets):
        panel, query, position = project(blocks, offsets, key_weight, value_weight, query_slab)
        plan.append(offsets)
        queries.append(query)
        positions.append(position)
        own.append(panel)
        other.append(lax.ppermute(panel, "exp", sibling))

    def after_projection(parts):
        tied = lax.optimization_barrier((positions[-1], *parts))
        positions[-1] = tied[0]
        return list(tied[1:])

    halves = norm_rows(tokens, norm_gain, routes)
    ahead, behind = list(halves), list(halves)
    steps = ctx_count // 2
    for step in range(1, steps + 1):
        held = ahead + behind
        if step > 1:
            ahead[0], behind[1] = after_projection([ahead[0], behind[1]])
        if step < steps:
            ahead = [lax.ppermute(part, "ctx", forward) for part in ahead]
            behind = [lax.ppermute(part, "ctx", backward) for part in behind[::-1]][::-1]
        else:
            last = [
                lax.ppermute(ahead[0], "ctx", forward),
                lax.ppermute(behind[1], "ctx", backward),
            ]
        if step == 1:
            serve(held[:2], [0])
        else:
            serve(held, [1 - step, step - 1])
    serve(last, [steps])

    attended = attend(plan, queries, positions, own, other)
    pieces = jnp.dot(attended, output_slab, preferred_element_type=jnp.float32).astype(
        jnp.bfloat16
    )
    returned = lax.all_to_all(
        pieces.reshape(ctx_count, MOST, model_width), "ctx", split_axis=0, concat_axis=0, tiled=True
    )

    message = jnp.concatenate(halves, axis=0)
    logits = jnp.dot(
        message[:, :model_width].astype(jnp.float32), router_weight, precision=lax.Precision.HIGHEST
    )
    slots = message[:, model_width : model_width + EXPERTS].astype(jnp.float32)
    gating = jax.nn.softmax(jnp.where(slots >= 0, logits, -jnp.inf), axis=1)
    slot_index = jnp.arange(MOST, dtype=jnp.float32)[None, None, :]
    combine_mat = jnp.where(slots[:, :, None] == slot_index, gating[:, :, None], 0.0)
    combine_mat = combine_mat.reshape(tok_count, EXPERTS * MOST)
    summed = (
        returned.astype(jnp.float32).reshape(EXPERTS, quarter_count, MOST, model_width).sum(axis=1)
    )
    summed = summed.reshape(EXPERTS * MOST, model_width)
    combined = jnp.dot(combine_mat, summed, precision=lax.Precision.HIGHEST)
    return combined.astype(jnp.bfloat16)


def solution(mesh):
    in_specs = (
        P(("groups", "ctx", "exp"), None),
        P(),
        P(),
        P(("groups", "ctx", "exp"), None),
        P(),
        P(),
        P("ctx", None, None),
        P("ctx", None, None),
    )
    out_specs = P(("groups", "ctx", "exp"), None)
    return jax.shard_map(
        per_device, mesh=mesh, in_specs=in_specs, out_specs=out_specs, check_vma=False
    )
```

```python
import functools
import math

import jax
import jax.numpy as jnp
from jax import lax
from jax.experimental import pallas as pl
from jax.experimental.pallas import tpu as pltpu
from jax.sharding import PartitionSpec as P

HS = 128
EXPERTS = 8
MOST = 40
SLOTS = 48
MASKED = -1e30
LANES = 128
MIB = 1 << 20


def ring_rank(place, count):
    place = lax.rem(place + 2 * count, count)
    return jnp.where(place < count // 2, 2 * place, 2 * (count - 1 - place) + 1)


def ring_place(rank, count):
    return jnp.where(rank % 2 == 0, rank // 2, count - 1 - rank // 2)


def ring_owner(offset):
    count = lax.axis_size("ctx")
    return ring_rank(ring_place(lax.axis_index("ctx"), count) + offset, count)


def norm_kernel(tokens_ref, gain_ref, routes_ref, top_ref, bottom_ref):
    floats = tokens_ref[...].astype(jnp.float32)
    count, width = floats.shape
    factor = lax.rsqrt(jnp.mean(floats * floats, axis=1, keepdims=True) + 1e-06)
    normed = (floats * factor * gain_ref[...]).astype(jnp.bfloat16)
    expert = lax.broadcasted_iota(jnp.int32, (LANES, count), 0)
    named = (expert == routes_ref[0:1, :]) | (expert == routes_ref[1:2, :])
    before = lax.broadcasted_iota(jnp.int32, (count, count), 0) < lax.broadcasted_iota(
        jnp.int32, (count, count), 1
    )
    rank = jnp.dot(
        named.astype(jnp.bfloat16),
        before.astype(jnp.bfloat16),
        preferred_element_type=jnp.float32,
    )
    slots = jnp.where(named, rank, -1.0).T.astype(jnp.bfloat16)
    half = count // 2
    for ref, part in ((top_ref, slice(0, half)), (bottom_ref, slice(half, count))):
        ref[:, :width] = normed[part]
        ref[:, width:] = slots[part]


def norm_rows(tokens, norm_gain, routes):
    count, width = tokens.shape
    half = jax.ShapeDtypeStruct((count // 2, width + LANES), jnp.bfloat16)
    return pl.pallas_call(
        norm_kernel, out_shape=[half, half], name="norm_rows"
    )(tokens, norm_gain.reshape(1, -1), routes.T)


def keys_kernel(count, *refs):
    blocks = refs[:count]
    weight_ref, out_ref, mark_ref = refs[count:]
    rows = jnp.concatenate([block[:, : weight_ref.shape[0]] for block in blocks], axis=0)
    product = jnp.dot(rows, weight_ref[...], preferred_element_type=jnp.float32)
    out_ref[...] = product.astype(jnp.bfloat16)
    mark_ref[...] = product[:8, :LANES]


def project_keys(blocks, key_weight):
    row_count = sum(block.shape[0] for block in blocks)
    model_width, width = key_weight.shape
    step = min(width, 256)
    return pl.pallas_call(
        functools.partial(keys_kernel, len(blocks)),
        grid=(width // step,),
        in_specs=[pl.BlockSpec(block.shape, lambda n: (0, 0)) for block in blocks]
        + [pl.BlockSpec((model_width, step), lambda n: (0, n))],
        out_specs=[
            pl.BlockSpec((row_count, step), lambda n: (0, n)),
            pl.BlockSpec((8, LANES), lambda n: (0, 0)),
        ],
        out_shape=[
            jax.ShapeDtypeStruct((row_count, width), jnp.bfloat16),
            jax.ShapeDtypeStruct((8, LANES), jnp.float32),
        ],
        compiler_params=pltpu.CompilerParams(vmem_limit_bytes=12 * MIB),
        name="project_keys",
    )(*blocks, key_weight)


def values_kernel(offsets, count, experts, mark_ref, *refs):
    blocks = refs[:count]
    value_ref, query_ref, panel_ref, out_ref, pos_ref, picked = refs[count:]
    width = value_ref.shape[0]
    rows = jnp.concatenate([block[:, :width] for block in blocks], axis=0)
    tok_count = rows.shape[0] // len(offsets)

    @pl.when(pl.program_id(0) == 0)
    def _():
        slots = jnp.concatenate([block[:, width:] for block in blocks], axis=0)
        slots = slots.astype(jnp.float32)
        expert = lax.axis_index("ctx") // (lax.axis_size("ctx") // experts)
        lane = lax.broadcasted_iota(jnp.int32, slots.shape, 1)
        slot = jnp.sum(jnp.where(lane == expert, slots, 0.0), axis=1, keepdims=True)
        select = (slot == lane.astype(jnp.float32)).astype(jnp.float32)
        number = lax.broadcasted_iota(jnp.int32, (tok_count, LANES), 0).astype(jnp.bfloat16)
        for g, offset in enumerate(offsets):
            part = slice(g * tok_count, (g + 1) * tok_count)
            chosen = select[part].T[:SLOTS].astype(jnp.bfloat16)
            picked[pl.ds(g * SLOTS, SLOTS), :] = jnp.dot(
                chosen, rows[part], preferred_element_type=jnp.float32
            ).astype(jnp.bfloat16)
            start = (ring_owner(offset) * lax.axis_size("exp") + lax.axis_index("exp")) * tok_count
            pos_ref[g] = jnp.dot(
                chosen, number, preferred_element_type=jnp.float32
            ) + start.astype(jnp.float32)

    panel_ref[...] = jnp.dot(
        rows, value_ref[...], preferred_element_type=jnp.float32
    ).astype(jnp.bfloat16)
    queries = jnp.dot(picked[...], query_ref[...], preferred_element_type=jnp.float32)
    for g in range(len(offsets)):
        out_ref[g] = queries[g * SLOTS : (g + 1) * SLOTS].astype(jnp.bfloat16)


def project_values(blocks, offsets, mark, value_weight, query_slab):
    row_count = sum(block.shape[0] for block in blocks)
    model_width, width = value_weight.shape
    step = min(width, 256)
    owners = len(offsets)
    weight_spec = pl.BlockSpec((model_width, step), lambda n: (0, n))
    return pl.pallas_call(
        functools.partial(values_kernel, offsets, len(blocks), EXPERTS),
        grid=(width // step,),
        in_specs=[pl.BlockSpec(mark.shape, lambda n: (0, 0))]
        + [pl.BlockSpec(block.shape, lambda n: (0, 0)) for block in blocks]
        + [weight_spec] * 2,
        out_specs=[
            pl.BlockSpec((row_count, step), lambda n: (0, n)),
            pl.BlockSpec((owners, SLOTS, step), lambda n: (0, 0, n)),
            pl.BlockSpec((owners, SLOTS, LANES), lambda n: (0, 0, 0)),
        ],
        out_shape=[
            jax.ShapeDtypeStruct((row_count, width), jnp.bfloat16),
            jax.ShapeDtypeStruct((owners, SLOTS, width), jnp.bfloat16),
            jax.ShapeDtypeStruct((owners, SLOTS, LANES), jnp.float32),
        ],
        scratch_shapes=[pltpu.VMEM((owners * SLOTS, model_width), jnp.bfloat16)],
        compiler_params=pltpu.CompilerParams(vmem_limit_bytes=16 * MIB),
        name="project_values",
    )(mark, *blocks, value_weight, query_slab)


def attend_kernel(plan, tok_count, heads, flip, *refs):
    count = len(plan)
    query_refs, pos_refs, own_keys, own_values, other_keys, other_values = (
        refs[k * count : (k + 1) * count] for k in range(6)
    )
    out_ref, places, queries, keys, values, scores, weights = refs[6 * count :]
    side = lax.axis_index("exp")
    exp_count = 2
    rate = math.log2(math.e) / math.sqrt(HS)
    tile = 2 * MOST
    per_span = 2 * exp_count
    span = per_span * tok_count
    owners = queries.shape[1]
    half_tiles = owners // 4
    group = min(half_tiles, 4)

    @pl.when(pl.program_id(0) == 0)
    def _():
        for offsets, pos_ref in zip(plan, pos_refs):
            for g, offset in enumerate(offsets):
                places[ring_owner(offset)] = pos_ref[g, :MOST]

    for p, offsets in enumerate(plan):
        for g, offset in enumerate(offsets):
            owner = ring_owner(offset)
            part = pl.ds(g * tok_count, tok_count)
            here, there = owner * exp_count + side, owner * exp_count + 1 - side
            for h in range(heads):
                lanes = pl.ds(h * HS, HS)
                queries[h, owner] = query_refs[p][g, :, lanes].astype(jnp.float32)[:MOST]
                keys[h, here] = own_keys[p][part, lanes]
                values[h, here] = own_values[p][part, lanes]
                keys[h, there] = other_keys[p][part, lanes]
                values[h, there] = other_values[p][part, lanes]

    def serve(lead, first):
        top = lead + group
        for h in range(heads):
            held = queries[h, 2 * lead : 2 * top].reshape(group * tile, HS).astype(jnp.bfloat16)
            for j in range(top):
                skip = max(0, j - lead) * tile
                key_part = keys[h, per_span * j : per_span * (j + 1)].reshape(span, HS)
                scores[h, pl.ds(skip, group * tile - skip), pl.ds(j * span, span)] = (
                    lax.dot_general(
                        held[skip:],
                        key_part,
                        (((1,), (1,)), ((), ())),
                        preferred_element_type=jnp.float32,
                    )
                )
        for h in range(heads):
            for i in range(lead, top):
                reach = (i + 1) * span
                spots = places[2 * i : 2 * i + 2].reshape(tile, LANES)
                for sub in range(0, tile, 16):
                    rows = pl.ds((i - lead) * tile + sub, 16)
                    part = scores[h, rows, pl.ds(0, reach)]
                    last = part[:, reach - span :]
                    key_index = lax.broadcasted_iota(jnp.int32, last.shape, 1) + (reach - span)
                    spot = spots[sub : sub + 16, 0:1]
                    last = jnp.where(key_index.astype(jnp.float32) <= spot, last, MASKED)
                    if i > 0:
                        part = jnp.concatenate([part[:, : reach - span], last], axis=1)
                    else:
                        part = last
                    peak = jnp.max(part, axis=1, keepdims=True)
                    raised = jnp.exp2((part - peak) * rate)
                    total = jnp.sum(raised, axis=1, keepdims=True)
                    weights[h, rows, pl.ds(0, reach)] = (raised * (1.0 / total)).astype(
                        jnp.bfloat16
                    )
        for h in range(heads):
            sums = [None] * group
            for j in range(top):
                skip = max(0, j - lead)
                value_part = values[h, per_span * j : per_span * (j + 1)].reshape(span, HS)
                product = jnp.dot(
                    weights[h, pl.ds(skip * tile, (group - skip) * tile), pl.ds(j * span, span)],
                    value_part,
                    preferred_element_type=jnp.float32,
                )
                for i in range(skip, group):
                    piece = product[(i - skip) * tile : (i - skip + 1) * tile]
                    sums[i] = piece if sums[i] is None else sums[i] + piece
            spare = jnp.zeros((SLOTS - MOST, HS), jnp.float32)
            for i in range(group):
                for part in range(2):
                    rows = jnp.concatenate([sums[i][part * MOST : (part + 1) * MOST], spare], axis=0)
                    place = 2 * (lead - first + i) + part
                    out_ref[place, :, pl.ds(h * HS, HS)] = rows.astype(jnp.bfloat16)

    late = (lax.axis_index("ctx") >= owners // 2) != flip

    @pl.when(late)
    def _():
        for lead in range(half_tiles, 2 * half_tiles, group):
            serve(lead, half_tiles)

    @pl.when(jnp.logical_not(late))
    def _():
        for lead in range(0, half_tiles, group):
            serve(lead, 0)


def attend(flip, plan, queries, positions, own_keys, own_values, other_keys, other_values):
    owners = sum(len(offsets) for offsets in plan)
    row_count = owners * MOST
    width = queries[0].shape[-1]
    heads = 2 if owners <= 8 else 1
    step = heads * HS
    tok_count = own_keys[0].shape[0] // len(plan[0])
    length = owners * 2 * tok_count
    group_rows = min(row_count // 2, 8 * MOST)
    query_specs = [pl.BlockSpec((q.shape[0], SLOTS, step), lambda h: (0, 0, h)) for q in queries]
    pos_specs = [pl.BlockSpec(p.shape, lambda h: (0, 0, 0)) for p in positions]
    panel_specs = [pl.BlockSpec((p.shape[0], step), lambda h: (0, h)) for p in own_keys]
    scratch = heads * (group_rows * length * 6 + length * HS * 4 + row_count * HS * 4)
    windows = 2 * (length * step * 4 + row_count * step * 5) + 5 * row_count * LANES * 4
    return pl.pallas_call(
        functools.partial(attend_kernel, plan, tok_count, heads, flip),
        grid=(width // step,),
        in_specs=query_specs + pos_specs + panel_specs * 4,
        out_specs=pl.BlockSpec((owners // 2, SLOTS, step), lambda h: (0, 0, h)),
        out_shape=jax.ShapeDtypeStruct((owners // 2, SLOTS, width), jnp.bfloat16),
        scratch_shapes=[
            pltpu.VMEM((owners, MOST, LANES), jnp.float32),
            pltpu.VMEM((heads, owners, MOST, HS), jnp.float32),
            pltpu.VMEM((heads, 2 * owners, tok_count, HS), jnp.bfloat16),
            pltpu.VMEM((heads, 2 * owners, tok_count, HS), jnp.bfloat16),
            pltpu.VMEM((heads, group_rows, length), jnp.float32),
            pltpu.VMEM((heads, group_rows, length), jnp.bfloat16),
        ],
        compiler_params=pltpu.CompilerParams(vmem_limit_bytes=scratch + windows * 5 // 4 + 4 * MIB),
        name="attend",
    )(*queries, *positions, *own_keys, *own_values, *other_keys, *other_values)


def output_kernel(attended_ref, weight_ref, *refs):
    outs, pieces = refs[:-1], refs[-1]
    count, _, width = attended_ref.shape
    rows = attended_ref[...].reshape(count * SLOTS, width)
    product = jnp.dot(rows, weight_ref[...], preferred_element_type=jnp.float32)
    for b in range(count):
        pieces[b] = product[b * SLOTS : b * SLOTS + MOST]
    own = lax.rem(lax.axis_index("ctx"), count)
    for r, out_ref in enumerate(outs):
        out_ref[...] = pieces[own ^ r].astype(jnp.bfloat16)


def project_output(attended, output_slab):
    count, _, width = attended.shape
    model_width = output_slab.shape[1]
    step = 512
    return pl.pallas_call(
        output_kernel,
        grid=(model_width // step,),
        in_specs=[
            pl.BlockSpec(attended.shape, lambda n: (0, 0, 0)),
            pl.BlockSpec((width, step), lambda n: (0, n)),
        ],
        out_specs=[pl.BlockSpec((MOST, step), lambda n: (0, n))] * count,
        out_shape=[jax.ShapeDtypeStruct((MOST, model_width), jnp.bfloat16)] * count,
        scratch_shapes=[pltpu.VMEM((count, MOST, step), jnp.float32)],
        compiler_params=pltpu.CompilerParams(vmem_limit_bytes=12 * MIB),
        name="project_output",
    )(attended, output_slab)


def combine_kernel(quarter_count, slots_ref, gates_ref, *refs):
    pieces, out_ref, mix = refs[:-2], refs[-2], refs[-1]
    tok_count = slots_ref.shape[0]

    @pl.when(pl.program_id(0) == 0)
    def _():
        slots = slots_ref[...].astype(jnp.float32)
        gates = gates_ref[...]
        lane = lax.broadcasted_iota(jnp.int32, slots.shape, 1)
        wide = lax.broadcasted_iota(jnp.int32, (tok_count, len(pieces) * SLOTS), 1).astype(
            jnp.float32
        )
        total = jnp.zeros_like(wide)
        for k in range(len(pieces)):
            mine = lane == (lax.axis_index("ctx") ^ k) // quarter_count
            slot = jnp.sum(jnp.where(mine, slots, 0.0), axis=1, keepdims=True)
            gate = jnp.sum(jnp.where(mine, gates, 0.0), axis=1, keepdims=True)
            spot = jnp.where(slot >= 0, slot + float(k * SLOTS), -1.0)
            total = total + jnp.where(wide == spot, gate, 0.0)
        for part in range(3):
            term = total.astype(jnp.bfloat16)
            mix[pl.ds(part * tok_count, tok_count), :] = term
            total = total - term.astype(jnp.float32)

    spare = jnp.zeros((SLOTS - MOST, out_ref.shape[1]), jnp.float32)
    rows = []
    for piece in pieces:
        rows += [piece[...].astype(jnp.float32), spare]
    rows = jnp.concatenate(rows, axis=0).astype(jnp.bfloat16)
    product = jnp.dot(mix[...], rows, preferred_element_type=jnp.float32)
    total = product[:tok_count] + (
        product[tok_count : 2 * tok_count] + product[2 * tok_count :]
    )
    out_ref[...] = total.astype(jnp.bfloat16)


def combine(quarter_count, slots, gates, pieces):
    tok_count = slots.shape[0]
    model_width = pieces[0].shape[1]
    step = 512
    return pl.pallas_call(
        functools.partial(combine_kernel, quarter_count),
        grid=(model_width // step,),
        in_specs=[pl.BlockSpec((tok_count, LANES), lambda n: (0, 0))] * 2
        + [pl.BlockSpec((MOST, step), lambda n: (0, n))] * len(pieces),
        out_specs=pl.BlockSpec((tok_count, step), lambda n: (0, n)),
        out_shape=jax.ShapeDtypeStruct((tok_count, model_width), jnp.bfloat16),
        scratch_shapes=[pltpu.VMEM((3 * tok_count, len(pieces) * SLOTS), jnp.bfloat16)],
        compiler_params=pltpu.CompilerParams(vmem_limit_bytes=24 * MIB),
        name="combine",
    )(slots, gates, *pieces)


def per_device(
    tokens, norm_gain, router_weight, routes, key_weight, value_weight, query_weight, output_weight
):
    tok_count, model_width = tokens.shape
    ctx_count = lax.axis_size("ctx")
    exp_count = lax.axis_size("exp")
    quarter_count = ctx_count // EXPERTS
    head_width = query_weight.shape[2]
    ranks = list(range(0, ctx_count, 2)) + list(range(1, ctx_count, 2))[::-1]
    forward = [(ranks[p], ranks[(p + 1) % ctx_count]) for p in range(ctx_count)]
    backward = [(b, a) for a, b in forward]
    sibling = [(e, 1 - e) for e in range(exp_count)]
    query_slab = query_weight[0]
    output_slab = output_weight[0]
    if quarter_count > 1:
        first = (lax.axis_index("ctx") % quarter_count) * head_width
        key_weight = lax.dynamic_slice_in_dim(key_weight, first, head_width, axis=1)
        value_weight = lax.dynamic_slice_in_dim(value_weight, first, head_width, axis=1)

    halves = norm_rows(tokens, norm_gain, routes)
    steps = ctx_count // 2
    plan = [[0]] + [[-step, step] for step in range(1, steps)] + [[steps]]
    arrived = {0: list(halves)}
    own_keys, own_values, queries, positions = [], [], [], []
    lead = [halves[0], halves[1]]
    rest = [halves[1], halves[0]]
    for step in range(1, steps + 1):
        done = step - 1
        blocks = arrived[done]
        if done == 0:
            lead = [lax.ppermute(lead[0], "ctx", forward), lax.ppermute(lead[1], "ctx", backward)]
            rest = [lax.ppermute(rest[0], "ctx", forward), lax.ppermute(rest[1], "ctx", backward)]
        keys, mark = project_keys(blocks, key_weight)
        if step < steps:
            mark, *lead_next = lax.optimization_barrier((mark, *lead))
        else:
            lead_next = lead
        values, query, position = project_values(
            blocks, plan[done], mark, value_weight, query_slab
        )
        if step < steps:
            position, *rest_next = lax.optimization_barrier((position, *rest))
            arrived[step] = [lead[0], rest[0], rest[1], lead[1]]
            lead = [
                lax.ppermute(lead_next[0], "ctx", forward),
                lax.ppermute(lead_next[1], "ctx", backward),
            ]
            if step < steps - 1:
                rest = [
                    lax.ppermute(rest_next[0], "ctx", forward),
                    lax.ppermute(rest_next[1], "ctx", backward),
                ]
        else:
            arrived[step] = [lead[0], lead[1]]
        own_keys.append(keys)
        own_values.append(values)
        queries.append(query)
        positions.append(position)

    def hand_over(panel):
        return lax.ppermute(panel, "exp", sibling)

    other_keys = [hand_over(panel) for panel in own_keys[:-1]]
    other_values = [hand_over(panel) for panel in own_values[:-1]]
    late_keys, late_values, *last = lax.optimization_barrier(
        (own_keys[-1], own_values[-1], *arrived[steps])
    )
    other_keys.append(hand_over(late_keys))
    other_values.append(hand_over(late_values))
    keys, mark = project_keys(last, key_weight)
    values, query, position = project_values(last, plan[-1], mark, value_weight, query_slab)
    own_keys.append(keys)
    own_values.append(values)
    queries.append(query)
    positions.append(position)
    other_keys.append(hand_over(keys))
    other_values.append(hand_over(values))

    panels = (own_keys, own_values, other_keys, other_values)
    attended = attend(True, plan, queries, positions, *panels)
    far = project_output(attended, output_slab)
    positions[0], *far = lax.optimization_barrier((positions[0], *far))
    half = ctx_count // 2

    def swap(piece, k):
        return lax.ppermute(piece, "ctx", [(c, c ^ k) for c in range(ctx_count)])

    far = [swap(piece, half + r) for r, piece in enumerate(far)]
    attended = attend(False, plan, queries, positions, *panels)
    near = project_output(attended, output_slab)
    tied = lax.optimization_barrier((*near, *far))
    near, far = tied[:half], list(tied[half:])
    near = [near[0]] + [swap(near[r], r) for r in range(1, half)]

    message = jnp.concatenate(halves, axis=0)
    logits = jnp.dot(
        message[:, :model_width].astype(jnp.float32), router_weight, precision=lax.Precision.HIGHEST
    )
    slots = message[:, model_width:]
    gating = jax.nn.softmax(jnp.where(slots[:, :EXPERTS] >= 0, logits, -jnp.inf), axis=1)
    gates = jnp.pad(gating, ((0, 0), (0, LANES - EXPERTS)))
    return combine(quarter_count, slots, gates, near + far)


def solution(mesh):
    in_specs = (
        P(("groups", "ctx", "exp"), None),
        P(),
        P(),
        P(("groups", "ctx", "exp"), None),
        P(),
        P(),
        P("ctx", None, None),
        P("ctx", None, None),
    )
    out_specs = P(("groups", "ctx", "exp"), None)
    return jax.shard_map(
        per_device, mesh=mesh, in_specs=in_specs, out_specs=out_specs, check_vma=False
    )
```

```python
import functools
import math

import jax
import jax.numpy as jnp
from jax import lax
from jax.experimental import pallas as pl
from jax.experimental.pallas import tpu as pltpu
from jax.sharding import PartitionSpec as P

HS = 128
EXPERTS = 8
MOST = 40
SLOTS = 48
MASKED = -1e30
LANES = 128
MIB = 1 << 20


def ring_rank(place, count):
    place = lax.rem(place + 2 * count, count)
    return jnp.where(place < count // 2, 2 * place, 2 * (count - 1 - place) + 1)


def ring_place(rank, count):
    return jnp.where(rank % 2 == 0, rank // 2, count - 1 - rank // 2)


def ring_owner(offset):
    count = lax.axis_size("ctx")
    return ring_rank(ring_place(lax.axis_index("ctx"), count) + offset, count)


def norm_kernel(tokens_ref, gain_ref, routes_ref, top_ref, bottom_ref):
    floats = tokens_ref[...].astype(jnp.float32)
    count, width = floats.shape
    factor = lax.rsqrt(jnp.mean(floats * floats, axis=1, keepdims=True) + 1e-06)
    normed = (floats * factor * gain_ref[...]).astype(jnp.bfloat16)
    expert = lax.broadcasted_iota(jnp.int32, (LANES, count), 0)
    named = (expert == routes_ref[0:1, :]) | (expert == routes_ref[1:2, :])
    before = lax.broadcasted_iota(jnp.int32, (count, count), 0) < lax.broadcasted_iota(
        jnp.int32, (count, count), 1
    )
    rank = jnp.dot(
        named.astype(jnp.bfloat16),
        before.astype(jnp.bfloat16),
        preferred_element_type=jnp.float32,
    )
    slots = jnp.where(named, rank, -1.0).T.astype(jnp.bfloat16)
    half = count // 2
    for ref, part in ((top_ref, slice(0, half)), (bottom_ref, slice(half, count))):
        ref[:, :width] = normed[part]
        ref[:, width:] = slots[part]


def norm_rows(tokens, norm_gain, routes):
    count, width = tokens.shape
    half = jax.ShapeDtypeStruct((count // 2, width + LANES), jnp.bfloat16)
    return pl.pallas_call(
        norm_kernel, out_shape=[half, half], name="norm_rows"
    )(tokens, norm_gain.reshape(1, -1), routes.T)


def keys_kernel(count, *refs):
    blocks = refs[:count]
    weight_ref, panel_ref, mark_ref = refs[count:]
    rows = jnp.concatenate([block[:, : weight_ref.shape[0]] for block in blocks], axis=0)
    product = jnp.dot(rows, weight_ref[...], preferred_element_type=jnp.float32)
    panel_ref[0] = product.astype(jnp.bfloat16)
    mark_ref[...] = product[:8, :LANES]


def project_keys(blocks, key_weight):
    row_count = sum(block.shape[0] for block in blocks)
    model_width, width = key_weight.shape
    step = min(width, 256)
    return pl.pallas_call(
        functools.partial(keys_kernel, len(blocks)),
        grid=(width // step,),
        in_specs=[pl.BlockSpec(block.shape, lambda n: (0, 0)) for block in blocks]
        + [pl.BlockSpec((model_width, step), lambda n: (0, n))],
        out_specs=[
            pl.BlockSpec((1, row_count, step), lambda n: (0, 0, n)),
            pl.BlockSpec((8, LANES), lambda n: (0, 0)),
        ],
        out_shape=[
            jax.ShapeDtypeStruct((2, row_count, width), jnp.bfloat16),
            jax.ShapeDtypeStruct((8, LANES), jnp.float32),
        ],
        compiler_params=pltpu.CompilerParams(vmem_limit_bytes=12 * MIB),
        name="project_keys",
    )(*blocks, key_weight)


def values_kernel(offsets, count, experts, mark_ref, half_panel_ref, *refs):
    blocks = refs[:count]
    value_ref, panel_ref, picked_ref, pos_ref = refs[count:]
    width = value_ref.shape[0]
    rows = jnp.concatenate([block[:, :width] for block in blocks], axis=0)
    tok_count = rows.shape[0] // len(offsets)

    @pl.when(pl.program_id(0) == 0)
    def _():
        slots = jnp.concatenate([block[:, width:] for block in blocks], axis=0)
        slots = slots.astype(jnp.float32)
        expert = lax.axis_index("ctx") // (lax.axis_size("ctx") // experts)
        lane = lax.broadcasted_iota(jnp.int32, slots.shape, 1)
        slot = jnp.sum(jnp.where(lane == expert, slots, 0.0), axis=1, keepdims=True)
        select = (slot == lane.astype(jnp.float32)).astype(jnp.float32)
        number = lax.broadcasted_iota(jnp.int32, (tok_count, LANES), 0).astype(jnp.bfloat16)
        for g, offset in enumerate(offsets):
            part = slice(g * tok_count, (g + 1) * tok_count)
            chosen = select[part].T[:SLOTS].astype(jnp.bfloat16)
            picked_ref[g] = jnp.dot(
                chosen, rows[part], preferred_element_type=jnp.float32
            ).astype(jnp.bfloat16)
            start = (ring_owner(offset) * lax.axis_size("exp") + lax.axis_index("exp")) * tok_count
            pos_ref[g] = jnp.dot(
                chosen, number, preferred_element_type=jnp.float32
            ) + start.astype(jnp.float32)

    panel_ref[0] = jnp.dot(
        rows, value_ref[...], preferred_element_type=jnp.float32
    ).astype(jnp.bfloat16)


def project_values(blocks, offsets, mark, panel, value_weight):
    row_count = sum(block.shape[0] for block in blocks)
    model_width, width = value_weight.shape
    step = min(width, 256)
    owners = len(offsets)
    return pl.pallas_call(
        functools.partial(values_kernel, offsets, len(blocks), EXPERTS),
        grid=(width // step,),
        in_specs=[
            pl.BlockSpec(mark.shape, lambda n: (0, 0)),
            pl.BlockSpec(memory_space=pl.ANY),
        ]
        + [pl.BlockSpec(block.shape, lambda n: (0, 0)) for block in blocks]
        + [pl.BlockSpec((model_width, step), lambda n: (0, n))],
        out_specs=[
            pl.BlockSpec((1, row_count, step), lambda n: (1, 0, n)),
            pl.BlockSpec((owners, SLOTS, model_width), lambda n: (0, 0, 0)),
            pl.BlockSpec((owners, SLOTS, LANES), lambda n: (0, 0, 0)),
        ],
        out_shape=[
            jax.ShapeDtypeStruct((2, row_count, width), jnp.bfloat16),
            jax.ShapeDtypeStruct((owners, SLOTS, model_width), jnp.bfloat16),
            jax.ShapeDtypeStruct((owners, SLOTS, LANES), jnp.float32),
        ],
        input_output_aliases={1: 0},
        compiler_params=pltpu.CompilerParams(vmem_limit_bytes=12 * MIB),
        name="project_values",
    )(mark, panel, *blocks, value_weight)


def queries_kernel(*refs):
    *picked, weight_ref, out_ref = refs
    rows = [ref[g] for ref in picked for g in range(ref.shape[0])]
    product = jnp.dot(
        jnp.concatenate(rows, axis=0), weight_ref[...], preferred_element_type=jnp.float32
    )
    for g in range(len(rows)):
        out_ref[g] = product[g * SLOTS : (g + 1) * SLOTS].astype(jnp.bfloat16)


def project_queries(picked, query_slab):
    model_width, width = query_slab.shape
    step = min(width, 256)
    owners = sum(rows.shape[0] for rows in picked)
    held = owners * SLOTS * (4 * model_width + 12 * step) * 2
    return pl.pallas_call(
        queries_kernel,
        grid=(width // step,),
        in_specs=[pl.BlockSpec(rows.shape, lambda n: (0, 0, 0)) for rows in picked]
        + [pl.BlockSpec((model_width, step), lambda n: (0, n))],
        out_specs=pl.BlockSpec((owners, SLOTS, step), lambda n: (0, 0, n)),
        out_shape=jax.ShapeDtypeStruct((owners, SLOTS, width), jnp.bfloat16),
        compiler_params=pltpu.CompilerParams(vmem_limit_bytes=held + 6 * MIB),
        name="project_queries",
    )(*picked, query_slab)


def attend_kernel(plan, tok_count, heads, flip, query_count, *refs):
    count = len(plan)
    query_refs, refs = refs[:query_count], refs[query_count:]
    pos_refs, own_refs, other_refs = (refs[k * count : (k + 1) * count] for k in range(3))
    out_ref, places, queries, keys, values, scores, weights = refs[3 * count :]
    query_parts = [(ref, g) for ref in query_refs for g in range(ref.shape[0])]
    side = lax.axis_index("exp")
    exp_count = 2
    rate = math.log2(math.e) / math.sqrt(HS)
    tile = 2 * MOST
    per_span = 2 * exp_count
    span = per_span * tok_count
    owners = queries.shape[1]
    half_tiles = owners // 4
    group = min(half_tiles, 4)

    @pl.when(pl.program_id(0) == 0)
    def _():
        for offsets, pos_ref in zip(plan, pos_refs):
            for g, offset in enumerate(offsets):
                places[ring_owner(offset)] = pos_ref[g, :MOST]

    for offsets, own_ref, other_ref in zip(plan, own_refs, other_refs):
        for g, offset in enumerate(offsets):
            owner = ring_owner(offset)
            query_ref, place = query_parts.pop(0)
            part = pl.ds(g * tok_count, tok_count)
            here, there = owner * exp_count + side, owner * exp_count + 1 - side
            for h in range(heads):
                lanes = pl.ds(h * HS, HS)
                queries[h, owner] = query_ref[place, :, lanes].astype(jnp.float32)[:MOST]
                keys[h, here] = own_ref[0, part, lanes]
                values[h, here] = own_ref[1, part, lanes]
                keys[h, there] = other_ref[0, part, lanes]
                values[h, there] = other_ref[1, part, lanes]

    def serve(lead, first):
        top = lead + group
        for h in range(heads):
            held = queries[h, 2 * lead : 2 * top].reshape(group * tile, HS).astype(jnp.bfloat16)
            for j in range(top):
                skip = max(0, j - lead) * tile
                key_part = keys[h, per_span * j : per_span * (j + 1)].reshape(span, HS)
                scores[h, pl.ds(skip, group * tile - skip), pl.ds(j * span, span)] = (
                    lax.dot_general(
                        held[skip:],
                        key_part,
                        (((1,), (1,)), ((), ())),
                        preferred_element_type=jnp.float32,
                    )
                )
        for h in range(heads):
            for i in range(lead, top):
                reach = (i + 1) * span
                spots = places[2 * i : 2 * i + 2].reshape(tile, LANES)
                for sub in range(0, tile, 16):
                    rows = pl.ds((i - lead) * tile + sub, 16)
                    part = scores[h, rows, pl.ds(0, reach)]
                    last = part[:, reach - span :]
                    key_index = lax.broadcasted_iota(jnp.int32, last.shape, 1) + (reach - span)
                    spot = spots[sub : sub + 16, 0:1]
                    last = jnp.where(key_index.astype(jnp.float32) <= spot, last, MASKED)
                    if i > 0:
                        part = jnp.concatenate([part[:, : reach - span], last], axis=1)
                    else:
                        part = last
                    peak = jnp.max(part, axis=1, keepdims=True)
                    raised = jnp.exp2((part - peak) * rate)
                    total = jnp.sum(raised, axis=1, keepdims=True)
                    weights[h, rows, pl.ds(0, reach)] = (raised * (1.0 / total)).astype(
                        jnp.bfloat16
                    )
        for h in range(heads):
            sums = [None] * group
            for j in range(top):
                skip = max(0, j - lead)
                value_part = values[h, per_span * j : per_span * (j + 1)].reshape(span, HS)
                product = jnp.dot(
                    weights[h, pl.ds(skip * tile, (group - skip) * tile), pl.ds(j * span, span)],
                    value_part,
                    preferred_element_type=jnp.float32,
                )
                for i in range(skip, group):
                    piece = product[(i - skip) * tile : (i - skip + 1) * tile]
                    sums[i] = piece if sums[i] is None else sums[i] + piece
            spare = jnp.zeros((SLOTS - MOST, HS), jnp.float32)
            for i in range(group):
                for part in range(2):
                    rows = jnp.concatenate([sums[i][part * MOST : (part + 1) * MOST], spare], axis=0)
                    place = 2 * (lead - first + i) + part
                    out_ref[place, :, pl.ds(h * HS, HS)] = rows.astype(jnp.bfloat16)

    late = (lax.axis_index("ctx") >= owners // 2) != flip

    @pl.when(late)
    def _():
        for lead in range(half_tiles, 2 * half_tiles, group):
            serve(lead, half_tiles)

    @pl.when(jnp.logical_not(late))
    def _():
        for lead in range(0, half_tiles, group):
            serve(lead, 0)


def attend(flip, plan, queries, positions, own, other):
    owners = sum(len(offsets) for offsets in plan)
    row_count = owners * MOST
    width = queries[0].shape[-1]
    heads = 2 if owners <= 8 else 1
    step = heads * HS
    tok_count = own[0].shape[1] // len(plan[0])
    length = owners * 2 * tok_count
    group_rows = min(row_count // 2, 8 * MOST)
    query_specs = [pl.BlockSpec((q.shape[0], SLOTS, step), lambda h: (0, 0, h)) for q in queries]
    pos_specs = [pl.BlockSpec(p.shape, lambda h: (0, 0, 0)) for p in positions]
    panel_specs = [pl.BlockSpec((2, p.shape[1], step), lambda h: (0, 0, h)) for p in own]
    scratch = heads * (group_rows * length * 6 + length * HS * 4 + row_count * HS * 4)
    windows = 2 * (length * step * 4 + row_count * step * 5) + 5 * row_count * LANES * 4
    return pl.pallas_call(
        functools.partial(attend_kernel, plan, tok_count, heads, flip, len(queries)),
        grid=(width // step,),
        in_specs=query_specs + pos_specs + panel_specs * 2,
        out_specs=pl.BlockSpec((owners // 2, SLOTS, step), lambda h: (0, 0, h)),
        out_shape=jax.ShapeDtypeStruct((owners // 2, SLOTS, width), jnp.bfloat16),
        scratch_shapes=[
            pltpu.VMEM((owners, MOST, LANES), jnp.float32),
            pltpu.VMEM((heads, owners, MOST, HS), jnp.float32),
            pltpu.VMEM((heads, 2 * owners, tok_count, HS), jnp.bfloat16),
            pltpu.VMEM((heads, 2 * owners, tok_count, HS), jnp.bfloat16),
            pltpu.VMEM((heads, group_rows, length), jnp.float32),
            pltpu.VMEM((heads, group_rows, length), jnp.bfloat16),
        ],
        compiler_params=pltpu.CompilerParams(vmem_limit_bytes=scratch + windows * 5 // 4 + 4 * MIB),
        name="attend",
    )(*queries, *positions, *own, *other)


def output_kernel(attended_ref, weight_ref, *refs):
    outs, pieces = refs[:-1], refs[-1]
    count, _, width = attended_ref.shape
    rows = attended_ref[...].reshape(count * SLOTS, width)
    product = jnp.dot(rows, weight_ref[...], preferred_element_type=jnp.float32)
    for b in range(count):
        pieces[b] = product[b * SLOTS : b * SLOTS + MOST]
    own = lax.rem(lax.axis_index("ctx"), count)
    for r, out_ref in enumerate(outs):
        out_ref[...] = pieces[own ^ r].astype(jnp.bfloat16)


def project_output(attended, output_slab):
    count, _, width = attended.shape
    model_width = output_slab.shape[1]
    step = 512
    return pl.pallas_call(
        output_kernel,
        grid=(model_width // step,),
        in_specs=[
            pl.BlockSpec(attended.shape, lambda n: (0, 0, 0)),
            pl.BlockSpec((width, step), lambda n: (0, n)),
        ],
        out_specs=[pl.BlockSpec((MOST, step), lambda n: (0, n))] * count,
        out_shape=[jax.ShapeDtypeStruct((MOST, model_width), jnp.bfloat16)] * count,
        scratch_shapes=[pltpu.VMEM((count, MOST, step), jnp.float32)],
        compiler_params=pltpu.CompilerParams(vmem_limit_bytes=12 * MIB),
        name="project_output",
    )(attended, output_slab)


def mix_kernel(quarter_count, top_ref, bottom_ref, logits_ref, mix_ref):
    slots = jnp.concatenate([top_ref[...], bottom_ref[...]], axis=0).astype(jnp.float32)
    tok_count = slots.shape[0]
    logits = jnp.where(slots >= 0, logits_ref[...], -jnp.inf)
    raised = jnp.exp(logits - jnp.max(logits, axis=1, keepdims=True))
    gates = raised / jnp.sum(raised, axis=1, keepdims=True)
    lane = lax.broadcasted_iota(jnp.int32, slots.shape, 1)
    count = mix_ref.shape[1] // SLOTS
    wide = lax.broadcasted_iota(jnp.int32, (tok_count, count * SLOTS), 1).astype(jnp.float32)
    total = jnp.zeros_like(wide)
    for k in range(count):
        mine = lane == (lax.axis_index("ctx") ^ k) // quarter_count
        slot = jnp.sum(jnp.where(mine, slots, 0.0), axis=1, keepdims=True)
        gate = jnp.sum(jnp.where(mine, gates, 0.0), axis=1, keepdims=True)
        spot = jnp.where(slot >= 0, slot + float(k * SLOTS), -1.0)
        total = total + jnp.where(wide == spot, gate, 0.0)
    for part in range(3):
        term = total.astype(jnp.bfloat16)
        mix_ref[pl.ds(part * tok_count, tok_count), :] = term
        total = total - term.astype(jnp.float32)


def gate_mix(quarter_count, halves, logits, count):
    half, width = halves[0].shape
    tok_count = 2 * half
    lanes = width // LANES - 1
    return pl.pallas_call(
        functools.partial(mix_kernel, quarter_count),
        grid=(1,),
        in_specs=[pl.BlockSpec((half, LANES), lambda n: (0, lanes))] * 2
        + [pl.BlockSpec((tok_count, LANES), lambda n: (0, 0))],
        out_specs=pl.BlockSpec((3 * tok_count, count * SLOTS), lambda n: (0, 0)),
        out_shape=jax.ShapeDtypeStruct((3 * tok_count, count * SLOTS), jnp.bfloat16),
        compiler_params=pltpu.CompilerParams(vmem_limit_bytes=16 * MIB),
        name="gate_mix",
    )(*halves, logits)


def combine_kernel(mix_ref, *refs):
    pieces, out_ref = refs[:-1], refs[-1]
    tok_count = out_ref.shape[0]
    spare = jnp.zeros((SLOTS - MOST, out_ref.shape[1]), jnp.float32)
    rows = []
    for piece in pieces:
        rows += [piece[...].astype(jnp.float32), spare]
    rows = jnp.concatenate(rows, axis=0).astype(jnp.bfloat16)
    product = jnp.dot(mix_ref[...], rows, preferred_element_type=jnp.float32)
    total = product[:tok_count] + (
        product[tok_count : 2 * tok_count] + product[2 * tok_count :]
    )
    out_ref[...] = total.astype(jnp.bfloat16)


def combine(mix, pieces):
    tok_count = mix.shape[0] // 3
    model_width = pieces[0].shape[1]
    step = 512
    return pl.pallas_call(
        combine_kernel,
        grid=(model_width // step,),
        in_specs=[pl.BlockSpec(mix.shape, lambda n: (0, 0))]
        + [pl.BlockSpec((MOST, step), lambda n: (0, n))] * len(pieces),
        out_specs=pl.BlockSpec((tok_count, step), lambda n: (0, n)),
        out_shape=jax.ShapeDtypeStruct((tok_count, model_width), jnp.bfloat16),
        compiler_params=pltpu.CompilerParams(vmem_limit_bytes=24 * MIB),
        name="combine",
    )(mix, *pieces)


def per_device(
    tokens, norm_gain, router_weight, routes, key_weight, value_weight, query_weight, output_weight
):
    tok_count, model_width = tokens.shape
    ctx_count = lax.axis_size("ctx")
    exp_count = lax.axis_size("exp")
    quarter_count = ctx_count // EXPERTS
    head_width = query_weight.shape[2]
    ranks = list(range(0, ctx_count, 2)) + list(range(1, ctx_count, 2))[::-1]
    forward = [(ranks[p], ranks[(p + 1) % ctx_count]) for p in range(ctx_count)]
    backward = [(b, a) for a, b in forward]
    sibling = [(e, 1 - e) for e in range(exp_count)]
    query_slab = query_weight[0]
    output_slab = output_weight[0]
    if quarter_count > 1:
        first = (lax.axis_index("ctx") % quarter_count) * head_width
        key_weight = lax.dynamic_slice_in_dim(key_weight, first, head_width, axis=1)
        value_weight = lax.dynamic_slice_in_dim(value_weight, first, head_width, axis=1)

    halves = norm_rows(tokens, norm_gain, routes)
    steps = ctx_count // 2
    plan = [[0]] + [[-step, step] for step in range(1, steps)] + [[steps]]
    own, other, picked, queries, positions = [], [], [], [], []

    def send(parts):
        return [lax.ppermute(parts[0], "ctx", forward), lax.ppermute(parts[1], "ctx", backward)]

    def hand_over(panel):
        return lax.ppermute(panel, "exp", sibling)

    def tie(*arrays):
        return lax.optimization_barrier(arrays)

    blocks = halves
    lead = send([halves[0], halves[1]])
    rest = send([halves[1], halves[0]])
    for step in range(steps):
        panel, mark = project_keys(blocks, key_weight)
        following = [lead[0], rest[0], rest[1], lead[1]]
        if step == steps - 2:
            queries.append(project_queries(picked, query_slab))
            picked = []
        if step < steps - 1:
            mark, *lead_next = tie(mark, *lead, *queries)
            if queries:
                queries = lead_next[-1:]
            lead = send(lead_next[:2])
        panel, rows, position = project_values(blocks, plan[step], mark, panel, value_weight)
        if step < steps - 2:
            position, *rest_next = tie(position, *rest)
            rest = send(rest_next)
        own.append(panel)
        picked.append(rows)
        positions.append(position)
        if step < steps - 1:
            other.append(hand_over(panel))
        blocks = following
    own[-1], last_one, last_two = tie(own[-1], *lead)
    other.append(hand_over(own[-1]))
    blocks = [last_one, last_two]
    panel, mark = project_keys(blocks, key_weight)
    panel, rows, position = project_values(blocks, plan[-1], mark, panel, value_weight)
    own.append(panel)
    other.append(hand_over(panel))
    positions.append(position)
    queries.append(project_queries(picked + [rows], query_slab))

    attended = attend(True, plan, queries, positions, own, other)
    far = project_output(attended, output_slab)
    positions[0], *far = tie(positions[0], *far)
    half = ctx_count // 2

    def swap(piece, k):
        return lax.ppermute(piece, "ctx", [(c, c ^ k) for c in range(ctx_count)])

    far = [swap(piece, half + r) for r, piece in enumerate(far)]
    attended = attend(False, plan, queries, positions, own, other)
    near = project_output(attended, output_slab)
    tied = tie(*near, *far[: half // 2])
    near, far = tied[:half], list(tied[half:]) + far[half // 2 :]
    near = [near[0]] + [swap(near[r], r) for r in range(1, half)]

    normed = jnp.concatenate([part[:, :model_width] for part in halves], axis=0)
    logits = jnp.dot(normed.astype(jnp.float32), router_weight, precision=lax.Precision.HIGHEST)
    logits = jnp.pad(logits, ((0, 0), (0, LANES - EXPERTS)))
    mix = gate_mix(quarter_count, halves, logits, ctx_count)
    return combine(mix, near + far)


def solution(mesh):
    in_specs = (
        P(("groups", "ctx", "exp"), None),
        P(),
        P(),
        P(("groups", "ctx", "exp"), None),
        P(),
        P(),
        P("ctx", None, None),
        P("ctx", None, None),
    )
    out_specs = P(("groups", "ctx", "exp"), None)
    return jax.shard_map(
        per_device, mesh=mesh, in_specs=in_specs, out_specs=out_specs, check_vma=False
    )
```

```python
import functools
import math

import jax
import jax.numpy as jnp
from jax import lax
from jax.experimental import pallas as pl
from jax.experimental.pallas import tpu as pltpu
from jax.sharding import PartitionSpec as P

HS = 128
EXPERTS = 8
MOST = 40
SLOTS = 48
MASKED = -1e30
LANES = 128
MIB = 1 << 20


def ring_rank(place, count):
    place = lax.rem(place + 2 * count, count)
    return jnp.where(place < count // 2, 2 * place, 2 * (count - 1 - place) + 1)


def ring_place(rank, count):
    return jnp.where(rank % 2 == 0, rank // 2, count - 1 - rank // 2)


def ring_owner(offset):
    count = lax.axis_size("ctx")
    return ring_rank(ring_place(lax.axis_index("ctx"), count) + offset, count)


def norm_kernel(tokens_ref, gain_ref, routes_ref, top_ref, bottom_ref):
    floats = tokens_ref[...].astype(jnp.float32)
    count, width = floats.shape
    factor = lax.rsqrt(jnp.mean(floats * floats, axis=1, keepdims=True) + 1e-06)
    normed = (floats * factor * gain_ref[...]).astype(jnp.bfloat16)
    expert = lax.broadcasted_iota(jnp.int32, (LANES, count), 0)
    named = (expert == routes_ref[0:1, :]) | (expert == routes_ref[1:2, :])
    before = lax.broadcasted_iota(jnp.int32, (count, count), 0) < lax.broadcasted_iota(
        jnp.int32, (count, count), 1
    )
    rank = jnp.dot(
        named.astype(jnp.bfloat16),
        before.astype(jnp.bfloat16),
        preferred_element_type=jnp.float32,
    )
    slots = jnp.where(named, rank, -1.0).T.astype(jnp.bfloat16)
    half = count // 2
    for ref, part in ((top_ref, slice(0, half)), (bottom_ref, slice(half, count))):
        ref[:, :width] = normed[part]
        ref[:, width:] = slots[part]


def norm_rows(tokens, norm_gain, routes):
    count, width = tokens.shape
    half = jax.ShapeDtypeStruct((count // 2, width + LANES), jnp.bfloat16)
    return pl.pallas_call(
        norm_kernel,
        out_shape=[half, half],
        compiler_params=pltpu.CompilerParams(vmem_limit_bytes=8 * MIB),
        name="norm_rows",
    )(tokens, norm_gain.reshape(1, -1), routes.T)


def column_parts(ref):
    step = min(ref.shape[1], 256)
    return [pl.ds(start, step) for start in range(0, ref.shape[1], step)]


WHOLE = pl.BlockSpec(memory_space=pltpu.VMEM)


def keys_kernel(count, *refs):
    blocks = refs[:count]
    weight_ref, panel_ref, mark_ref = refs[count:]
    rows = jnp.concatenate([block[:, : weight_ref.shape[0]] for block in blocks], axis=0)
    for cols in column_parts(weight_ref):
        product = jnp.dot(rows, weight_ref[:, cols], preferred_element_type=jnp.float32)
        panel_ref[:, cols] = product.astype(jnp.bfloat16)
    mark_ref[...] = product[:8, :LANES]


def project_keys(blocks, key_weight):
    row_count = sum(block.shape[0] for block in blocks)
    width = key_weight.shape[1]
    return pl.pallas_call(
        functools.partial(keys_kernel, len(blocks)),
        in_specs=[WHOLE] * (len(blocks) + 1),
        out_specs=[WHOLE] * 2,
        out_shape=[
            jax.ShapeDtypeStruct((row_count, width), jnp.bfloat16),
            jax.ShapeDtypeStruct((8, LANES), jnp.float32),
        ],
        compiler_params=pltpu.CompilerParams(vmem_limit_bytes=12 * MIB),
        name="project_keys",
    )(*blocks, key_weight)


def values_kernel(offsets, count, experts, mark_ref, keys_ref, *refs):
    blocks = refs[:count]
    value_ref, panel_ref, picked_ref, pos_ref = refs[count:]
    width = value_ref.shape[0]
    rows = jnp.concatenate([block[:, :width] for block in blocks], axis=0)
    tok_count = rows.shape[0] // len(offsets)

    slots = jnp.concatenate([block[:, width:] for block in blocks], axis=0)
    slots = slots.astype(jnp.float32)
    expert = lax.axis_index("ctx") // (lax.axis_size("ctx") // experts)
    lane = lax.broadcasted_iota(jnp.int32, slots.shape, 1)
    slot = jnp.sum(jnp.where(lane == expert, slots, 0.0), axis=1, keepdims=True)
    select = (slot == lane.astype(jnp.float32)).astype(jnp.float32)
    number = lax.broadcasted_iota(jnp.int32, (tok_count, LANES), 0).astype(jnp.bfloat16)
    for g, offset in enumerate(offsets):
        part = slice(g * tok_count, (g + 1) * tok_count)
        chosen = select[part].T[:SLOTS].astype(jnp.bfloat16)
        picked_ref[g] = jnp.dot(
            chosen, rows[part], preferred_element_type=jnp.float32
        ).astype(jnp.bfloat16)
        start = (ring_owner(offset) * lax.axis_size("exp") + lax.axis_index("exp")) * tok_count
        pos_ref[g] = jnp.dot(
            chosen, number, preferred_element_type=jnp.float32
        ) + start.astype(jnp.float32)
    panel_ref[0] = keys_ref[...]
    for cols in column_parts(value_ref):
        panel_ref[1, :, cols] = jnp.dot(
            rows, value_ref[:, cols], preferred_element_type=jnp.float32
        ).astype(jnp.bfloat16)


def project_values(blocks, offsets, mark, keys, value_weight):
    row_count = sum(block.shape[0] for block in blocks)
    model_width, width = value_weight.shape
    owners = len(offsets)
    return pl.pallas_call(
        functools.partial(values_kernel, offsets, len(blocks), EXPERTS),
        in_specs=[WHOLE] * (len(blocks) + 3),
        out_specs=[WHOLE] * 3,
        out_shape=[
            jax.ShapeDtypeStruct((2, row_count, width), jnp.bfloat16),
            jax.ShapeDtypeStruct((owners, SLOTS, model_width), jnp.bfloat16),
            jax.ShapeDtypeStruct((owners, SLOTS, LANES), jnp.float32),
        ],
        compiler_params=pltpu.CompilerParams(vmem_limit_bytes=12 * MIB),
        name="project_values",
    )(mark, keys, *blocks, value_weight)


def queries_kernel(*refs):
    *picked, weight_ref, out_ref = refs
    rows = [ref[g] for ref in picked for g in range(ref.shape[0])]
    count = len(rows)
    rows = jnp.concatenate(rows, axis=0)
    for cols in column_parts(weight_ref):
        product = jnp.dot(rows, weight_ref[:, cols], preferred_element_type=jnp.float32)
        for g in range(count):
            out_ref[g, :, cols] = product[g * SLOTS : (g + 1) * SLOTS].astype(jnp.bfloat16)


def project_queries(picked, query_slab):
    model_width, width = query_slab.shape
    owners = sum(rows.shape[0] for rows in picked)
    held = 2 * model_width * width + owners * SLOTS * (4 * model_width + 4 * width)
    return pl.pallas_call(
        queries_kernel,
        in_specs=[WHOLE] * (len(picked) + 1),
        out_specs=WHOLE,
        out_shape=jax.ShapeDtypeStruct((owners, SLOTS, width), jnp.bfloat16),
        compiler_params=pltpu.CompilerParams(vmem_limit_bytes=held + 6 * MIB),
        name="project_queries",
    )(*picked, query_slab)


def attend_kernel(plan, tok_count, heads, flip, query_count, *refs):
    count = len(plan)
    query_refs, refs = refs[:query_count], refs[query_count:]
    pos_refs, own_refs, other_refs = (refs[k * count : (k + 1) * count] for k in range(3))
    out_ref, places, queries, panel, scores, weights, arrivals = refs[3 * count :]
    query_parts = [(ref, g) for ref in query_refs for g in range(ref.shape[0])]
    side = lax.axis_index("exp")
    exp_count = 2
    rate = math.log2(math.e) / math.sqrt(HS)
    tile = 2 * MOST
    per_span = 2 * exp_count
    span = per_span * tok_count
    owners = queries.shape[1]
    half_tiles = owners // 4
    group = min(half_tiles, 4)

    step = heads * HS
    steps = panel.shape[-1] // step
    now = pl.program_id(0)

    @pl.when(now == 0)
    def _():
        for s in range(steps):
            lanes = pl.ds(s * step, step)
            for offsets, own_ref, other_ref in zip(plan, own_refs, other_refs):
                for g, offset in enumerate(offsets):
                    block = ring_owner(offset) * exp_count
                    part = pl.ds(g * tok_count, tok_count)
                    for ref, place in ((own_ref, block + side), (other_ref, block + 1 - side)):
                        pltpu.make_async_copy(
                            ref.at[:, part, lanes], panel.at[:, place, :, lanes], arrivals.at[s]
                        ).start()
        for offsets, pos_ref in zip(plan, pos_refs):
            for g, offset in enumerate(offsets):
                places[ring_owner(offset)] = pos_ref[g, :MOST]

    for offsets in plan:
        for offset in offsets:
            query_ref, place = query_parts.pop(0)
            for h in range(heads):
                queries[h, ring_owner(offset)] = query_ref[
                    place, :, pl.ds(h * HS, HS)
                ].astype(jnp.float32)[:MOST]

    first_lane = pl.multiple_of(now * step, step)
    lanes_now = pl.ds(first_lane, step)
    held_now = panel.at[:, :, :, lanes_now]
    pltpu.make_async_copy(held_now, held_now, arrivals.at[now]).wait()

    def panel_part(which, h, j):
        lanes = pl.ds(pl.multiple_of(now * step + h * HS, HS), HS)
        return panel[which, per_span * j : per_span * (j + 1), :, lanes].reshape(span, HS)

    def serve(lead, first):
        top = lead + group
        for h in range(heads):
            held = queries[h, 2 * lead : 2 * top].reshape(group * tile, HS).astype(jnp.bfloat16)
            for j in range(top):
                skip = max(0, j - lead) * tile
                key_part = panel_part(0, h, j)
                scores[h, pl.ds(skip, group * tile - skip), pl.ds(j * span, span)] = (
                    lax.dot_general(
                        held[skip:],
                        key_part,
                        (((1,), (1,)), ((), ())),
                        preferred_element_type=jnp.float32,
                    )
                )
        for h in range(heads):
            for i in range(lead, top):
                reach = (i + 1) * span
                spots = places[2 * i : 2 * i + 2].reshape(tile, LANES)
                for sub in range(0, tile, 16):
                    rows = pl.ds((i - lead) * tile + sub, 16)
                    part = scores[h, rows, pl.ds(0, reach)]
                    last = part[:, reach - span :]
                    key_index = lax.broadcasted_iota(jnp.int32, last.shape, 1) + (reach - span)
                    spot = spots[sub : sub + 16, 0:1]
                    last = jnp.where(key_index.astype(jnp.float32) <= spot, last, MASKED)
                    if i > 0:
                        part = jnp.concatenate([part[:, : reach - span], last], axis=1)
                    else:
                        part = last
                    peak = jnp.max(part, axis=1, keepdims=True)
                    raised = jnp.exp2((part - peak) * rate)
                    total = jnp.sum(raised, axis=1, keepdims=True)
                    weights[h, rows, pl.ds(0, reach)] = (raised * (1.0 / total)).astype(
                        jnp.bfloat16
                    )
        for h in range(heads):
            sums = [None] * group
            for j in range(top):
                skip = max(0, j - lead)
                value_part = panel_part(1, h, j)
                product = jnp.dot(
                    weights[h, pl.ds(skip * tile, (group - skip) * tile), pl.ds(j * span, span)],
                    value_part,
                    preferred_element_type=jnp.float32,
                )
                for i in range(skip, group):
                    piece = product[(i - skip) * tile : (i - skip + 1) * tile]
                    sums[i] = piece if sums[i] is None else sums[i] + piece
            spare = jnp.zeros((SLOTS - MOST, HS), jnp.float32)
            for i in range(group):
                for part in range(2):
                    rows = jnp.concatenate([sums[i][part * MOST : (part + 1) * MOST], spare], axis=0)
                    place = 2 * (lead - first + i) + part
                    out_ref[place, :, pl.ds(h * HS, HS)] = rows.astype(jnp.bfloat16)

    late = (lax.axis_index("ctx") >= owners // 2) != flip

    @pl.when(late)
    def _():
        for lead in range(half_tiles, 2 * half_tiles, group):
            serve(lead, half_tiles)

    @pl.when(jnp.logical_not(late))
    def _():
        for lead in range(0, half_tiles, group):
            serve(lead, 0)


def attend(flip, plan, queries, positions, own, other):
    owners = sum(len(offsets) for offsets in plan)
    row_count = owners * MOST
    width = queries[0].shape[-1]
    heads = 2 if owners <= 8 else 1
    step = heads * HS
    tok_count = own[0].shape[1] // len(plan[0])
    length = owners * 2 * tok_count
    group_rows = min(row_count // 2, 8 * MOST)
    query_specs = [pl.BlockSpec((q.shape[0], SLOTS, step), lambda h: (0, 0, h)) for q in queries]
    pos_specs = [pl.BlockSpec(p.shape, lambda h: (0, 0, 0)) for p in positions]
    panel_specs = [pl.BlockSpec(memory_space=pl.ANY)] * len(own)
    scratch = heads * (group_rows * length * 6 + row_count * HS * 4) + length * width * 4
    windows = 2 * row_count * step * 5 + 5 * row_count * LANES * 4
    return pl.pallas_call(
        functools.partial(attend_kernel, plan, tok_count, heads, flip, len(queries)),
        grid=(width // step,),
        in_specs=query_specs + pos_specs + panel_specs * 2,
        out_specs=pl.BlockSpec((owners // 2, SLOTS, step), lambda h: (0, 0, h)),
        out_shape=jax.ShapeDtypeStruct((owners // 2, SLOTS, width), jnp.bfloat16),
        scratch_shapes=[
            pltpu.VMEM((owners, MOST, LANES), jnp.float32),
            pltpu.VMEM((heads, owners, MOST, HS), jnp.float32),
            pltpu.VMEM((2, 2 * owners, tok_count, width), jnp.bfloat16),
            pltpu.VMEM((heads, group_rows, length), jnp.float32),
            pltpu.VMEM((heads, group_rows, length), jnp.bfloat16),
            pltpu.SemaphoreType.DMA((width // step,)),
        ],
        compiler_params=pltpu.CompilerParams(vmem_limit_bytes=(scratch + windows) * 5 // 4 + 3 * MIB),
        name="attend",
    )(*queries, *positions, *own, *other)


def output_kernel(attended_ref, weight_ref, *refs):
    outs, pieces = refs[:-1], refs[-1]
    count, _, width = attended_ref.shape
    rows = attended_ref[...].reshape(count * SLOTS, width)
    product = jnp.dot(rows, weight_ref[...], preferred_element_type=jnp.float32)
    for b in range(count):
        pieces[b] = product[b * SLOTS : b * SLOTS + MOST]
    own = lax.rem(lax.axis_index("ctx"), count)
    for r, out_ref in enumerate(outs):
        out_ref[...] = pieces[own ^ r].astype(jnp.bfloat16)


def project_output(attended, output_slab):
    count, _, width = attended.shape
    model_width = output_slab.shape[1]
    step = 512
    return pl.pallas_call(
        output_kernel,
        grid=(model_width // step,),
        in_specs=[
            pl.BlockSpec(attended.shape, lambda n: (0, 0, 0)),
            pl.BlockSpec((width, step), lambda n: (0, n)),
        ],
        out_specs=[pl.BlockSpec((MOST, step), lambda n: (0, n))] * count,
        out_shape=[jax.ShapeDtypeStruct((MOST, model_width), jnp.bfloat16)] * count,
        scratch_shapes=[pltpu.VMEM((count, MOST, step), jnp.float32)],
        compiler_params=pltpu.CompilerParams(vmem_limit_bytes=12 * MIB),
        name="project_output",
    )(attended, output_slab)


def mix_kernel(quarter_count, top_ref, bottom_ref, logits_ref, mix_ref):
    slots = jnp.concatenate([top_ref[...], bottom_ref[...]], axis=0).astype(jnp.float32)
    tok_count = slots.shape[0]
    logits = jnp.where(slots >= 0, logits_ref[...], -jnp.inf)
    raised = jnp.exp(logits - jnp.max(logits, axis=1, keepdims=True))
    gates = raised / jnp.sum(raised, axis=1, keepdims=True)
    lane = lax.broadcasted_iota(jnp.int32, slots.shape, 1)
    count = mix_ref.shape[1] // SLOTS
    wide = lax.broadcasted_iota(jnp.int32, (tok_count, count * SLOTS), 1).astype(jnp.float32)
    total = jnp.zeros_like(wide)
    for k in range(count):
        mine = lane == (lax.axis_index("ctx") ^ k) // quarter_count
        slot = jnp.sum(jnp.where(mine, slots, 0.0), axis=1, keepdims=True)
        gate = jnp.sum(jnp.where(mine, gates, 0.0), axis=1, keepdims=True)
        spot = jnp.where(slot >= 0, slot + float(k * SLOTS), -1.0)
        total = total + jnp.where(wide == spot, gate, 0.0)
    for part in range(3):
        term = total.astype(jnp.bfloat16)
        mix_ref[pl.ds(part * tok_count, tok_count), :] = term
        total = total - term.astype(jnp.float32)


def gate_mix(quarter_count, halves, logits, count):
    half, width = halves[0].shape
    tok_count = 2 * half
    lanes = width // LANES - 1
    return pl.pallas_call(
        functools.partial(mix_kernel, quarter_count),
        grid=(1,),
        in_specs=[pl.BlockSpec((half, LANES), lambda n: (0, lanes))] * 2
        + [pl.BlockSpec((tok_count, LANES), lambda n: (0, 0))],
        out_specs=pl.BlockSpec((3 * tok_count, count * SLOTS), lambda n: (0, 0)),
        out_shape=jax.ShapeDtypeStruct((3 * tok_count, count * SLOTS), jnp.bfloat16),
        compiler_params=pltpu.CompilerParams(vmem_limit_bytes=16 * MIB),
        name="gate_mix",
    )(*halves, logits)


def combine_kernel(mix_ref, *refs):
    pieces, out_ref = refs[:-1], refs[-1]
    tok_count = out_ref.shape[0]
    spare = jnp.zeros((SLOTS - MOST, out_ref.shape[1]), jnp.float32)
    rows = []
    for piece in pieces:
        rows += [piece[...].astype(jnp.float32), spare]
    rows = jnp.concatenate(rows, axis=0).astype(jnp.bfloat16)
    product = jnp.dot(mix_ref[...], rows, preferred_element_type=jnp.float32)
    total = product[:tok_count] + (
        product[tok_count : 2 * tok_count] + product[2 * tok_count :]
    )
    out_ref[...] = total.astype(jnp.bfloat16)


def combine(mix, pieces):
    tok_count = mix.shape[0] // 3
    model_width = pieces[0].shape[1]
    step = 1024
    return pl.pallas_call(
        combine_kernel,
        grid=(model_width // step,),
        in_specs=[pl.BlockSpec(mix.shape, lambda n: (0, 0))]
        + [pl.BlockSpec((MOST, step), lambda n: (0, n))] * len(pieces),
        out_specs=pl.BlockSpec((tok_count, step), lambda n: (0, n)),
        out_shape=jax.ShapeDtypeStruct((tok_count, model_width), jnp.bfloat16),
        compiler_params=pltpu.CompilerParams(vmem_limit_bytes=24 * MIB),
        name="combine",
    )(mix, *pieces)


def per_device(
    tokens, norm_gain, router_weight, routes, key_weight, value_weight, query_weight, output_weight
):
    tok_count, model_width = tokens.shape
    ctx_count = lax.axis_size("ctx")
    exp_count = lax.axis_size("exp")
    quarter_count = ctx_count // EXPERTS
    head_width = query_weight.shape[2]
    ranks = list(range(0, ctx_count, 2)) + list(range(1, ctx_count, 2))[::-1]
    forward = [(ranks[p], ranks[(p + 1) % ctx_count]) for p in range(ctx_count)]
    backward = [(b, a) for a, b in forward]
    sibling = [(e, 1 - e) for e in range(exp_count)]
    query_slab = query_weight[0]
    output_slab = output_weight[0]
    if quarter_count > 1:
        first = (lax.axis_index("ctx") % quarter_count) * head_width
        key_weight = lax.dynamic_slice_in_dim(key_weight, first, head_width, axis=1)
        value_weight = lax.dynamic_slice_in_dim(value_weight, first, head_width, axis=1)

    halves = norm_rows(tokens, norm_gain, routes)
    steps = ctx_count // 2
    plan = [[0]] + [[-step, step] for step in range(1, steps)] + [[steps]]
    own, other, picked, queries, positions = [], [], [], [], []

    def send(parts):
        return [lax.ppermute(parts[0], "ctx", forward), lax.ppermute(parts[1], "ctx", backward)]

    def hand_over(panel):
        return lax.ppermute(panel, "exp", sibling)

    def tie(*arrays):
        return lax.optimization_barrier(arrays)

    blocks = halves
    lead = send([halves[0], halves[1]])
    rest = send([halves[1], halves[0]])
    for step in range(steps):
        keys, mark = project_keys(blocks, key_weight)
        following = [lead[0], rest[0], rest[1], lead[1]]
        if step == steps - 2:
            queries.append(project_queries(picked, query_slab))
            picked = []
        if step < steps - 1:
            mark, *lead_next = tie(mark, *lead, *queries)
            if queries:
                queries = lead_next[-1:]
            lead = send(lead_next[:2])
        panel, rows, position = project_values(blocks, plan[step], mark, keys, value_weight)
        if step < steps - 2:
            position, *rest_next = tie(position, *rest)
            rest = send(rest_next)
        own.append(panel)
        picked.append(rows)
        positions.append(position)
        if step < steps - 1:
            other.append(hand_over(panel))
        blocks = following
    own[-1], last_one, last_two = tie(own[-1], *lead)
    other.append(hand_over(own[-1]))
    blocks = [last_one, last_two]
    keys, mark = project_keys(blocks, key_weight)
    panel, rows, position = project_values(blocks, plan[-1], mark, keys, value_weight)
    own.append(panel)
    other.append(hand_over(panel))
    positions.append(position)
    queries.append(project_queries(picked + [rows], query_slab))

    attended = attend(True, plan, queries, positions, own, other)
    far = project_output(attended, output_slab)
    positions[0], *far = tie(positions[0], *far)
    half = ctx_count // 2

    def swap(piece, k):
        return lax.ppermute(piece, "ctx", [(c, c ^ k) for c in range(ctx_count)])

    first_lot = [swap(far[r], half + r) for r in range(half // 2)]
    attended = attend(False, plan, queries, positions, own, other)
    near = project_output(attended, output_slab)
    tied = tie(*near, *first_lot, *far[half // 2 :])
    near, first_lot, second_lot = (
        tied[:half], tied[half : half + half // 2], tied[half + half // 2 :]
    )
    far = list(first_lot) + [swap(p, half + half // 2 + r) for r, p in enumerate(second_lot)]
    near = [near[0]] + [swap(near[r], r) for r in range(1, half)]

    normed = jnp.concatenate([part[:, :model_width] for part in halves], axis=0)
    logits = jnp.dot(normed.astype(jnp.float32), router_weight, precision=lax.Precision.HIGHEST)
    logits = jnp.pad(logits, ((0, 0), (0, LANES - EXPERTS)))
    mix = gate_mix(quarter_count, halves, logits, ctx_count)
    return combine(mix, near + far)


def solution(mesh):
    in_specs = (
        P(("groups", "ctx", "exp"), None),
        P(),
        P(),
        P(("groups", "ctx", "exp"), None),
        P(),
        P(),
        P("ctx", None, None),
        P("ctx", None, None),
    )
    out_specs = P(("groups", "ctx", "exp"), None)
    return jax.shard_map(
        per_device, mesh=mesh, in_specs=in_specs, out_specs=out_specs, check_vma=False
    )
```

```python
import functools
import math

import jax
import jax.numpy as jnp
from jax import lax
from jax.experimental import pallas as pl
from jax.experimental.pallas import tpu as pltpu
from jax.sharding import PartitionSpec as P

HS = 128
EXPERTS = 8
MOST = 40
SLOTS = 48
MASKED = -1e30
LANES = 128
MIB = 1 << 20
WHOLE = pl.BlockSpec(memory_space=pltpu.VMEM)


def ring_rank(place, count):
    place = lax.rem(place + 2 * count, count)
    return jnp.where(place < count // 2, 2 * place, 2 * (count - 1 - place) + 1)


def ring_place(rank, count):
    return jnp.where(rank % 2 == 0, rank // 2, count - 1 - rank // 2)


def ring_owner(offset):
    count = lax.axis_size("ctx")
    return ring_rank(ring_place(lax.axis_index("ctx"), count) + offset, count)


def norm_kernel(*refs):
    sources, top_ref, bottom_ref, *held, arrivals = refs[:3], *refs[3:]
    copies = [
        pltpu.make_async_copy(source, target, arrivals.at[i])
        for i, (source, target) in enumerate(zip(sources, held))
    ]
    for copy in copies:
        copy.start()
    for copy in copies:
        copy.wait()
    tokens_ref, gain_ref, routes_ref = held
    floats = tokens_ref[...].astype(jnp.float32)
    count, width = floats.shape
    factor = lax.rsqrt(jnp.mean(floats * floats, axis=1, keepdims=True) + 1e-06)
    normed = (floats * factor * gain_ref[...]).astype(jnp.bfloat16)
    expert = lax.broadcasted_iota(jnp.int32, (LANES, count), 0)
    named = (expert == routes_ref[0:1, :]) | (expert == routes_ref[1:2, :])
    before = lax.broadcasted_iota(jnp.int32, (count, count), 0) < lax.broadcasted_iota(
        jnp.int32, (count, count), 1
    )
    rank = jnp.dot(
        named.astype(jnp.bfloat16),
        before.astype(jnp.bfloat16),
        preferred_element_type=jnp.float32,
    )
    slots = jnp.where(named, rank, -1.0).T.astype(jnp.bfloat16)
    half = count // 2
    for ref, part in ((top_ref, slice(0, half)), (bottom_ref, slice(half, count))):
        ref[:, :width] = normed[part]
        ref[:, width:] = slots[part]


def norm_rows(tokens, norm_gain, routes):
    count, width = tokens.shape
    half = jax.ShapeDtypeStruct((count // 2, width + LANES), jnp.bfloat16)
    operands = (tokens, norm_gain.reshape(1, -1), routes.T)
    return pl.pallas_call(
        norm_kernel,
        in_specs=[pl.BlockSpec(memory_space=pl.ANY)] * 3,
        out_specs=[WHOLE] * 2,
        out_shape=[half, half],
        scratch_shapes=[pltpu.VMEM(x.shape, x.dtype) for x in operands]
        + [pltpu.SemaphoreType.DMA((3,))],
        compiler_params=pltpu.CompilerParams(vmem_limit_bytes=8 * MIB),
        name="norm_rows",
    )(*operands)


def column_parts(ref):
    step = min(ref.shape[1], 256)
    return [pl.ds(start, step) for start in range(0, ref.shape[1], step)]


def keys_kernel(count, *refs):
    blocks = refs[:count]
    weight_ref, panel_ref, mark_ref = refs[count:]
    rows = jnp.concatenate([block[:, : weight_ref.shape[0]] for block in blocks], axis=0)
    for cols in column_parts(weight_ref):
        product = jnp.dot(rows, weight_ref[:, cols], preferred_element_type=jnp.float32)
        panel_ref[:, cols] = product.astype(jnp.bfloat16)
    mark_ref[...] = product[:8, :LANES]


def project_keys(blocks, key_weight):
    row_count = sum(block.shape[0] for block in blocks)
    width = key_weight.shape[1]
    return pl.pallas_call(
        functools.partial(keys_kernel, len(blocks)),
        in_specs=[WHOLE] * (len(blocks) + 1),
        out_specs=[WHOLE] * 2,
        out_shape=[
            jax.ShapeDtypeStruct((row_count, width), jnp.bfloat16),
            jax.ShapeDtypeStruct((8, LANES), jnp.float32),
        ],
        compiler_params=pltpu.CompilerParams(vmem_limit_bytes=12 * MIB),
        name="project_keys",
    )(*blocks, key_weight)


def values_kernel(offsets, count, experts, mark_ref, keys_ref, *refs):
    blocks = refs[:count]
    value_ref, panel_ref, picked_ref, pos_ref = refs[count:]
    width = value_ref.shape[0]
    rows = jnp.concatenate([block[:, :width] for block in blocks], axis=0)
    tok_count = rows.shape[0] // len(offsets)

    slots = jnp.concatenate([block[:, width:] for block in blocks], axis=0)
    slots = slots.astype(jnp.float32)
    expert = lax.axis_index("ctx") // (lax.axis_size("ctx") // experts)
    lane = lax.broadcasted_iota(jnp.int32, slots.shape, 1)
    slot = jnp.sum(jnp.where(lane == expert, slots, 0.0), axis=1, keepdims=True)
    select = (slot == lane.astype(jnp.float32)).astype(jnp.float32)
    number = lax.broadcasted_iota(jnp.int32, (tok_count, LANES), 0).astype(jnp.bfloat16)
    for g, offset in enumerate(offsets):
        part = slice(g * tok_count, (g + 1) * tok_count)
        chosen = select[part].T[:SLOTS].astype(jnp.bfloat16)
        picked_ref[g] = jnp.dot(
            chosen, rows[part], preferred_element_type=jnp.float32
        ).astype(jnp.bfloat16)
        start = (ring_owner(offset) * lax.axis_size("exp") + lax.axis_index("exp")) * tok_count
        pos_ref[g] = jnp.dot(
            chosen, number, preferred_element_type=jnp.float32
        ) + start.astype(jnp.float32)
    panel_ref[0] = keys_ref[...]
    for cols in column_parts(value_ref):
        panel_ref[1, :, cols] = jnp.dot(
            rows, value_ref[:, cols], preferred_element_type=jnp.float32
        ).astype(jnp.bfloat16)


def project_values(blocks, offsets, mark, keys, value_weight):
    row_count = sum(block.shape[0] for block in blocks)
    model_width, width = value_weight.shape
    owners = len(offsets)
    return pl.pallas_call(
        functools.partial(values_kernel, offsets, len(blocks), EXPERTS),
        in_specs=[WHOLE] * (len(blocks) + 3),
        out_specs=[WHOLE] * 3,
        out_shape=[
            jax.ShapeDtypeStruct((2, row_count, width), jnp.bfloat16),
            jax.ShapeDtypeStruct((owners, SLOTS, model_width), jnp.bfloat16),
            jax.ShapeDtypeStruct((owners, SLOTS, LANES), jnp.float32),
        ],
        compiler_params=pltpu.CompilerParams(vmem_limit_bytes=12 * MIB),
        name="project_values",
    )(mark, keys, *blocks, value_weight)


def queries_kernel(*refs):
    count = len(refs) // 2
    picked, weight_ref, outs = refs[:count], refs[count], refs[count + 1 :]
    rows = jnp.concatenate([ref[g] for ref in picked for g in range(ref.shape[0])], axis=0)
    places = [(ref, g) for ref in outs for g in range(ref.shape[0])]
    for cols in column_parts(weight_ref):
        product = jnp.dot(rows, weight_ref[:, cols], preferred_element_type=jnp.float32)
        for i, (ref, g) in enumerate(places):
            ref[g, :, cols] = product[i * SLOTS : (i + 1) * SLOTS].astype(jnp.bfloat16)


def project_queries(picked, query_slab):
    model_width, width = query_slab.shape
    owners = sum(rows.shape[0] for rows in picked)
    held = 2 * model_width * width + owners * SLOTS * (4 * model_width + 4 * width)
    return pl.pallas_call(
        queries_kernel,
        in_specs=[WHOLE] * (len(picked) + 1),
        out_specs=[WHOLE] * len(picked),
        out_shape=[
            jax.ShapeDtypeStruct((rows.shape[0], SLOTS, width), jnp.bfloat16) for rows in picked
        ],
        compiler_params=pltpu.CompilerParams(vmem_limit_bytes=held + 6 * MIB),
        name="project_queries",
    )(*picked, query_slab)


def arrange_kernel(plan, *refs):
    count = len(plan)
    own_refs, other_refs, query_refs, pos_refs = (refs[k * count : (k + 1) * count] for k in range(4))
    panel_ref, queries_ref, places_ref = refs[4 * count :]
    exp_count = 2
    side = lax.axis_index("exp")
    tok_count = panel_ref.shape[2]
    for offsets, own_ref, other_ref, query_ref, pos_ref in zip(
        plan, own_refs, other_refs, query_refs, pos_refs
    ):
        for g, offset in enumerate(offsets):
            owner = ring_owner(offset)
            part = pl.ds(g * tok_count, tok_count)
            for which in range(2):
                panel_ref[which, owner * exp_count + side] = own_ref[which, part]
                panel_ref[which, owner * exp_count + 1 - side] = other_ref[which, part]
            queries_ref[owner] = query_ref[g]
            places_ref[owner] = pos_ref[g]


def arrange(owners, plan, own, other, queries, positions):
    width = own[0].shape[2]
    tok_count = own[0].shape[1] // len(plan[0])
    shapes = [
        jax.ShapeDtypeStruct((2, 2 * owners, tok_count, width), jnp.bfloat16),
        jax.ShapeDtypeStruct((owners, SLOTS, width), jnp.bfloat16),
        jax.ShapeDtypeStruct((owners, SLOTS, LANES), jnp.float32),
    ]
    operands = (*own, *other, *queries, *positions)
    return pl.pallas_call(
        functools.partial(arrange_kernel, plan),
        in_specs=[WHOLE] * len(operands),
        out_specs=[WHOLE] * 3,
        out_shape=shapes,
        compiler_params=pltpu.CompilerParams(
            vmem_limit_bytes=owners * tok_count * width * 24 + 4 * MIB
        ),
        name="arrange",
    )(*operands)


def attend_kernel(lots, heads, panel_ref, queries_ref, places_ref, weight_ref, *refs):
    outs, (attended, scores, weights) = refs[:-3], refs[-3:]
    first, count = lots
    blocks, tok_count, width = panel_ref.shape[1:]
    rate = math.log2(math.e) / math.sqrt(HS)
    rank = lax.axis_index("ctx")
    tiles = blocks // 4
    tile = 2 * SLOTS
    parts = 4
    span = blocks * tok_count // parts
    per_span = blocks // parts
    passes = width // (heads * HS)

    def serve(part_id, number, lot, lanes):
        reach = (part_id + 1) * span
        pair = pl.ds(2 * number, 2)
        spots = places_ref[pair].reshape(tile, LANES)
        for h in range(heads):
            held = queries_ref[pair, :, lanes[h]].reshape(tile, HS)
            for j in range(part_id + 1):
                key_part = panel_ref[0, per_span * j : per_span * (j + 1), :, lanes[h]]
                scores[h, :, pl.ds(j * span, span)] = lax.dot_general(
                    held,
                    key_part.reshape(span, HS),
                    (((1,), (1,)), ((), ())),
                    preferred_element_type=jnp.float32,
                )
        for h in range(heads):
            for sub in range(0, tile, 16):
                rows = pl.ds(sub, 16)
                part = scores[h, rows, pl.ds(0, reach)]
                last = part[:, reach - span :]
                key_index = lax.broadcasted_iota(jnp.int32, last.shape, 1) + (reach - span)
                spot = spots[sub : sub + 16, 0:1]
                last = jnp.where(key_index.astype(jnp.float32) <= spot, last, MASKED)
                if part_id > 0:
                    part = jnp.concatenate([part[:, : reach - span], last], axis=1)
                else:
                    part = last
                peak = jnp.max(part, axis=1, keepdims=True)
                raised = jnp.exp2((part - peak) * rate)
                total = jnp.sum(raised, axis=1, keepdims=True)
                weights[h, rows, pl.ds(0, reach)] = (raised * (1.0 / total)).astype(jnp.bfloat16)
        for h in range(heads):
            total = None
            for j in range(part_id + 1):
                value_part = panel_ref[1, per_span * j : per_span * (j + 1), :, lanes[h]]
                product = jnp.dot(
                    weights[h, :, pl.ds(j * span, span)],
                    value_part.reshape(span, HS),
                    preferred_element_type=jnp.float32,
                )
                total = product if total is None else total + product
            total = total.astype(jnp.bfloat16)
            for side in range(2):
                attended[2 * lot + (side ^ (rank % 2)), :, lanes[h]] = total[
                    side * SLOTS : (side + 1) * SLOTS
                ]

    def one(at, carry):
        lot, now = at // passes, at % passes
        number = (rank // 2) ^ (first + lot)
        lanes = [pl.ds(pl.multiple_of((now * heads + h) * HS, HS), HS) for h in range(heads)]
        for part_id in range(parts):
            pl.when(number // (tiles // parts) == part_id)(
                functools.partial(serve, part_id, number, lot, lanes)
            )
        return carry

    lax.fori_loop(0, count * passes, one, 0)
    rows = attended[...].reshape(2 * count * SLOTS, width)
    for cols in column_parts(weight_ref):
        product = jnp.dot(rows, weight_ref[:, cols], preferred_element_type=jnp.float32)
        for k, out_ref in enumerate(outs):
            out_ref[:, cols] = product[k * SLOTS : k * SLOTS + MOST].astype(jnp.bfloat16)


def attend(lots, panel, queries, places, output_slab):
    first, count = lots
    _, blocks, tok_count, width = panel.shape
    length = blocks * tok_count
    heads = min(4, width // HS) if blocks <= 16 else 1
    model_width = output_slab.shape[1]
    held = heads * 2 * SLOTS * length * 6 + 2 * length * width * 2 + width * model_width * 2
    held += 2 * count * SLOTS * (model_width * 8 + width * 2)
    return pl.pallas_call(
        functools.partial(attend_kernel, lots, heads),
        in_specs=[WHOLE] * 4,
        out_specs=[WHOLE] * (2 * count),
        out_shape=[jax.ShapeDtypeStruct((MOST, model_width), jnp.bfloat16)] * (2 * count),
        scratch_shapes=[
            pltpu.VMEM((2 * count, SLOTS, width), jnp.bfloat16),
            pltpu.VMEM((heads, 2 * SLOTS, length), jnp.float32),
            pltpu.VMEM((heads, 2 * SLOTS, length), jnp.bfloat16),
        ],
        compiler_params=pltpu.CompilerParams(vmem_limit_bytes=held * 9 // 8 + 4 * MIB),
        cost_estimate=pl.CostEstimate(
            flops=count * 2 * SLOTS * width * (4 * length + 2 * model_width),
            bytes_accessed=4 * length * width,
            transcendentals=count * 2 * SLOTS * length * width // HS,
        ),
        name="attend",
    )(panel, queries, places, output_slab)


def mix_kernel(quarter_count, top_ref, bottom_ref, logits_ref, mix_ref):
    slots = jnp.concatenate([top_ref[...], bottom_ref[...]], axis=0).astype(jnp.float32)
    tok_count = slots.shape[0]
    logits = jnp.where(slots >= 0, logits_ref[...], -jnp.inf)
    raised = jnp.exp(logits - jnp.max(logits, axis=1, keepdims=True))
    gates = raised / jnp.sum(raised, axis=1, keepdims=True)
    lane = lax.broadcasted_iota(jnp.int32, slots.shape, 1)
    count = mix_ref.shape[1] // SLOTS
    wide = lax.broadcasted_iota(jnp.int32, (tok_count, count * SLOTS), 1).astype(jnp.float32)
    total = jnp.zeros_like(wide)
    for k in range(count):
        mine = lane == (lax.axis_index("ctx") ^ k) // quarter_count
        slot = jnp.sum(jnp.where(mine, slots, 0.0), axis=1, keepdims=True)
        gate = jnp.sum(jnp.where(mine, gates, 0.0), axis=1, keepdims=True)
        spot = jnp.where(slot >= 0, slot + float(k * SLOTS), -1.0)
        total = total + jnp.where(wide == spot, gate, 0.0)
    for part in range(3):
        term = total.astype(jnp.bfloat16)
        mix_ref[pl.ds(part * tok_count, tok_count), :] = term
        total = total - term.astype(jnp.float32)


def gate_mix(quarter_count, halves, logits, count):
    half, width = halves[0].shape
    tok_count = 2 * half
    lanes = width // LANES - 1
    return pl.pallas_call(
        functools.partial(mix_kernel, quarter_count),
        grid=(1,),
        in_specs=[pl.BlockSpec((half, LANES), lambda n: (0, lanes))] * 2
        + [pl.BlockSpec((tok_count, LANES), lambda n: (0, 0))],
        out_specs=pl.BlockSpec((3 * tok_count, count * SLOTS), lambda n: (0, 0)),
        out_shape=jax.ShapeDtypeStruct((3 * tok_count, count * SLOTS), jnp.bfloat16),
        compiler_params=pltpu.CompilerParams(vmem_limit_bytes=16 * MIB),
        name="gate_mix",
    )(*halves, logits)


def combine_kernel(mix_ref, *refs):
    pieces, out_ref = refs[:-1], refs[-1]
    tok_count, model_width = out_ref.shape
    step = min(model_width, 512)
    spare = jnp.zeros((SLOTS - MOST, step), jnp.float32)
    for start in range(0, model_width, step):
        cols = pl.ds(start, step)
        rows = []
        for piece in pieces:
            rows += [piece[:, cols].astype(jnp.float32), spare]
        rows = jnp.concatenate(rows, axis=0).astype(jnp.bfloat16)
        product = jnp.dot(mix_ref[...], rows, preferred_element_type=jnp.float32)
        total = product[:tok_count] + (
            product[tok_count : 2 * tok_count] + product[2 * tok_count :]
        )
        out_ref[:, cols] = total.astype(jnp.bfloat16)


def combine(mix, pieces):
    tok_count = mix.shape[0] // 3
    model_width = pieces[0].shape[1]
    return pl.pallas_call(
        combine_kernel,
        in_specs=[WHOLE] * (1 + len(pieces)),
        out_specs=WHOLE,
        out_shape=jax.ShapeDtypeStruct((tok_count, model_width), jnp.bfloat16),
        compiler_params=pltpu.CompilerParams(vmem_limit_bytes=24 * MIB),
        name="combine",
    )(mix, *pieces)


def per_device(
    tokens, norm_gain, router_weight, routes, key_weight, value_weight, query_weight, output_weight
):
    tok_count, model_width = tokens.shape
    ctx_count = lax.axis_size("ctx")
    exp_count = lax.axis_size("exp")
    quarter_count = ctx_count // EXPERTS
    head_width = query_weight.shape[2]
    ranks = list(range(0, ctx_count, 2)) + list(range(1, ctx_count, 2))[::-1]
    forward = [(ranks[p], ranks[(p + 1) % ctx_count]) for p in range(ctx_count)]
    backward = [(b, a) for a, b in forward]
    sibling = [(e, 1 - e) for e in range(exp_count)]
    query_slab = query_weight[0]
    output_slab = output_weight[0]
    if quarter_count > 1:
        first = (lax.axis_index("ctx") % quarter_count) * head_width
        key_weight = lax.dynamic_slice_in_dim(key_weight, first, head_width, axis=1)
        value_weight = lax.dynamic_slice_in_dim(value_weight, first, head_width, axis=1)

    halves = norm_rows(tokens, norm_gain, routes)
    steps = ctx_count // 2
    plan = [[0]] + [[-step, step] for step in range(1, steps)] + [[steps]]
    own, other, picked, queries, positions = [], [], [], [], []

    def send(parts):
        return [lax.ppermute(parts[0], "ctx", forward), lax.ppermute(parts[1], "ctx", backward)]

    def hand_over(panel):
        return lax.ppermute(panel, "exp", sibling)

    def tie(*arrays):
        return lax.optimization_barrier(arrays)

    blocks = halves
    lead = send([halves[0], halves[1]])
    rest = send([halves[1], halves[0]])
    for step in range(steps):
        keys, mark = project_keys(blocks, key_weight)
        following = [lead[0], rest[0], rest[1], lead[1]]
        if step == steps - 2:
            queries = project_queries(picked, query_slab)
            picked = []
        if step < steps - 1:
            mark, *lead_next = tie(mark, *lead, *queries)
            queries = lead_next[2:]
            lead = send(lead_next[:2])
        panel, rows, position = project_values(blocks, plan[step], mark, keys, value_weight)
        if step < steps - 2:
            position, *rest_next = tie(position, *rest)
            rest = send(rest_next)
        own.append(panel)
        picked.append(rows)
        positions.append(position)
        if step < steps - 1:
            other.append(hand_over(panel))
        blocks = following
    own[-1], *blocks = tie(own[-1], *lead)
    other.append(hand_over(own[-1]))
    keys, mark = project_keys(blocks, key_weight)
    panel, rows, position = project_values(blocks, plan[-1], mark, keys, value_weight)
    own.append(panel)
    other.append(hand_over(panel))
    positions.append(position)
    queries = [*queries, *project_queries(picked + [rows], query_slab)]
    held = arrange(ctx_count, plan, own, other, queries, positions)

    def swap(piece, k):
        return lax.ppermute(piece, "ctx", [(c, c ^ k) for c in range(ctx_count)])

    half, quarter = ctx_count // 2, ctx_count // 4
    far, mine = [], []
    for start, count in ((half, quarter), (half + quarter, quarter), (0, half)):
        pieces = attend((start // 2, count // 2), *held, output_slab)
        if start > 0:
            places, *pieces = tie(held[2], *pieces)
            held = [*held[:2], places]
            far.append([swap(piece, start + r) for r, piece in enumerate(pieces)])
        else:
            near = pieces
    tied = tie(*near, *far[0])
    near, far[0] = tied[:half], tied[half:]
    near = [near[0]] + [swap(near[r], r) for r in range(1, half)]

    normed = jnp.concatenate([part[:, :model_width] for part in halves], axis=0)
    logits = jnp.dot(normed.astype(jnp.float32), router_weight, precision=lax.Precision.HIGHEST)
    logits = jnp.pad(logits, ((0, 0), (0, LANES - EXPERTS)))
    mix = gate_mix(quarter_count, halves, logits, ctx_count)
    return combine(mix, [*near, *far[0], *far[1]])


def solution(mesh):
    in_specs = (
        P(("groups", "ctx", "exp"), None),
        P(),
        P(),
        P(("groups", "ctx", "exp"), None),
        P(),
        P(),
        P("ctx", None, None),
        P("ctx", None, None),
    )
    out_specs = P(("groups", "ctx", "exp"), None)
    return jax.shard_map(
        per_device, mesh=mesh, in_specs=in_specs, out_specs=out_specs, check_vma=False
    )
```

```python
import functools
import math

import jax
import jax.numpy as jnp
from jax import lax
from jax.experimental import pallas as pl
from jax.experimental.pallas import tpu as pltpu
from jax.sharding import PartitionSpec as P

HS = 128
EXPERTS = 8
MOST = 40
SLOTS = 48
MASKED = -1e30
LANES = 128
CODES = 16
TERMS = 3
MIB = 1 << 20
WHOLE = pl.BlockSpec(memory_space=pltpu.VMEM)


def ring_rank(place, count):
    place = lax.rem(place + 2 * count, count)
    return jnp.where(place < count // 2, 2 * place, 2 * (count - 1 - place) + 1)


def ring_place(rank, count):
    return jnp.where(rank % 2 == 0, rank // 2, count - 1 - rank // 2)


def ring_owner(offset):
    count = lax.axis_size("ctx")
    return ring_rank(ring_place(lax.axis_index("ctx"), count) + offset, count)


def norm_kernel(*refs):
    sources, top_ref, bottom_ref, *held, arrivals = refs[:3], *refs[3:]
    copies = [
        pltpu.make_async_copy(source, target, arrivals.at[i])
        for i, (source, target) in enumerate(zip(sources, held))
    ]
    for copy in copies:
        copy.start()
    for copy in copies:
        copy.wait()
    tokens_ref, gain_ref, routes_ref = held
    floats = tokens_ref[...].astype(jnp.float32)
    count, width = floats.shape
    factor = lax.rsqrt(jnp.mean(floats * floats, axis=1, keepdims=True) + 1e-06)
    normed = (floats * factor * gain_ref[...]).astype(jnp.bfloat16)
    expert = lax.broadcasted_iota(jnp.int32, (CODES, count), 0)
    named = (expert == routes_ref[0:1, :]) | (expert == routes_ref[1:2, :])
    before = lax.broadcasted_iota(jnp.int32, (count, count), 0) < lax.broadcasted_iota(
        jnp.int32, (count, count), 1
    )
    rank = jnp.dot(
        named.astype(jnp.bfloat16),
        before.astype(jnp.bfloat16),
        preferred_element_type=jnp.float32,
    )
    codes = jnp.where(named, rank, -1.0).astype(jnp.bfloat16)
    half = count // 2
    for ref, first in ((top_ref, 0), (bottom_ref, half)):
        for c in range(width // LANES):
            ref[pl.ds(c * half, half), :] = normed[
                first : first + half, c * LANES : (c + 1) * LANES
            ]
        ref[pl.ds(width // LANES * half, CODES), :] = codes


def message_rows(ref, half):
    tiles = (ref.shape[0] - CODES) // half
    return jnp.concatenate([ref[pl.ds(c * half, half), :] for c in range(tiles)], axis=1)


def message_codes(ref):
    return ref[pl.ds(ref.shape[0] - CODES, CODES), :].astype(jnp.float32)


def norm_rows(tokens, norm_gain, routes):
    count, width = tokens.shape
    half = jax.ShapeDtypeStruct((width // LANES * (count // 2) + CODES, LANES), jnp.bfloat16)
    operands = (tokens, norm_gain.reshape(1, -1), routes.T)
    return pl.pallas_call(
        norm_kernel,
        in_specs=[pl.BlockSpec(memory_space=pltpu.HBM)] * 3,
        out_specs=[WHOLE] * 2,
        out_shape=[half, half],
        scratch_shapes=[pltpu.VMEM(x.shape, x.dtype) for x in operands]
        + [pltpu.SemaphoreType.DMA((3,))],
        compiler_params=pltpu.CompilerParams(vmem_limit_bytes=8 * MIB),
        name="norm_rows",
    )(*operands)


def column_parts(ref):
    step = min(ref.shape[1], 256)
    return [pl.ds(start, step) for start in range(0, ref.shape[1], step)]


def keys_kernel(half, count, *refs):
    blocks = refs[:count]
    weight_ref, panel_ref, mark_ref = refs[count:]
    rows = jnp.concatenate([message_rows(block, half) for block in blocks], axis=0)
    for cols in column_parts(weight_ref):
        product = jnp.dot(rows, weight_ref[:, cols], preferred_element_type=jnp.float32)
        panel_ref[:, cols] = product.astype(jnp.bfloat16)
    mark_ref[...] = product[:8, :LANES]


def project_keys(half, blocks, key_weight):
    row_count = half * len(blocks)
    width = key_weight.shape[1]
    return pl.pallas_call(
        functools.partial(keys_kernel, half, len(blocks)),
        in_specs=[WHOLE] * (len(blocks) + 1),
        out_specs=[WHOLE] * 2,
        out_shape=[
            jax.ShapeDtypeStruct((row_count, width), jnp.bfloat16),
            jax.ShapeDtypeStruct((8, LANES), jnp.float32),
        ],
        compiler_params=pltpu.CompilerParams(vmem_limit_bytes=12 * MIB),
        name="project_keys",
    )(*blocks, key_weight)


def values_kernel(half, offsets, count, experts, mark_ref, keys_ref, *refs):
    blocks = refs[:count]
    value_ref, panel_ref, picked_ref, pos_ref = refs[count:]
    rows = jnp.concatenate([message_rows(block, half) for block in blocks], axis=0)
    tok_count = 2 * half
    expert = lax.axis_index("ctx") // (lax.axis_size("ctx") // experts)
    number = lax.broadcasted_iota(jnp.int32, (tok_count, LANES), 0).astype(jnp.bfloat16)
    for g, offset in enumerate(offsets):
        part = slice(g * tok_count, (g + 1) * tok_count)
        codes = message_codes(blocks[2 * g])
        mine = lax.broadcasted_iota(jnp.int32, codes.shape, 0) == expert
        slot = jnp.sum(jnp.where(mine, codes, 0.0), axis=0, keepdims=True)
        order = lax.broadcasted_iota(jnp.int32, (SLOTS, tok_count), 0).astype(jnp.float32)
        chosen = (order == slot).astype(jnp.bfloat16)
        picked_ref[g] = jnp.dot(
            chosen, rows[part], preferred_element_type=jnp.float32
        ).astype(jnp.bfloat16)
        start = (ring_owner(offset) * lax.axis_size("exp") + lax.axis_index("exp")) * tok_count
        pos_ref[g] = jnp.dot(
            chosen, number, preferred_element_type=jnp.float32
        ) + start.astype(jnp.float32)
    panel_ref[0] = keys_ref[...]
    for cols in column_parts(value_ref):
        panel_ref[1, :, cols] = jnp.dot(
            rows, value_ref[:, cols], preferred_element_type=jnp.float32
        ).astype(jnp.bfloat16)


def project_values(half, blocks, offsets, mark, keys, value_weight):
    row_count = half * len(blocks)
    model_width, width = value_weight.shape
    owners = len(offsets)
    return pl.pallas_call(
        functools.partial(values_kernel, half, offsets, len(blocks), EXPERTS),
        in_specs=[WHOLE] * (len(blocks) + 3),
        out_specs=[WHOLE] * 3,
        out_shape=[
            jax.ShapeDtypeStruct((2, row_count, width), jnp.bfloat16),
            jax.ShapeDtypeStruct((owners, SLOTS, model_width), jnp.bfloat16),
            jax.ShapeDtypeStruct((owners, SLOTS, LANES), jnp.float32),
        ],
        compiler_params=pltpu.CompilerParams(vmem_limit_bytes=12 * MIB),
        name="project_values",
    )(mark, keys, *blocks, value_weight)


def queries_kernel(*refs):
    count = len(refs) // 2
    picked, weight_ref, outs = refs[:count], refs[count], refs[count + 1 :]
    rows = jnp.concatenate([ref[g] for ref in picked for g in range(ref.shape[0])], axis=0)
    places = [(ref, g) for ref in outs for g in range(ref.shape[0])]
    for cols in column_parts(weight_ref):
        product = jnp.dot(rows, weight_ref[:, cols], preferred_element_type=jnp.float32)
        for i, (ref, g) in enumerate(places):
            ref[g, :, cols] = product[i * SLOTS : (i + 1) * SLOTS].astype(jnp.bfloat16)


def project_queries(picked, query_slab):
    model_width, width = query_slab.shape
    owners = sum(rows.shape[0] for rows in picked)
    held = 2 * model_width * width + owners * SLOTS * (4 * model_width + 4 * width)
    return pl.pallas_call(
        queries_kernel,
        in_specs=[WHOLE] * (len(picked) + 1),
        out_specs=[WHOLE] * len(picked),
        out_shape=[
            jax.ShapeDtypeStruct((rows.shape[0], SLOTS, width), jnp.bfloat16) for rows in picked
        ],
        compiler_params=pltpu.CompilerParams(vmem_limit_bytes=held + 6 * MIB),
        name="project_queries",
    )(*picked, query_slab)


def arrange_kernel(plan, *refs):
    count = len(plan)
    own_refs, other_refs, query_refs, pos_refs = (refs[k * count : (k + 1) * count] for k in range(4))
    panel_ref, queries_ref, places_ref = refs[4 * count :]
    exp_count = 2
    side = lax.axis_index("exp")
    tok_count = panel_ref.shape[2]
    for offsets, own_ref, other_ref, query_ref, pos_ref in zip(
        plan, own_refs, other_refs, query_refs, pos_refs
    ):
        for g, offset in enumerate(offsets):
            owner = ring_owner(offset)
            part = pl.ds(g * tok_count, tok_count)
            for which in range(2):
                panel_ref[which, owner * exp_count + side] = own_ref[which, part]
                panel_ref[which, owner * exp_count + 1 - side] = other_ref[which, part]
            queries_ref[owner] = query_ref[g]
            places_ref[owner] = pos_ref[g]


def arrange(owners, plan, own, other, queries, positions):
    width = own[0].shape[2]
    tok_count = own[0].shape[1] // len(plan[0])
    shapes = [
        jax.ShapeDtypeStruct((2, 2 * owners, tok_count, width), jnp.bfloat16),
        jax.ShapeDtypeStruct((owners, SLOTS, width), jnp.bfloat16),
        jax.ShapeDtypeStruct((owners, SLOTS, LANES), jnp.float32),
    ]
    operands = (*own, *other, *queries, *positions)
    return pl.pallas_call(
        functools.partial(arrange_kernel, plan),
        in_specs=[WHOLE] * len(operands),
        out_specs=[WHOLE] * 3,
        out_shape=shapes,
        compiler_params=pltpu.CompilerParams(
            vmem_limit_bytes=8 * MIB
        ),
        name="arrange",
    )(*operands)


def attend_kernel(lots, heads, panel_ref, queries_ref, places_ref, weight_ref, *refs):
    outs, (attended, scores, weights) = refs[:-3], refs[-3:]
    first, count = lots
    blocks, tok_count, width = panel_ref.shape[1:]
    rate = math.log2(math.e) / math.sqrt(HS)
    rank = lax.axis_index("ctx")
    tiles = blocks // 4
    tile = 2 * SLOTS
    parts = 4
    span = blocks * tok_count // parts
    per_span = blocks // parts
    passes = width // (heads * HS)

    def serve(part_id, number, lot, lanes):
        reach = (part_id + 1) * span
        pair = pl.ds(2 * number, 2)
        spots = places_ref[pair].reshape(tile, LANES)
        for h in range(heads):
            held = queries_ref[pair, :, lanes[h]].reshape(tile, HS)
            for j in range(part_id + 1):
                key_part = panel_ref[0, per_span * j : per_span * (j + 1), :, lanes[h]]
                scores[h, :, pl.ds(j * span, span)] = lax.dot_general(
                    held,
                    key_part.reshape(span, HS),
                    (((1,), (1,)), ((), ())),
                    preferred_element_type=jnp.float32,
                )
        for h in range(heads):
            for sub in range(0, tile, 16):
                rows = pl.ds(sub, 16)
                part = scores[h, rows, pl.ds(0, reach)]
                last = part[:, reach - span :]
                key_index = lax.broadcasted_iota(jnp.int32, last.shape, 1) + (reach - span)
                spot = spots[sub : sub + 16, 0:1]
                last = jnp.where(key_index.astype(jnp.float32) <= spot, last, MASKED)
                if part_id > 0:
                    part = jnp.concatenate([part[:, : reach - span], last], axis=1)
                else:
                    part = last
                peak = jnp.max(part, axis=1, keepdims=True)
                raised = jnp.exp2((part - peak) * rate)
                total = jnp.sum(raised, axis=1, keepdims=True)
                weights[h, rows, pl.ds(0, reach)] = (raised * (1.0 / total)).astype(jnp.bfloat16)
        for h in range(heads):
            total = None
            for j in range(part_id + 1):
                value_part = panel_ref[1, per_span * j : per_span * (j + 1), :, lanes[h]]
                product = jnp.dot(
                    weights[h, :, pl.ds(j * span, span)],
                    value_part.reshape(span, HS),
                    preferred_element_type=jnp.float32,
                )
                total = product if total is None else total + product
            total = total.astype(jnp.bfloat16)
            for side in range(2):
                attended[2 * lot + (side ^ (rank % 2)), :, lanes[h]] = total[
                    side * SLOTS : (side + 1) * SLOTS
                ]

    def one(at, carry):
        lot, now = at // passes, at % passes
        number = (rank // 2) ^ (first + lot)
        lanes = [pl.ds(pl.multiple_of((now * heads + h) * HS, HS), HS) for h in range(heads)]
        for part_id in range(parts):
            pl.when(number // (tiles // parts) == part_id)(
                functools.partial(serve, part_id, number, lot, lanes)
            )
        return carry

    lax.fori_loop(0, count * passes, one, 0)
    rows = attended[...].reshape(2 * count * SLOTS, width)
    for cols in column_parts(weight_ref):
        product = jnp.dot(rows, weight_ref[:, cols], preferred_element_type=jnp.float32)
        for k, out_ref in enumerate(outs):
            out_ref[:, cols] = product[k * SLOTS : k * SLOTS + MOST].astype(jnp.bfloat16)


def attend(lots, panel, queries, places, output_slab):
    first, count = lots
    _, blocks, tok_count, width = panel.shape
    length = blocks * tok_count
    heads = min(4, width // HS) if blocks <= 16 else 1
    model_width = output_slab.shape[1]
    held = heads * 2 * SLOTS * length * 6 + 2 * length * width * 2 + width * model_width * 2
    held += 2 * count * SLOTS * (model_width * 8 + width * 2)
    return pl.pallas_call(
        functools.partial(attend_kernel, lots, heads),
        in_specs=[WHOLE] * 4,
        out_specs=[WHOLE] * (2 * count),
        out_shape=[jax.ShapeDtypeStruct((MOST, model_width), jnp.bfloat16)] * (2 * count),
        scratch_shapes=[
            pltpu.VMEM((2 * count, SLOTS, width), jnp.bfloat16),
            pltpu.VMEM((heads, 2 * SLOTS, length), jnp.float32),
            pltpu.VMEM((heads, 2 * SLOTS, length), jnp.bfloat16),
        ],
        compiler_params=pltpu.CompilerParams(vmem_limit_bytes=held * 9 // 8 + 4 * MIB),
        cost_estimate=pl.CostEstimate(
            flops=count * 2 * SLOTS * width * (4 * length + 2 * model_width),
            bytes_accessed=4 * length * width,
            transcendentals=count * 2 * SLOTS * length * width // HS,
        ),
        name="attend",
    )(panel, queries, places, output_slab)


def mix_kernel(quarter_count, top_ref, bottom_ref, router_ref, mix_ref, slots_ref, gates_ref):
    half = LANES // 2
    rows = jnp.concatenate([message_rows(ref, half) for ref in (top_ref, bottom_ref)], axis=0)
    rest, terms = router_ref[...], []
    for _ in range(3):
        terms.append(rest.astype(jnp.bfloat16).astype(jnp.float32))
        rest = rest - terms[-1]
    experts = rest.shape[0]
    router = jnp.concatenate([*terms, jnp.zeros_like(rest)], axis=0).astype(jnp.bfloat16)
    products = lax.dot_general(
        router, rows, (((1,), (1,)), ((), ())), preferred_element_type=jnp.float32
    )
    logits = products[:experts] + (
        products[experts : 2 * experts] + products[2 * experts : 3 * experts]
    )
    slots = message_codes(top_ref)[:experts]
    logits = jnp.where(slots >= 0, logits, -jnp.inf)
    raised = jnp.exp(logits - jnp.max(logits, axis=0, keepdims=True))
    slots_ref[...] = slots
    gates_ref[...] = raised / jnp.sum(raised, axis=0, keepdims=True)
    tok_count = slots.shape[1]
    order = lax.broadcasted_iota(jnp.int32, (SLOTS, tok_count), 0).astype(jnp.float32)
    parts = []
    for k in range(mix_ref.shape[1] // SLOTS):
        expert = pl.ds((lax.axis_index("ctx") ^ k) // quarter_count, 1)
        parts.append(jnp.where(order == slots_ref[expert, :], gates_ref[expert, :], 0.0))
    total = jnp.concatenate(parts, axis=0).T
    for part in range(TERMS):
        term = total.astype(jnp.bfloat16)
        mix_ref[pl.ds(part * tok_count, tok_count), :] = term
        total = total - term.astype(jnp.float32)


def gate_mix(quarter_count, halves, router, count):
    tok_count = LANES
    held = pltpu.VMEM((router.shape[0], tok_count), jnp.float32)
    return pl.pallas_call(
        functools.partial(mix_kernel, quarter_count),
        in_specs=[WHOLE] * 3,
        out_specs=WHOLE,
        out_shape=jax.ShapeDtypeStruct((TERMS * tok_count, count * SLOTS), jnp.bfloat16),
        scratch_shapes=[held, held],
        compiler_params=pltpu.CompilerParams(vmem_limit_bytes=16 * MIB),
        name="gate_mix",
    )(*halves, router)


def combine_kernel(mix_ref, *refs):
    pieces, out_ref = refs[:-1], refs[-1]
    tok_count, model_width = out_ref.shape
    step = min(model_width, 512)
    spare = jnp.zeros((SLOTS - MOST, step), jnp.float32)
    for start in range(0, model_width, step):
        cols = pl.ds(start, step)
        rows = []
        for piece in pieces:
            rows += [piece[:, cols].astype(jnp.float32), spare]
        rows = jnp.concatenate(rows, axis=0).astype(jnp.bfloat16)
        product = jnp.dot(mix_ref[...], rows, preferred_element_type=jnp.float32)
        total = product[-tok_count:]
        for part in range(TERMS - 2, -1, -1):
            total = product[part * tok_count : (part + 1) * tok_count] + total
        out_ref[:, cols] = total.astype(jnp.bfloat16)


def combine(mix, pieces):
    tok_count = mix.shape[0] // TERMS
    model_width = pieces[0].shape[1]
    return pl.pallas_call(
        combine_kernel,
        in_specs=[WHOLE] * (1 + len(pieces)),
        out_specs=WHOLE,
        out_shape=jax.ShapeDtypeStruct((tok_count, model_width), jnp.bfloat16),
        compiler_params=pltpu.CompilerParams(vmem_limit_bytes=24 * MIB),
        name="combine",
    )(mix, *pieces)


def per_device(
    tokens, norm_gain, router_weight, routes, key_weight, value_weight, query_weight, output_weight
):
    tok_count, model_width = tokens.shape
    ctx_count = lax.axis_size("ctx")
    exp_count = lax.axis_size("exp")
    quarter_count = ctx_count // EXPERTS
    head_width = query_weight.shape[2]
    ranks = list(range(0, ctx_count, 2)) + list(range(1, ctx_count, 2))[::-1]
    forward = [(ranks[p], ranks[(p + 1) % ctx_count]) for p in range(ctx_count)]
    backward = [(b, a) for a, b in forward]
    sibling = [(e, 1 - e) for e in range(exp_count)]
    query_slab = query_weight[0]
    output_slab = output_weight[0]
    if quarter_count > 1:
        first = (lax.axis_index("ctx") % quarter_count) * head_width
        key_weight = lax.dynamic_slice_in_dim(key_weight, first, head_width, axis=1)
        value_weight = lax.dynamic_slice_in_dim(value_weight, first, head_width, axis=1)

    halves = norm_rows(tokens, norm_gain, routes)
    token_half = tok_count // 2
    steps = ctx_count // 2
    plan = [[0]] + [[-step, step] for step in range(1, steps)] + [[steps]]
    own, other, picked, queries, positions = [], [], [], [], []

    def send(parts):
        return [lax.ppermute(parts[0], "ctx", forward), lax.ppermute(parts[1], "ctx", backward)]

    def hand_over(panel):
        return lax.ppermute(panel, "exp", sibling)

    def tie(*arrays):
        return lax.optimization_barrier(arrays)

    blocks = halves
    lead = send([halves[0], halves[1]])
    rest = send([halves[1], halves[0]])
    for step in range(steps):
        keys, mark = project_keys(token_half, blocks, key_weight)
        following = [lead[0], rest[0], rest[1], lead[1]]
        if step == steps - 2:
            queries = project_queries(picked, query_slab)
            picked = []
        if step < steps - 1:
            mark, *lead_next = tie(mark, *lead, *queries)
            queries = lead_next[2:]
            lead = send(lead_next[:2])
        panel, rows, position = project_values(token_half, blocks, plan[step], mark, keys, value_weight)
        if step < steps - 2:
            position, *rest_next = tie(position, *rest)
            rest = send(rest_next)
        own.append(panel)
        picked.append(rows)
        positions.append(position)
        if step < steps - 1:
            other.append(hand_over(panel))
        blocks = following
    own[-1], *blocks = tie(own[-1], *lead)
    other.append(hand_over(own[-1]))
    keys, mark = project_keys(token_half, blocks, key_weight)
    panel, rows, position = project_values(token_half, blocks, plan[-1], mark, keys, value_weight)
    own.append(panel)
    other.append(hand_over(panel))
    positions.append(position)
    queries = [*queries, *project_queries(picked + [rows], query_slab)]
    held = arrange(ctx_count, plan, own, other, queries, positions)

    def swap(piece, k):
        return lax.ppermute(piece, "ctx", [(c, c ^ k) for c in range(ctx_count)])

    half, quarter = ctx_count // 2, ctx_count // 4
    far, mine = [], []
    for start, count in ((half, quarter), (half + quarter, quarter), (0, half)):
        pieces = attend((start // 2, count // 2), *held, output_slab)
        if start > 0:
            places, *pieces = tie(held[2], *pieces)
            held = [*held[:2], places]
            far.append([swap(piece, start + r) for r, piece in enumerate(pieces)])
        else:
            near = pieces
    *near, far[0][0] = tie(*near, far[0][0])
    near = [near[0]] + [swap(near[r], r) for r in range(1, half)]

    mix = gate_mix(quarter_count, halves, router_weight.T, ctx_count)
    return combine(mix, [*near, *far[0], *far[1]])


def solution(mesh):
    in_specs = (
        P(("groups", "ctx", "exp"), None),
        P(),
        P(),
        P(("groups", "ctx", "exp"), None),
        P(),
        P(),
        P("ctx", None, None),
        P("ctx", None, None),
    )
    out_specs = P(("groups", "ctx", "exp"), None)
    return jax.shard_map(
        per_device, mesh=mesh, in_specs=in_specs, out_specs=out_specs, check_vma=False
    )
```

```python
import functools
import math

import jax
import jax.numpy as jnp
from jax import lax
from jax.experimental import pallas as pl
from jax.experimental.pallas import tpu as pltpu
from jax.sharding import PartitionSpec as P

HS = 128
EXPERTS = 8
MOST = 40
SLOTS = 48
MASKED = -1e30
LANES = 128
CODES = 16
TERMS = 2
MIB = 1 << 20
WHOLE = pl.BlockSpec(memory_space=pltpu.VMEM)


def ring_rank(place, count):
    place = lax.rem(place + 2 * count, count)
    return jnp.where(place < count // 2, 2 * place, 2 * (count - 1 - place) + 1)


def ring_place(rank, count):
    return jnp.where(rank % 2 == 0, rank // 2, count - 1 - rank // 2)


def ring_owner(offset):
    count = lax.axis_size("ctx")
    return ring_rank(ring_place(lax.axis_index("ctx"), count) + offset, count)


def norm_kernel(*refs):
    sources, top_ref, bottom_ref, *held, arrivals = refs[:3], *refs[3:]
    copies = [
        pltpu.make_async_copy(source, target, arrivals.at[i])
        for i, (source, target) in enumerate(zip(sources, held))
    ]
    for copy in copies:
        copy.start()
    for copy in copies:
        copy.wait()
    tokens_ref, gain_ref, routes_ref = held
    floats = tokens_ref[...].astype(jnp.float32)
    count, width = floats.shape
    factor = lax.rsqrt(jnp.mean(floats * floats, axis=1, keepdims=True) + 1e-06)
    normed = (floats * factor * gain_ref[...]).astype(jnp.bfloat16)
    expert = lax.broadcasted_iota(jnp.int32, (CODES, count), 0)
    named = (expert == routes_ref[0:1, :]) | (expert == routes_ref[1:2, :])
    before = lax.broadcasted_iota(jnp.int32, (count, count), 0) < lax.broadcasted_iota(
        jnp.int32, (count, count), 1
    )
    rank = jnp.dot(
        named.astype(jnp.bfloat16),
        before.astype(jnp.bfloat16),
        preferred_element_type=jnp.float32,
    )
    codes = jnp.where(named, rank, -1.0).astype(jnp.bfloat16)
    half = count // 2
    for ref, first in ((top_ref, 0), (bottom_ref, half)):
        for c in range(width // LANES):
            ref[pl.ds(c * half, half), :] = normed[
                first : first + half, c * LANES : (c + 1) * LANES
            ]
        ref[pl.ds(width // LANES * half, CODES), :] = codes


def message_rows(ref, half):
    tiles = (ref.shape[0] - CODES) // half
    return jnp.concatenate([ref[pl.ds(c * half, half), :] for c in range(tiles)], axis=1)


def message_codes(ref):
    return ref[pl.ds(ref.shape[0] - CODES, CODES), :].astype(jnp.float32)


def norm_rows(tokens, norm_gain, routes):
    count, width = tokens.shape
    half = jax.ShapeDtypeStruct((width // LANES * (count // 2) + CODES, LANES), jnp.bfloat16)
    operands = (tokens, norm_gain.reshape(1, -1), routes.T)
    return pl.pallas_call(
        norm_kernel,
        in_specs=[pl.BlockSpec(memory_space=pltpu.HBM)] * 3,
        out_specs=[WHOLE] * 2,
        out_shape=[half, half],
        scratch_shapes=[pltpu.VMEM(x.shape, x.dtype) for x in operands]
        + [pltpu.SemaphoreType.DMA((3,))],
        compiler_params=pltpu.CompilerParams(vmem_limit_bytes=60 * MIB),
        name="norm_rows",
    )(*operands)


def column_parts(ref):
    step = min(ref.shape[1], 256)
    return [pl.ds(start, step) for start in range(0, ref.shape[1], step)]


def keys_kernel(half, count, *refs):
    blocks = refs[:count]
    weight_ref, panel_ref, mark_ref = refs[count:]
    rows = jnp.concatenate([message_rows(block, half) for block in blocks], axis=0)
    for cols in column_parts(weight_ref):
        product = jnp.dot(rows, weight_ref[:, cols], preferred_element_type=jnp.float32)
        panel_ref[:, cols] = product.astype(jnp.bfloat16)
    mark_ref[...] = product[:8, :LANES]


def project_keys(half, blocks, key_weight):
    row_count = half * len(blocks)
    width = key_weight.shape[1]
    return pl.pallas_call(
        functools.partial(keys_kernel, half, len(blocks)),
        in_specs=[WHOLE] * (len(blocks) + 1),
        out_specs=[WHOLE] * 2,
        out_shape=[
            jax.ShapeDtypeStruct((row_count, width), jnp.bfloat16),
            jax.ShapeDtypeStruct((8, LANES), jnp.float32),
        ],
        compiler_params=pltpu.CompilerParams(vmem_limit_bytes=12 * MIB),
        name="project_keys",
    )(*blocks, key_weight)


def values_kernel(half, offsets, count, experts, mark_ref, keys_ref, *refs):
    blocks = refs[:count]
    value_ref, panel_ref, picked_ref, pos_ref = refs[count:]
    rows = jnp.concatenate([message_rows(block, half) for block in blocks], axis=0)
    tok_count = 2 * half
    expert = lax.axis_index("ctx") // (lax.axis_size("ctx") // experts)
    number = lax.broadcasted_iota(jnp.int32, (tok_count, LANES), 0).astype(jnp.bfloat16)
    for g, offset in enumerate(offsets):
        part = slice(g * tok_count, (g + 1) * tok_count)
        codes = message_codes(blocks[2 * g])
        mine = lax.broadcasted_iota(jnp.int32, codes.shape, 0) == expert
        slot = jnp.sum(jnp.where(mine, codes, 0.0), axis=0, keepdims=True)
        order = lax.broadcasted_iota(jnp.int32, (SLOTS, tok_count), 0).astype(jnp.float32)
        chosen = (order == slot).astype(jnp.bfloat16)
        picked_ref[g] = jnp.dot(
            chosen, rows[part], preferred_element_type=jnp.float32
        ).astype(jnp.bfloat16)
        start = (ring_owner(offset) * lax.axis_size("exp") + lax.axis_index("exp")) * tok_count
        pos_ref[g] = jnp.dot(
            chosen, number, preferred_element_type=jnp.float32
        ) + start.astype(jnp.float32)
    panel_ref[0] = keys_ref[...]
    for cols in column_parts(value_ref):
        panel_ref[1, :, cols] = jnp.dot(
            rows, value_ref[:, cols], preferred_element_type=jnp.float32
        ).astype(jnp.bfloat16)


def project_values(half, blocks, offsets, mark, keys, value_weight):
    row_count = half * len(blocks)
    model_width, width = value_weight.shape
    owners = len(offsets)
    return pl.pallas_call(
        functools.partial(values_kernel, half, offsets, len(blocks), EXPERTS),
        in_specs=[WHOLE] * (len(blocks) + 3),
        out_specs=[WHOLE] * 3,
        out_shape=[
            jax.ShapeDtypeStruct((2, row_count, width), jnp.bfloat16),
            jax.ShapeDtypeStruct((owners, SLOTS, model_width), jnp.bfloat16),
            jax.ShapeDtypeStruct((owners, SLOTS, LANES), jnp.float32),
        ],
        compiler_params=pltpu.CompilerParams(vmem_limit_bytes=12 * MIB),
        name="project_values",
    )(mark, keys, *blocks, value_weight)


def queries_kernel(*refs):
    count = len(refs) // 2 - 1
    picked, weight_ref, outs = refs[:count], refs[count], refs[count + 2 :]
    rows = jnp.concatenate([ref[g] for ref in picked for g in range(ref.shape[0])], axis=0)
    places = [(ref, g) for ref in outs for g in range(ref.shape[0])]
    for cols in column_parts(weight_ref):
        product = jnp.dot(rows, weight_ref[:, cols], preferred_element_type=jnp.float32)
        for i, (ref, g) in enumerate(places):
            ref[g, :, cols] = product[i * SLOTS : (i + 1) * SLOTS].astype(jnp.bfloat16)


def project_queries(picked, query_slab, next_slab):
    model_width, width = query_slab.shape
    owners = sum(rows.shape[0] for rows in picked)
    held = 4 * model_width * width + owners * SLOTS * (4 * model_width + 4 * width)
    return pl.pallas_call(
        queries_kernel,
        in_specs=[WHOLE] * (len(picked) + 2),
        out_specs=[WHOLE] * len(picked),
        out_shape=[
            jax.ShapeDtypeStruct((rows.shape[0], SLOTS, width), jnp.bfloat16) for rows in picked
        ],
        compiler_params=pltpu.CompilerParams(vmem_limit_bytes=held + 6 * MIB),
        name="project_queries",
    )(*picked, query_slab, next_slab)


def arrange_kernel(plan, *refs):
    count = len(plan)
    own_refs, other_refs, query_refs, pos_refs = (refs[k * count : (k + 1) * count] for k in range(4))
    panel_ref, queries_ref, places_ref = refs[4 * count :]
    exp_count = 2
    side = lax.axis_index("exp")
    tok_count = panel_ref.shape[2]
    for offsets, own_ref, other_ref, query_ref, pos_ref in zip(
        plan, own_refs, other_refs, query_refs, pos_refs
    ):
        for g, offset in enumerate(offsets):
            owner = ring_owner(offset)
            part = pl.ds(g * tok_count, tok_count)
            for which in range(2):
                panel_ref[which, owner * exp_count + side] = own_ref[which, part]
                panel_ref[which, owner * exp_count + 1 - side] = other_ref[which, part]
            queries_ref[owner] = query_ref[g]
            places_ref[owner] = pos_ref[g]


def arrange(owners, plan, own, other, queries, positions):
    width = own[0].shape[2]
    tok_count = own[0].shape[1] // len(plan[0])
    shapes = [
        jax.ShapeDtypeStruct((2, 2 * owners, tok_count, width), jnp.bfloat16),
        jax.ShapeDtypeStruct((owners, SLOTS, width), jnp.bfloat16),
        jax.ShapeDtypeStruct((owners, SLOTS, LANES), jnp.float32),
    ]
    operands = (*own, *other, *queries, *positions)
    return pl.pallas_call(
        functools.partial(arrange_kernel, plan),
        in_specs=[WHOLE] * len(operands),
        out_specs=[WHOLE] * 3,
        out_shape=shapes,
        compiler_params=pltpu.CompilerParams(
            vmem_limit_bytes=8 * MIB
        ),
        name="arrange",
    )(*operands)


def attend_kernel(lots, heads, panel_ref, queries_ref, places_ref, weight_ref, *refs):
    outs, (attended, scores, weights) = refs[:-3], refs[-3:]
    first, count = lots
    blocks, tok_count, width = panel_ref.shape[1:]
    rate = math.log2(math.e) / math.sqrt(HS)
    rank = lax.axis_index("ctx")
    tiles = blocks // 4
    tile = 2 * SLOTS
    parts = 4
    span = blocks * tok_count // parts
    per_span = blocks // parts
    passes = width // (heads * HS)

    def serve(part_id, number, lot, lanes):
        reach = (part_id + 1) * span
        pair = pl.ds(2 * number, 2)
        spots = places_ref[pair].reshape(tile, LANES)
        held, sums = {}, {}

        def score(h, j):
            if j == 0:
                held[h] = queries_ref[pair, :, lanes[h]].reshape(tile, HS)
            key_part = panel_ref[0, per_span * j : per_span * (j + 1), :, lanes[h]]
            scores[h, :, pl.ds(j * span, span)] = lax.dot_general(
                held[h],
                key_part.reshape(span, HS),
                (((1,), (1,)), ((), ())),
                preferred_element_type=jnp.float32,
            )

        def weigh(h, sub):
            rows = pl.ds(sub * 16, 16)
            part = scores[h, rows, pl.ds(0, reach)]
            last = part[:, reach - span :]
            key_index = lax.broadcasted_iota(jnp.int32, last.shape, 1) + (reach - span)
            spot = spots[sub * 16 : sub * 16 + 16, 0:1]
            last = jnp.where(key_index.astype(jnp.float32) <= spot, last, MASKED)
            if part_id > 0:
                part = jnp.concatenate([part[:, : reach - span], last], axis=1)
            else:
                part = last
            peak = jnp.max(part, axis=1, keepdims=True)
            raised = jnp.exp2((part - peak) * rate)
            total = jnp.sum(raised, axis=1, keepdims=True)
            weights[h, rows, pl.ds(0, reach)] = (raised * (1.0 / total)).astype(jnp.bfloat16)

        def gather(h, j):
            value_part = panel_ref[1, per_span * j : per_span * (j + 1), :, lanes[h]]
            product = jnp.dot(
                weights[h, :, pl.ds(j * span, span)],
                value_part.reshape(span, HS),
                preferred_element_type=jnp.float32,
            )
            sums[h] = product if j == 0 else sums[h] + product
            if j == part_id:
                total = sums[h].astype(jnp.bfloat16)
                for side in range(2):
                    attended[2 * lot + (side ^ (rank % 2)), :, lanes[h]] = total[
                        side * SLOTS : (side + 1) * SLOTS
                    ]

        for h in range(heads + 2):
            for i in range(max(tile // 16, parts)):
                if 0 < h <= heads and i < tile // 16:
                    weigh(h - 1, i)
                if h < heads and i <= part_id:
                    score(h, i)
                if h > 1 and i <= part_id:
                    gather(h - 2, i)

    def one(at, carry):
        lot, now = at // passes, at % passes
        number = (rank // 2) ^ (first + lot)
        lanes = [pl.ds(pl.multiple_of((now * heads + h) * HS, HS), HS) for h in range(heads)]
        for part_id in range(parts):
            pl.when(number // (tiles // parts) == part_id)(
                functools.partial(serve, part_id, number, lot, lanes)
            )
        return carry

    lax.fori_loop(0, count * passes, one, 0)
    rows = attended[...].reshape(2 * count * SLOTS, width)
    for cols in column_parts(weight_ref):
        product = jnp.dot(rows, weight_ref[:, cols], preferred_element_type=jnp.float32)
        for k, out_ref in enumerate(outs):
            out_ref[:, cols] = product[k * SLOTS : k * SLOTS + MOST].astype(jnp.bfloat16)


def attend(lots, panel, queries, places, output_slab):
    first, count = lots
    _, blocks, tok_count, width = panel.shape
    length = blocks * tok_count
    heads = min(4, width // HS) if blocks <= 16 else 1
    model_width = output_slab.shape[1]
    held = heads * 2 * SLOTS * length * 6 + 2 * length * width * 2 + width * model_width * 2
    held += 2 * count * SLOTS * (model_width * 8 + width * 2)
    return pl.pallas_call(
        functools.partial(attend_kernel, lots, heads),
        in_specs=[WHOLE] * 4,
        out_specs=[WHOLE] * (2 * count),
        out_shape=[jax.ShapeDtypeStruct((MOST, model_width), jnp.bfloat16)] * (2 * count),
        scratch_shapes=[
            pltpu.VMEM((2 * count, SLOTS, width), jnp.bfloat16),
            pltpu.VMEM((heads, 2 * SLOTS, length), jnp.float32),
            pltpu.VMEM((heads, 2 * SLOTS, length), jnp.bfloat16),
        ],
        compiler_params=pltpu.CompilerParams(vmem_limit_bytes=held * 9 // 8 + 4 * MIB),
        cost_estimate=pl.CostEstimate(
            flops=count * 2 * SLOTS * width * (4 * length + 2 * model_width),
            bytes_accessed=4 * length * width,
            transcendentals=count * 2 * SLOTS * length * width // HS,
        ),
        name="attend",
    )(panel, queries, places, output_slab)


def mix_kernel(quarter_count, top_ref, bottom_ref, router_ref, mix_ref, slots_ref, gates_ref):
    half = LANES // 2
    rows = jnp.concatenate([message_rows(ref, half) for ref in (top_ref, bottom_ref)], axis=0)
    rest, terms = router_ref[...], []
    for _ in range(3):
        terms.append(rest.astype(jnp.bfloat16).astype(jnp.float32))
        rest = rest - terms[-1]
    experts = rest.shape[0]
    router = jnp.concatenate([*terms, jnp.zeros_like(rest)], axis=0).astype(jnp.bfloat16)
    products = lax.dot_general(
        router, rows, (((1,), (1,)), ((), ())), preferred_element_type=jnp.float32
    )
    logits = products[:experts] + (
        products[experts : 2 * experts] + products[2 * experts : 3 * experts]
    )
    slots = message_codes(top_ref)[:experts]
    logits = jnp.where(slots >= 0, logits, -jnp.inf)
    raised = jnp.exp(logits - jnp.max(logits, axis=0, keepdims=True))
    slots_ref[...] = slots
    gates_ref[...] = raised / jnp.sum(raised, axis=0, keepdims=True)
    tok_count = slots.shape[1]
    order = lax.broadcasted_iota(jnp.int32, (SLOTS, tok_count), 0).astype(jnp.float32)
    parts = []
    for k in range(mix_ref.shape[1] // SLOTS):
        expert = pl.ds((lax.axis_index("ctx") ^ k) // quarter_count, 1)
        parts.append(jnp.where(order == slots_ref[expert, :], gates_ref[expert, :], 0.0))
    total = jnp.concatenate(parts, axis=0).T
    for part in range(TERMS):
        term = total.astype(jnp.bfloat16)
        mix_ref[pl.ds(part * tok_count, tok_count), :] = term
        total = total - term.astype(jnp.float32)


def gate_mix(quarter_count, halves, router, count):
    tok_count = LANES
    held = pltpu.VMEM((router.shape[0], tok_count), jnp.float32)
    return pl.pallas_call(
        functools.partial(mix_kernel, quarter_count),
        in_specs=[WHOLE] * 3,
        out_specs=WHOLE,
        out_shape=jax.ShapeDtypeStruct((TERMS * tok_count, count * SLOTS), jnp.bfloat16),
        scratch_shapes=[held, held],
        compiler_params=pltpu.CompilerParams(vmem_limit_bytes=16 * MIB),
        name="gate_mix",
    )(*halves, router)


def combine_kernel(mix_ref, *refs):
    pieces, out_ref = refs[:-1], refs[-1]
    tok_count, model_width = out_ref.shape
    step = min(model_width, 512)
    spare = jnp.zeros((SLOTS - MOST, step), jnp.float32)
    for start in range(0, model_width, step):
        cols = pl.ds(start, step)
        rows = []
        for piece in pieces:
            rows += [piece[:, cols].astype(jnp.float32), spare]
        rows = jnp.concatenate(rows, axis=0).astype(jnp.bfloat16)
        product = jnp.dot(mix_ref[...], rows, preferred_element_type=jnp.float32)
        total = product[-tok_count:]
        for part in range(TERMS - 2, -1, -1):
            total = product[part * tok_count : (part + 1) * tok_count] + total
        out_ref[:, cols] = total.astype(jnp.bfloat16)


def combine(mix, pieces):
    tok_count = mix.shape[0] // TERMS
    model_width = pieces[0].shape[1]
    return pl.pallas_call(
        combine_kernel,
        in_specs=[WHOLE] * (1 + len(pieces)),
        out_specs=WHOLE,
        out_shape=jax.ShapeDtypeStruct((tok_count, model_width), jnp.bfloat16),
        compiler_params=pltpu.CompilerParams(vmem_limit_bytes=24 * MIB),
        name="combine",
    )(mix, *pieces)


def per_device(
    tokens, norm_gain, router_weight, routes, key_weight, value_weight, query_weight, output_weight
):
    tok_count, model_width = tokens.shape
    ctx_count = lax.axis_size("ctx")
    exp_count = lax.axis_size("exp")
    quarter_count = ctx_count // EXPERTS
    head_width = query_weight.shape[2]
    ranks = list(range(0, ctx_count, 2)) + list(range(1, ctx_count, 2))[::-1]
    forward = [(ranks[p], ranks[(p + 1) % ctx_count]) for p in range(ctx_count)]
    backward = [(b, a) for a, b in forward]
    sibling = [(e, 1 - e) for e in range(exp_count)]
    query_slab = query_weight[0]
    output_slab = output_weight[0]
    if quarter_count > 1:
        first = (lax.axis_index("ctx") % quarter_count) * head_width
        key_weight = lax.dynamic_slice_in_dim(key_weight, first, head_width, axis=1)
        value_weight = lax.dynamic_slice_in_dim(value_weight, first, head_width, axis=1)

    halves = norm_rows(tokens, norm_gain, routes)
    token_half = tok_count // 2
    steps = ctx_count // 2
    plan = [[0]] + [[-step, step] for step in range(1, steps)] + [[steps]]
    own, other, picked, queries, positions = [], [], [], [], []

    def send(parts):
        return [lax.ppermute(parts[0], "ctx", forward), lax.ppermute(parts[1], "ctx", backward)]

    def hand_over(panel):
        return lax.ppermute(panel, "exp", sibling)

    def tie(*arrays):
        return lax.optimization_barrier(arrays)

    blocks = halves
    lead = send([halves[0], halves[1]])
    rest = send([halves[1], halves[0]])
    for step in range(steps):
        keys, mark = project_keys(token_half, blocks, key_weight)
        following = [lead[0], rest[0], rest[1], lead[1]]
        if step == steps - 2:
            queries = project_queries(picked, query_slab, output_slab)
            picked = []
        if step < steps - 1:
            mark, *lead_next = tie(mark, *lead, *queries)
            queries = lead_next[2:]
            lead = send(lead_next[:2])
        panel, rows, position = project_values(token_half, blocks, plan[step], mark, keys, value_weight)
        if step < steps - 2:
            position, *rest_next = tie(position, *rest)
            rest = send(rest_next)
        own.append(panel)
        picked.append(rows)
        positions.append(position)
        if step < steps - 1:
            other.append(hand_over(panel))
        blocks = following
    queries = [*queries, *project_queries(picked, query_slab, output_slab)]
    own[-1], queries[-1], *blocks = tie(own[-1], queries[-1], *lead)
    other.append(hand_over(own[-1]))
    keys, mark = project_keys(token_half, blocks, key_weight)
    panel, rows, position = project_values(token_half, blocks, plan[-1], mark, keys, value_weight)
    own.append(panel)
    other.append(hand_over(panel))
    positions.append(position)
    queries = [*queries, *project_queries([rows], query_slab, output_slab)]
    held = arrange(ctx_count, plan, own, other, queries, positions)

    def swap(piece, k):
        return lax.ppermute(piece, "ctx", [(c, c ^ k) for c in range(ctx_count)])

    half, quarter = ctx_count // 2, ctx_count // 4
    far, mine = [], []
    for start, count in ((half, quarter), (half + quarter, quarter), (0, half)):
        pieces = attend((start // 2, count // 2), *held, output_slab)
        if start > 0:
            places, *pieces = tie(held[2], *pieces)
            held = [*held[:2], places]
            far.append([swap(piece, start + r) for r, piece in enumerate(pieces)])
        else:
            near = pieces
    *near, far[0][0] = tie(*near, far[0][0])
    near = [near[0]] + [swap(near[r], r) for r in range(1, half)]

    mix = gate_mix(quarter_count, halves, router_weight.T, ctx_count)
    return combine(mix, [*near, *far[0], *far[1]])


def solution(mesh):
    in_specs = (
        P(("groups", "ctx", "exp"), None),
        P(),
        P(),
        P(("groups", "ctx", "exp"), None),
        P(),
        P(),
        P("ctx", None, None),
        P("ctx", None, None),
    )
    out_specs = P(("groups", "ctx", "exp"), None)
    return jax.shard_map(
        per_device, mesh=mesh, in_specs=in_specs, out_specs=out_specs, check_vma=False
    )
```

```python
import functools
import math

import jax
import jax.numpy as jnp
from jax import lax
from jax.experimental import pallas as pl
from jax.experimental.pallas import tpu as pltpu
from jax.sharding import PartitionSpec as P

HS = 128
EXPERTS = 8
MOST = 40
SLOTS = 48
MASKED = -1e30
LANES = 128
CODES = 16
TERMS = 2
MIB = 1 << 20
WHOLE = pl.BlockSpec(memory_space=pltpu.VMEM)


def ring_rank(place, count):
    place = lax.rem(place + 2 * count, count)
    return jnp.where(place < count // 2, 2 * place, 2 * (count - 1 - place) + 1)


def ring_place(rank, count):
    return jnp.where(rank % 2 == 0, rank // 2, count - 1 - rank // 2)


def ring_owner(offset):
    count = lax.axis_size("ctx")
    return ring_rank(ring_place(lax.axis_index("ctx"), count) + offset, count)


def norm_kernel(*refs):
    sources, top_ref, bottom_ref, *held, arrivals = refs[:3], *refs[3:]
    copies = [
        pltpu.make_async_copy(source, target, arrivals.at[i])
        for i, (source, target) in enumerate(zip(sources, held))
    ]
    for copy in copies:
        copy.start()
    for copy in copies:
        copy.wait()
    tokens_ref, gain_ref, routes_ref = held
    floats = tokens_ref[...].astype(jnp.float32)
    count, width = floats.shape
    factor = lax.rsqrt(jnp.mean(floats * floats, axis=1, keepdims=True) + 1e-06)
    normed = (floats * factor * gain_ref[...]).astype(jnp.bfloat16)
    expert = lax.broadcasted_iota(jnp.int32, (CODES, count), 0)
    named = (expert == routes_ref[0:1, :]) | (expert == routes_ref[1:2, :])
    before = lax.broadcasted_iota(jnp.int32, (count, count), 0) < lax.broadcasted_iota(
        jnp.int32, (count, count), 1
    )
    rank = jnp.dot(
        named.astype(jnp.bfloat16),
        before.astype(jnp.bfloat16),
        preferred_element_type=jnp.float32,
    )
    codes = jnp.where(named, rank, -1.0).astype(jnp.bfloat16)
    half = count // 2
    for ref, first in ((top_ref, 0), (bottom_ref, half)):
        for c in range(width // LANES):
            ref[pl.ds(c * half, half), :] = normed[
                first : first + half, c * LANES : (c + 1) * LANES
            ]
        ref[pl.ds(width // LANES * half, CODES), :] = codes


def message_rows(ref, half):
    tiles = (ref.shape[0] - CODES) // half
    return jnp.concatenate([ref[pl.ds(c * half, half), :] for c in range(tiles)], axis=1)


def message_codes(ref):
    return ref[pl.ds(ref.shape[0] - CODES, CODES), :].astype(jnp.float32)


def norm_rows(tokens, norm_gain, routes):
    count, width = tokens.shape
    half = jax.ShapeDtypeStruct((width // LANES * (count // 2) + CODES, LANES), jnp.bfloat16)
    operands = (tokens, norm_gain.reshape(1, -1), routes.T)
    return pl.pallas_call(
        norm_kernel,
        in_specs=[pl.BlockSpec(memory_space=pltpu.HBM)] * 3,
        out_specs=[WHOLE] * 2,
        out_shape=[half, half],
        scratch_shapes=[pltpu.VMEM(x.shape, x.dtype) for x in operands]
        + [pltpu.SemaphoreType.DMA((3,))],
        compiler_params=pltpu.CompilerParams(vmem_limit_bytes=60 * MIB),
        name="norm_rows",
    )(*operands)


def column_parts(ref):
    step = min(ref.shape[1], 256)
    return [pl.ds(start, step) for start in range(0, ref.shape[1], step)]


def keys_kernel(half, count, *refs):
    blocks = refs[:count]
    weight_ref, panel_ref, mark_ref = refs[count:]
    rows = jnp.concatenate([message_rows(block, half) for block in blocks], axis=0)
    for cols in column_parts(weight_ref):
        product = jnp.dot(rows, weight_ref[:, cols], preferred_element_type=jnp.float32)
        panel_ref[:, cols] = product.astype(jnp.bfloat16)
    mark_ref[...] = product[:8, :LANES]


def project_keys(half, blocks, key_weight):
    row_count = half * len(blocks)
    width = key_weight.shape[1]
    return pl.pallas_call(
        functools.partial(keys_kernel, half, len(blocks)),
        in_specs=[WHOLE] * (len(blocks) + 1),
        out_specs=[WHOLE] * 2,
        out_shape=[
            jax.ShapeDtypeStruct((row_count, width), jnp.bfloat16),
            jax.ShapeDtypeStruct((8, LANES), jnp.float32),
        ],
        compiler_params=pltpu.CompilerParams(vmem_limit_bytes=12 * MIB),
        name="project_keys",
    )(*blocks, key_weight)


def values_kernel(half, offsets, count, experts, mark_ref, keys_ref, *refs):
    blocks = refs[:count]
    value_ref, panel_ref, picked_ref, pos_ref = refs[count:]
    rows = jnp.concatenate([message_rows(block, half) for block in blocks], axis=0)
    tok_count = 2 * half
    expert = lax.axis_index("ctx") // (lax.axis_size("ctx") // experts)
    number = lax.broadcasted_iota(jnp.int32, (tok_count, LANES), 0).astype(jnp.bfloat16)
    for g, offset in enumerate(offsets):
        part = slice(g * tok_count, (g + 1) * tok_count)
        codes = message_codes(blocks[2 * g])
        mine = lax.broadcasted_iota(jnp.int32, codes.shape, 0) == expert
        slot = jnp.sum(jnp.where(mine, codes, 0.0), axis=0, keepdims=True)
        order = lax.broadcasted_iota(jnp.int32, (SLOTS, tok_count), 0).astype(jnp.float32)
        chosen = (order == slot).astype(jnp.bfloat16)
        picked_ref[g] = jnp.dot(
            chosen, rows[part], preferred_element_type=jnp.float32
        ).astype(jnp.bfloat16)
        start = (ring_owner(offset) * lax.axis_size("exp") + lax.axis_index("exp")) * tok_count
        pos_ref[g] = jnp.dot(
            chosen, number, preferred_element_type=jnp.float32
        ) + start.astype(jnp.float32)
    panel_ref[0] = keys_ref[...]
    for cols in column_parts(value_ref):
        panel_ref[1, :, cols] = jnp.dot(
            rows, value_ref[:, cols], preferred_element_type=jnp.float32
        ).astype(jnp.bfloat16)


def project_values(half, blocks, offsets, mark, keys, value_weight):
    row_count = half * len(blocks)
    model_width, width = value_weight.shape
    owners = len(offsets)
    return pl.pallas_call(
        functools.partial(values_kernel, half, offsets, len(blocks), EXPERTS),
        in_specs=[WHOLE] * (len(blocks) + 3),
        out_specs=[WHOLE] * 3,
        out_shape=[
            jax.ShapeDtypeStruct((2, row_count, width), jnp.bfloat16),
            jax.ShapeDtypeStruct((owners, SLOTS, model_width), jnp.bfloat16),
            jax.ShapeDtypeStruct((owners, SLOTS, LANES), jnp.float32),
        ],
        compiler_params=pltpu.CompilerParams(vmem_limit_bytes=12 * MIB),
        name="project_values",
    )(mark, keys, *blocks, value_weight)


def queries_kernel(*refs):
    count = len(refs) // 2 - 1
    picked, weight_ref, outs = refs[:count], refs[count], refs[count + 2 :]
    rows = jnp.concatenate([ref[g] for ref in picked for g in range(ref.shape[0])], axis=0)
    places = [(ref, g) for ref in outs for g in range(ref.shape[0])]
    for cols in column_parts(weight_ref):
        product = jnp.dot(rows, weight_ref[:, cols], preferred_element_type=jnp.float32)
        for i, (ref, g) in enumerate(places):
            ref[g, :, cols] = product[i * SLOTS : (i + 1) * SLOTS].astype(jnp.bfloat16)


def project_queries(picked, query_slab, next_slab):
    model_width, width = query_slab.shape
    owners = sum(rows.shape[0] for rows in picked)
    held = 4 * model_width * width + owners * SLOTS * (4 * model_width + 4 * width)
    return pl.pallas_call(
        queries_kernel,
        in_specs=[WHOLE] * (len(picked) + 2),
        out_specs=[WHOLE] * len(picked),
        out_shape=[
            jax.ShapeDtypeStruct((rows.shape[0], SLOTS, width), jnp.bfloat16) for rows in picked
        ],
        compiler_params=pltpu.CompilerParams(vmem_limit_bytes=held + 6 * MIB),
        name="project_queries",
    )(*picked, query_slab, next_slab)


def arrange_kernel(plan, *refs):
    count = len(plan)
    own_refs, other_refs, query_refs, pos_refs = (refs[k * count : (k + 1) * count] for k in range(4))
    panel_ref, queries_ref, places_ref = refs[4 * count :]
    exp_count = 2
    side = lax.axis_index("exp")
    tok_count = panel_ref.shape[2]
    for offsets, own_ref, other_ref, query_ref, pos_ref in zip(
        plan, own_refs, other_refs, query_refs, pos_refs
    ):
        for g, offset in enumerate(offsets):
            owner = ring_owner(offset)
            part = pl.ds(g * tok_count, tok_count)
            for which in range(2):
                panel_ref[which, owner * exp_count + side] = own_ref[which, part]
                panel_ref[which, owner * exp_count + 1 - side] = other_ref[which, part]
            queries_ref[owner] = query_ref[g]
            places_ref[owner] = pos_ref[g]


def arrange(owners, plan, own, other, queries, positions):
    width = own[0].shape[2]
    tok_count = own[0].shape[1] // len(plan[0])
    shapes = [
        jax.ShapeDtypeStruct((2, 2 * owners, tok_count, width), jnp.bfloat16),
        jax.ShapeDtypeStruct((owners, SLOTS, width), jnp.bfloat16),
        jax.ShapeDtypeStruct((owners, SLOTS, LANES), jnp.float32),
    ]
    operands = (*own, *other, *queries, *positions)
    return pl.pallas_call(
        functools.partial(arrange_kernel, plan),
        in_specs=[WHOLE] * len(operands),
        out_specs=[WHOLE] * 3,
        out_shape=shapes,
        compiler_params=pltpu.CompilerParams(
            vmem_limit_bytes=8 * MIB
        ),
        name="arrange",
    )(*operands)


def attend_kernel(lots, heads, panel_ref, queries_ref, places_ref, weight_ref, *refs):
    outs, (attended, scores, weights) = refs[:-3], refs[-3:]
    first, count = lots
    blocks, tok_count, width = panel_ref.shape[1:]
    rate = math.log2(math.e) / math.sqrt(HS)
    rank = lax.axis_index("ctx")
    tiles = blocks // 4
    tile = 2 * SLOTS
    parts = 4
    span = blocks * tok_count // parts
    per_span = blocks // parts
    passes = width // (heads * HS)

    def serve(part_id, number, lot, lanes):
        reach = (part_id + 1) * span
        pair = pl.ds(2 * number, 2)
        spots = places_ref[pair].reshape(tile, LANES)
        for h in range(heads):
            held = queries_ref[pair, :, lanes[h]].reshape(tile, HS)
            for j in range(part_id + 1):
                key_part = panel_ref[0, per_span * j : per_span * (j + 1), :, lanes[h]]
                scores[h, :, pl.ds(j * span, span)] = lax.dot_general(
                    held,
                    key_part.reshape(span, HS),
                    (((1,), (1,)), ((), ())),
                    preferred_element_type=jnp.float32,
                )
        for h in range(heads):
            for sub in range(0, tile, 16):
                rows = pl.ds(sub, 16)
                part = scores[h, rows, pl.ds(0, reach)]
                last = part[:, reach - span :]
                key_index = lax.broadcasted_iota(jnp.int32, last.shape, 1) + (reach - span)
                spot = spots[sub : sub + 16, 0:1]
                last = jnp.where(key_index.astype(jnp.float32) <= spot, last, MASKED)
                if part_id > 0:
                    part = jnp.concatenate([part[:, : reach - span], last], axis=1)
                else:
                    part = last
                peak = jnp.max(part, axis=1, keepdims=True)
                raised = jnp.exp2((part - peak) * rate)
                total = jnp.sum(raised, axis=1, keepdims=True)
                weights[h, rows, pl.ds(0, reach)] = (raised * (1.0 / total)).astype(jnp.bfloat16)
        for h in range(heads):
            total = None
            for j in range(part_id + 1):
                value_part = panel_ref[1, per_span * j : per_span * (j + 1), :, lanes[h]]
                product = jnp.dot(
                    weights[h, :, pl.ds(j * span, span)],
                    value_part.reshape(span, HS),
                    preferred_element_type=jnp.float32,
                )
                total = product if total is None else total + product
            total = total.astype(jnp.bfloat16)
            for side in range(2):
                attended[2 * lot + (side ^ (rank % 2)), :, lanes[h]] = total[
                    side * SLOTS : (side + 1) * SLOTS
                ]

    def one(at, carry):
        lot, now = at // passes, at % passes
        number = (rank // 2) ^ (first + lot)
        lanes = [pl.ds(pl.multiple_of((now * heads + h) * HS, HS), HS) for h in range(heads)]
        for part_id in range(parts):
            pl.when(number // (tiles // parts) == part_id)(
                functools.partial(serve, part_id, number, lot, lanes)
            )
        return carry

    lax.fori_loop(0, count * passes, one, 0)
    rows = attended[...].reshape(2 * count * SLOTS, width)
    for cols in column_parts(weight_ref):
        product = jnp.dot(rows, weight_ref[:, cols], preferred_element_type=jnp.float32)
        for k, out_ref in enumerate(outs):
            out_ref[:, cols] = product[k * SLOTS : k * SLOTS + MOST].astype(jnp.bfloat16)


def attend(lots, panel, queries, places, output_slab):
    first, count = lots
    _, blocks, tok_count, width = panel.shape
    length = blocks * tok_count
    heads = min(2, width // HS) if blocks <= 16 else 1
    model_width = output_slab.shape[1]
    held = heads * 2 * SLOTS * length * 6 + 2 * length * width * 2 + width * model_width * 2
    held += 2 * count * SLOTS * (model_width * 8 + width * 2)
    return pl.pallas_call(
        functools.partial(attend_kernel, lots, heads),
        in_specs=[WHOLE] * 4,
        out_specs=[WHOLE] * (2 * count),
        out_shape=[jax.ShapeDtypeStruct((MOST, model_width), jnp.bfloat16)] * (2 * count),
        scratch_shapes=[
            pltpu.VMEM((2 * count, SLOTS, width), jnp.bfloat16),
            pltpu.VMEM((heads, 2 * SLOTS, length), jnp.float32),
            pltpu.VMEM((heads, 2 * SLOTS, length), jnp.bfloat16),
        ],
        compiler_params=pltpu.CompilerParams(vmem_limit_bytes=held * 9 // 8 + 4 * MIB),
        cost_estimate=pl.CostEstimate(
            flops=count * 2 * SLOTS * width * (4 * length + 2 * model_width),
            bytes_accessed=4 * length * width,
            transcendentals=count * 2 * SLOTS * length * width // HS,
        ),
        name="attend",
    )(panel, queries, places, output_slab)


def order_of_pieces(count):
    return [0, *range(count // 2 - 1, 0, -1), *range(count // 2, count)]


def mix_kernel(quarter_count, top_ref, bottom_ref, router_ref, mix_ref, slots_ref, gates_ref):
    half = LANES // 2
    rows = jnp.concatenate([message_rows(ref, half) for ref in (top_ref, bottom_ref)], axis=0)
    rest, terms = router_ref[...], []
    for _ in range(3):
        terms.append(rest.astype(jnp.bfloat16).astype(jnp.float32))
        rest = rest - terms[-1]
    experts = rest.shape[0]
    router = jnp.concatenate([*terms, jnp.zeros_like(rest)], axis=0).astype(jnp.bfloat16)
    products = lax.dot_general(
        router, rows, (((1,), (1,)), ((), ())), preferred_element_type=jnp.float32
    )
    logits = products[:experts] + (
        products[experts : 2 * experts] + products[2 * experts : 3 * experts]
    )
    slots = message_codes(top_ref)[:experts]
    logits = jnp.where(slots >= 0, logits, -jnp.inf)
    raised = jnp.exp(logits - jnp.max(logits, axis=0, keepdims=True))
    slots_ref[...] = slots
    gates_ref[...] = raised / jnp.sum(raised, axis=0, keepdims=True)
    tok_count = slots.shape[1]
    order = lax.broadcasted_iota(jnp.int32, (SLOTS, tok_count), 0).astype(jnp.float32)
    parts = []
    for k in order_of_pieces(mix_ref.shape[1] // SLOTS):
        expert = pl.ds((lax.axis_index("ctx") ^ k) // quarter_count, 1)
        parts.append(jnp.where(order == slots_ref[expert, :], gates_ref[expert, :], 0.0))
    total = jnp.concatenate(parts, axis=0).T
    for part in range(TERMS):
        term = total.astype(jnp.bfloat16)
        mix_ref[pl.ds(part * tok_count, tok_count), :] = term
        total = total - term.astype(jnp.float32)


def gate_mix(quarter_count, halves, router, count):
    tok_count = LANES
    held = pltpu.VMEM((router.shape[0], tok_count), jnp.float32)
    return pl.pallas_call(
        functools.partial(mix_kernel, quarter_count),
        in_specs=[WHOLE] * 3,
        out_specs=WHOLE,
        out_shape=jax.ShapeDtypeStruct((TERMS * tok_count, count * SLOTS), jnp.bfloat16),
        scratch_shapes=[held, held],
        compiler_params=pltpu.CompilerParams(vmem_limit_bytes=16 * MIB),
        name="gate_mix",
    )(*halves, router)


def combine_kernel(mix_ref, *refs):
    pieces, out_ref = refs[:-1], refs[-1]
    tok_count, model_width = out_ref.shape
    step = min(model_width, 512)
    spare = jnp.zeros((SLOTS - MOST, step), jnp.float32)
    for start in range(0, model_width, step):
        cols = pl.ds(start, step)
        rows = []
        for piece in pieces:
            rows += [piece[:, cols].astype(jnp.float32), spare]
        rows = jnp.concatenate(rows, axis=0).astype(jnp.bfloat16)
        product = jnp.dot(mix_ref[...], rows, preferred_element_type=jnp.float32)
        total = product[-tok_count:]
        for part in range(TERMS - 2, -1, -1):
            total = product[part * tok_count : (part + 1) * tok_count] + total
        out_ref[:, cols] = total.astype(jnp.bfloat16)


def combine(mix, pieces):
    tok_count = mix.shape[0] // TERMS
    model_width = pieces[0].shape[1]
    return pl.pallas_call(
        combine_kernel,
        in_specs=[WHOLE] * (1 + len(pieces)),
        out_specs=WHOLE,
        out_shape=jax.ShapeDtypeStruct((tok_count, model_width), jnp.bfloat16),
        compiler_params=pltpu.CompilerParams(vmem_limit_bytes=24 * MIB),
        name="combine",
    )(mix, *pieces)


def per_device(
    tokens, norm_gain, router_weight, routes, key_weight, value_weight, query_weight, output_weight
):
    tok_count, model_width = tokens.shape
    ctx_count = lax.axis_size("ctx")
    exp_count = lax.axis_size("exp")
    quarter_count = ctx_count // EXPERTS
    head_width = query_weight.shape[2]
    ranks = list(range(0, ctx_count, 2)) + list(range(1, ctx_count, 2))[::-1]
    forward = [(ranks[p], ranks[(p + 1) % ctx_count]) for p in range(ctx_count)]
    backward = [(b, a) for a, b in forward]
    sibling = [(e, 1 - e) for e in range(exp_count)]
    query_slab = query_weight[0]
    output_slab = output_weight[0]
    if quarter_count > 1:
        first = (lax.axis_index("ctx") % quarter_count) * head_width
        key_weight = lax.dynamic_slice_in_dim(key_weight, first, head_width, axis=1)
        value_weight = lax.dynamic_slice_in_dim(value_weight, first, head_width, axis=1)

    halves = norm_rows(tokens, norm_gain, routes)
    token_half = tok_count // 2
    steps = ctx_count // 2
    plan = [[0]] + [[-step, step] for step in range(1, steps)] + [[steps]]
    own, other, picked, queries, positions = [], [], [], [], []

    def send(parts):
        return [lax.ppermute(parts[0], "ctx", forward), lax.ppermute(parts[1], "ctx", backward)]

    def hand_over(panel):
        return lax.ppermute(panel, "exp", sibling)

    def tie(*arrays):
        return lax.optimization_barrier(arrays)

    blocks = halves
    lead = send([halves[0], halves[1]])
    rest = send([halves[1], halves[0]])
    for step in range(steps):
        keys, mark = project_keys(token_half, blocks, key_weight)
        following = [lead[0], rest[0], rest[1], lead[1]]
        if step == steps - 2:
            queries = project_queries(picked, query_slab, output_slab)
            picked = []
        if step < steps - 1:
            mark, *lead_next = tie(mark, *lead, *queries)
            queries = lead_next[2:]
            lead = send(lead_next[:2])
        panel, rows, position = project_values(token_half, blocks, plan[step], mark, keys, value_weight)
        if step < steps - 2:
            position, *rest_next = tie(position, *rest)
            rest = send(rest_next)
        own.append(panel)
        picked.append(rows)
        positions.append(position)
        if step < steps - 1:
            other.append(hand_over(panel))
        blocks = following
    queries = [*queries, *project_queries(picked, query_slab, output_slab)]
    own[-1], queries[-1], other[0], *blocks = tie(own[-1], queries[-1], other[0], *lead)
    other.append(hand_over(own[-1]))
    keys, mark = project_keys(token_half, blocks, key_weight)
    panel, rows, position = project_values(token_half, blocks, plan[-1], mark, keys, value_weight)
    own.append(panel)
    other.append(hand_over(panel))
    positions.append(position)
    queries = [*queries, *project_queries([rows], query_slab, output_slab)]
    held = arrange(ctx_count, plan, own, other, queries, positions)

    def swap(piece, k):
        return lax.ppermute(piece, "ctx", [(c, c ^ k) for c in range(ctx_count)])

    half, quarter = ctx_count // 2, ctx_count // 4
    far, mine = [], []
    for start, count in ((half, quarter), (half + quarter, quarter), (0, half)):
        pieces = attend((start // 2, count // 2), *held, output_slab)
        if start > 0:
            places, *pieces = tie(held[2], *pieces)
            held = [*held[:2], places]
            far.append([swap(piece, start + r) for r, piece in enumerate(pieces)])
        else:
            near = pieces
    *near, far[0][0] = tie(*near, far[0][0])
    near = [near[0]] + [swap(near[r], r) for r in range(1, half)]

    mix = gate_mix(quarter_count, halves, router_weight.T, ctx_count)
    pieces = [*near, *far[0], *far[1]]
    return combine(mix, [pieces[k] for k in order_of_pieces(ctx_count)])


def solution(mesh):
    in_specs = (
        P(("groups", "ctx", "exp"), None),
        P(),
        P(),
        P(("groups", "ctx", "exp"), None),
        P(),
        P(),
        P("ctx", None, None),
        P("ctx", None, None),
    )
    out_specs = P(("groups", "ctx", "exp"), None)
    return jax.shard_map(
        per_device, mesh=mesh, in_specs=in_specs, out_specs=out_specs, check_vma=False
    )
```

```python
import functools
import math

import jax
import jax.numpy as jnp
from jax import lax
from jax.experimental import pallas as pl
from jax.experimental.pallas import tpu as pltpu
from jax.sharding import PartitionSpec as P

HS = 128
EXPERTS = 8
MOST = 40
SLOTS = 48
MASKED = -1e30
LANES = 128
CODES = 16
TERMS = 2
MIB = 1 << 20
WHOLE = pl.BlockSpec(memory_space=pltpu.VMEM)


def ring_rank(place, count):
    place = lax.rem(place + 2 * count, count)
    return jnp.where(place < count // 2, 2 * place, 2 * (count - 1 - place) + 1)


def ring_place(rank, count):
    return jnp.where(rank % 2 == 0, rank // 2, count - 1 - rank // 2)


def ring_owner(offset):
    count = lax.axis_size("ctx")
    return ring_rank(ring_place(lax.axis_index("ctx"), count) + offset, count)


def norm_kernel(*refs):
    sources, top_ref, bottom_ref, *held, arrivals = refs[:3], *refs[3:]
    copies = [
        pltpu.make_async_copy(source, target, arrivals.at[i])
        for i, (source, target) in enumerate(zip(sources, held))
    ]
    for copy in copies:
        copy.start()
    for copy in copies:
        copy.wait()
    tokens_ref, gain_ref, routes_ref = held
    floats = tokens_ref[...].astype(jnp.float32)
    count, width = floats.shape
    factor = lax.rsqrt(jnp.mean(floats * floats, axis=1, keepdims=True) + 1e-06)
    normed = (floats * factor * gain_ref[...]).astype(jnp.bfloat16)
    expert = lax.broadcasted_iota(jnp.int32, (CODES, count), 0)
    named = (expert == routes_ref[0:1, :]) | (expert == routes_ref[1:2, :])
    before = lax.broadcasted_iota(jnp.int32, (count, count), 0) < lax.broadcasted_iota(
        jnp.int32, (count, count), 1
    )
    rank = jnp.dot(
        named.astype(jnp.bfloat16),
        before.astype(jnp.bfloat16),
        preferred_element_type=jnp.float32,
    )
    codes = jnp.where(named, rank, -1.0).astype(jnp.bfloat16)
    half = count // 2
    for ref, first in ((top_ref, 0), (bottom_ref, half)):
        for c in range(width // LANES):
            ref[pl.ds(c * half, half), :] = normed[
                first : first + half, c * LANES : (c + 1) * LANES
            ]
        ref[pl.ds(width // LANES * half, CODES), :] = codes


def message_rows(ref, half):
    tiles = (ref.shape[0] - CODES) // half
    return jnp.concatenate([ref[pl.ds(c * half, half), :] for c in range(tiles)], axis=1)


def message_codes(ref):
    return ref[pl.ds(ref.shape[0] - CODES, CODES), :].astype(jnp.float32)


def norm_rows(tokens, norm_gain, routes):
    count, width = tokens.shape
    half = jax.ShapeDtypeStruct((width // LANES * (count // 2) + CODES, LANES), jnp.bfloat16)
    operands = (tokens, norm_gain.reshape(1, -1), routes.T)
    return pl.pallas_call(
        norm_kernel,
        in_specs=[pl.BlockSpec(memory_space=pltpu.HBM)] * 3,
        out_specs=[WHOLE] * 2,
        out_shape=[half, half],
        scratch_shapes=[pltpu.VMEM(x.shape, x.dtype) for x in operands]
        + [pltpu.SemaphoreType.DMA((3,))],
        compiler_params=pltpu.CompilerParams(vmem_limit_bytes=60 * MIB),
        name="norm_rows",
    )(*operands)


def column_parts(ref):
    step = min(ref.shape[1], 256)
    return [pl.ds(start, step) for start in range(0, ref.shape[1], step)]


def keys_kernel(half, count, *refs):
    blocks = refs[:count]
    weight_ref, panel_ref, mark_ref = refs[count:]
    rows = jnp.concatenate([message_rows(block, half) for block in blocks], axis=0)
    for cols in column_parts(weight_ref):
        product = jnp.dot(rows, weight_ref[:, cols], preferred_element_type=jnp.float32)
        panel_ref[:, cols] = product.astype(jnp.bfloat16)
    mark_ref[...] = product[:8, :LANES]


def project_keys(half, blocks, key_weight):
    row_count = half * len(blocks)
    width = key_weight.shape[1]
    return pl.pallas_call(
        functools.partial(keys_kernel, half, len(blocks)),
        in_specs=[WHOLE] * (len(blocks) + 1),
        out_specs=[WHOLE] * 2,
        out_shape=[
            jax.ShapeDtypeStruct((row_count, width), jnp.bfloat16),
            jax.ShapeDtypeStruct((8, LANES), jnp.float32),
        ],
        compiler_params=pltpu.CompilerParams(vmem_limit_bytes=12 * MIB),
        name="project_keys",
    )(*blocks, key_weight)


def values_kernel(half, offsets, count, experts, mark_ref, keys_ref, *refs):
    blocks = refs[:count]
    value_ref, panel_ref, picked_ref, pos_ref = refs[count:]
    rows = jnp.concatenate([message_rows(block, half) for block in blocks], axis=0)
    tok_count = 2 * half
    expert = lax.axis_index("ctx") // (lax.axis_size("ctx") // experts)
    number = lax.broadcasted_iota(jnp.int32, (tok_count, LANES), 0).astype(jnp.bfloat16)
    for g, offset in enumerate(offsets):
        part = slice(g * tok_count, (g + 1) * tok_count)
        codes = message_codes(blocks[2 * g])
        mine = lax.broadcasted_iota(jnp.int32, codes.shape, 0) == expert
        slot = jnp.sum(jnp.where(mine, codes, 0.0), axis=0, keepdims=True)
        order = lax.broadcasted_iota(jnp.int32, (SLOTS, tok_count), 0).astype(jnp.float32)
        chosen = (order == slot).astype(jnp.bfloat16)
        picked_ref[g] = jnp.dot(
            chosen, rows[part], preferred_element_type=jnp.float32
        ).astype(jnp.bfloat16)
        start = (ring_owner(offset) * lax.axis_size("exp") + lax.axis_index("exp")) * tok_count
        pos_ref[g] = jnp.dot(
            chosen, number, preferred_element_type=jnp.float32
        ) + start.astype(jnp.float32)
    panel_ref[0] = keys_ref[...]
    for cols in column_parts(value_ref):
        panel_ref[1, :, cols] = jnp.dot(
            rows, value_ref[:, cols], preferred_element_type=jnp.float32
        ).astype(jnp.bfloat16)


def project_values(half, blocks, offsets, mark, keys, value_weight):
    row_count = half * len(blocks)
    model_width, width = value_weight.shape
    owners = len(offsets)
    return pl.pallas_call(
        functools.partial(values_kernel, half, offsets, len(blocks), EXPERTS),
        in_specs=[WHOLE] * (len(blocks) + 3),
        out_specs=[WHOLE] * 3,
        out_shape=[
            jax.ShapeDtypeStruct((2, row_count, width), jnp.bfloat16),
            jax.ShapeDtypeStruct((owners, SLOTS, model_width), jnp.bfloat16),
            jax.ShapeDtypeStruct((owners, SLOTS, LANES), jnp.float32),
        ],
        compiler_params=pltpu.CompilerParams(vmem_limit_bytes=12 * MIB),
        name="project_values",
    )(mark, keys, *blocks, value_weight)


def queries_kernel(*refs):
    count = len(refs) // 2 - 1
    picked, weight_ref, outs = refs[:count], refs[count], refs[count + 2 :]
    rows = jnp.concatenate([ref[g] for ref in picked for g in range(ref.shape[0])], axis=0)
    places = [(ref, g) for ref in outs for g in range(ref.shape[0])]
    for cols in column_parts(weight_ref):
        product = jnp.dot(rows, weight_ref[:, cols], preferred_element_type=jnp.float32)
        for i, (ref, g) in enumerate(places):
            ref[g, :, cols] = product[i * SLOTS : (i + 1) * SLOTS].astype(jnp.bfloat16)


def project_queries(picked, query_slab, next_slab):
    model_width, width = query_slab.shape
    owners = sum(rows.shape[0] for rows in picked)
    held = 4 * model_width * width + owners * SLOTS * (4 * model_width + 4 * width)
    return pl.pallas_call(
        queries_kernel,
        in_specs=[WHOLE] * (len(picked) + 2),
        out_specs=[WHOLE] * len(picked),
        out_shape=[
            jax.ShapeDtypeStruct((rows.shape[0], SLOTS, width), jnp.bfloat16) for rows in picked
        ],
        compiler_params=pltpu.CompilerParams(vmem_limit_bytes=held + 6 * MIB),
        name="project_queries",
    )(*picked, query_slab, next_slab)


def arrange_kernel(plan, *refs):
    count = len(plan)
    own_refs, other_refs, query_refs, pos_refs = (refs[k * count : (k + 1) * count] for k in range(4))
    panel_ref, queries_ref, places_ref = refs[4 * count :]
    exp_count = 2
    side = lax.axis_index("exp")
    tok_count = panel_ref.shape[2]
    for offsets, own_ref, other_ref, query_ref, pos_ref in zip(
        plan, own_refs, other_refs, query_refs, pos_refs
    ):
        for g, offset in enumerate(offsets):
            owner = ring_owner(offset)
            part = pl.ds(g * tok_count, tok_count)
            for which in range(2):
                panel_ref[which, owner * exp_count + side] = own_ref[which, part]
                panel_ref[which, owner * exp_count + 1 - side] = other_ref[which, part]
            queries_ref[owner] = query_ref[g].astype(jnp.float32)[:MOST]
            places_ref[owner] = pos_ref[g, :MOST]


def arrange(owners, plan, own, other, queries, positions):
    width = own[0].shape[2]
    tok_count = own[0].shape[1] // len(plan[0])
    shapes = [
        jax.ShapeDtypeStruct((2, 2 * owners, tok_count, width), jnp.bfloat16),
        jax.ShapeDtypeStruct((owners, MOST, width), jnp.float32),
        jax.ShapeDtypeStruct((owners, MOST, LANES), jnp.float32),
    ]
    operands = (*own, *other, *queries, *positions)
    return pl.pallas_call(
        functools.partial(arrange_kernel, plan),
        in_specs=[WHOLE] * len(operands),
        out_specs=[WHOLE] * 3,
        out_shape=shapes,
        compiler_params=pltpu.CompilerParams(
            vmem_limit_bytes=8 * MIB
        ),
        name="arrange",
    )(*operands)


def attend_kernel(lots, heads, panel_ref, queries_ref, places_ref, weight_ref, *refs):
    outs, (attended, scores, weights) = refs[:-3], refs[-3:]
    first, count = lots
    blocks, tok_count, width = panel_ref.shape[1:]
    rate = math.log2(math.e) / math.sqrt(HS)
    rank = lax.axis_index("ctx")
    tiles = blocks // 4
    tile = 2 * MOST
    parts = 4
    span = blocks * tok_count // parts
    per_span = blocks // parts
    passes = width // (heads * HS)

    def serve(part_id, number, lot, lanes):
        reach = (part_id + 1) * span
        pair = pl.ds(2 * number, 2)
        spots = places_ref[pair].reshape(tile, LANES)
        for h in range(heads):
            held = queries_ref[pair, :, lanes[h]].reshape(tile, HS).astype(jnp.bfloat16)
            for j in range(part_id + 1):
                key_part = panel_ref[0, per_span * j : per_span * (j + 1), :, lanes[h]]
                scores[h, :, pl.ds(j * span, span)] = lax.dot_general(
                    held,
                    key_part.reshape(span, HS),
                    (((1,), (1,)), ((), ())),
                    preferred_element_type=jnp.float32,
                )
        for h in range(heads):
            for sub in range(0, tile, 16):
                rows = pl.ds(sub, 16)
                part = scores[h, rows, pl.ds(0, reach)]
                last = part[:, reach - span :]
                key_index = lax.broadcasted_iota(jnp.int32, last.shape, 1) + (reach - span)
                spot = spots[sub : sub + 16, 0:1]
                last = jnp.where(key_index.astype(jnp.float32) <= spot, last, MASKED)
                if part_id > 0:
                    part = jnp.concatenate([part[:, : reach - span], last], axis=1)
                else:
                    part = last
                peak = jnp.max(part, axis=1, keepdims=True)
                raised = jnp.exp2((part - peak) * rate)
                total = jnp.sum(raised, axis=1, keepdims=True)
                weights[h, rows, pl.ds(0, reach)] = (raised * (1.0 / total)).astype(jnp.bfloat16)
        for h in range(heads):
            total = None
            for j in range(part_id + 1):
                value_part = panel_ref[1, per_span * j : per_span * (j + 1), :, lanes[h]]
                product = jnp.dot(
                    weights[h, :, pl.ds(j * span, span)],
                    value_part.reshape(span, HS),
                    preferred_element_type=jnp.float32,
                )
                total = product if total is None else total + product
            spare = jnp.zeros((SLOTS - MOST, HS), jnp.float32)
            for side in range(2):
                rows = jnp.concatenate([total[side * MOST : (side + 1) * MOST], spare], axis=0)
                attended[2 * lot + (side ^ (rank % 2)), :, lanes[h]] = rows.astype(jnp.bfloat16)

    def one(at, carry):
        lot, now = at // passes, at % passes
        number = (rank // 2) ^ (first + lot)
        lanes = [pl.ds(pl.multiple_of((now * heads + h) * HS, HS), HS) for h in range(heads)]
        for part_id in range(parts):
            pl.when(number // (tiles // parts) == part_id)(
                functools.partial(serve, part_id, number, lot, lanes)
            )
        return carry

    lax.fori_loop(0, count * passes, one, 0)
    rows = attended[...].reshape(2 * count * SLOTS, width)
    for cols in column_parts(weight_ref):
        product = jnp.dot(rows, weight_ref[:, cols], preferred_element_type=jnp.float32)
        for k, out_ref in enumerate(outs):
            out_ref[:, cols] = product[k * SLOTS : k * SLOTS + MOST].astype(jnp.bfloat16)


def attend(lots, panel, queries, places, output_slab):
    first, count = lots
    _, blocks, tok_count, width = panel.shape
    length = blocks * tok_count
    heads = min(8, width // HS) if blocks <= 16 else 1
    model_width = output_slab.shape[1]
    held = heads * 2 * SLOTS * length * 6 + 2 * length * width * 2 + width * model_width * 2
    held += 2 * count * SLOTS * (model_width * 8 + width * 2)
    return pl.pallas_call(
        functools.partial(attend_kernel, lots, heads),
        in_specs=[WHOLE] * 4,
        out_specs=[WHOLE] * (2 * count),
        out_shape=[jax.ShapeDtypeStruct((MOST, model_width), jnp.bfloat16)] * (2 * count),
        scratch_shapes=[
            pltpu.VMEM((2 * count, SLOTS, width), jnp.bfloat16),
            pltpu.VMEM((heads, 2 * MOST, length), jnp.float32),
            pltpu.VMEM((heads, 2 * MOST, length), jnp.bfloat16),
        ],
        compiler_params=pltpu.CompilerParams(vmem_limit_bytes=held * 9 // 8 + 4 * MIB),
        cost_estimate=pl.CostEstimate(
            flops=count * 2 * SLOTS * width * (4 * length + 2 * model_width),
            bytes_accessed=4 * length * width,
            transcendentals=count * 2 * SLOTS * length * width // HS,
        ),
        name="attend",
    )(panel, queries, places, output_slab)


def piece_groups(count):
    return [0, *range(count // 2, count)], list(range(count // 2 - 1, 0, -1))


def mix_kernel(quarter_count, top_ref, bottom_ref, router_ref, *refs):
    *mix_refs, slots_ref, gates_ref = refs
    half = LANES // 2
    rows = jnp.concatenate([message_rows(ref, half) for ref in (top_ref, bottom_ref)], axis=0)
    rest, terms = router_ref[...], []
    for _ in range(3):
        terms.append(rest.astype(jnp.bfloat16).astype(jnp.float32))
        rest = rest - terms[-1]
    experts = rest.shape[0]
    router = jnp.concatenate([*terms, jnp.zeros_like(rest)], axis=0).astype(jnp.bfloat16)
    products = lax.dot_general(
        router, rows, (((1,), (1,)), ((), ())), preferred_element_type=jnp.float32
    )
    logits = products[:experts] + (
        products[experts : 2 * experts] + products[2 * experts : 3 * experts]
    )
    slots = message_codes(top_ref)[:experts]
    logits = jnp.where(slots >= 0, logits, -jnp.inf)
    raised = jnp.exp(logits - jnp.max(logits, axis=0, keepdims=True))
    slots_ref[...] = slots
    gates_ref[...] = raised / jnp.sum(raised, axis=0, keepdims=True)
    tok_count = slots.shape[1]
    order = lax.broadcasted_iota(jnp.int32, (SLOTS, tok_count), 0).astype(jnp.float32)
    for mix_ref, group in zip(mix_refs, piece_groups(sum(r.shape[1] for r in mix_refs) // SLOTS)):
        parts = []
        for k in group:
            expert = pl.ds((lax.axis_index("ctx") ^ k) // quarter_count, 1)
            parts.append(jnp.where(order == slots_ref[expert, :], gates_ref[expert, :], 0.0))
        total = jnp.concatenate(parts, axis=0).T
        for part in range(TERMS):
            term = total.astype(jnp.bfloat16)
            mix_ref[pl.ds(part * tok_count, tok_count), :] = term
            total = total - term.astype(jnp.float32)


def gate_mix(quarter_count, halves, router, count):
    tok_count = LANES
    held = pltpu.VMEM((router.shape[0], tok_count), jnp.float32)
    return pl.pallas_call(
        functools.partial(mix_kernel, quarter_count),
        in_specs=[WHOLE] * 3,
        out_specs=[WHOLE] * 2,
        out_shape=[
            jax.ShapeDtypeStruct((TERMS * tok_count, len(group) * SLOTS), jnp.bfloat16)
            for group in piece_groups(count)
        ],
        scratch_shapes=[held, held],
        compiler_params=pltpu.CompilerParams(vmem_limit_bytes=16 * MIB),
        name="gate_mix",
    )(*halves, router)


def combine_kernel(ahead_count, mix_ref, *refs):
    ahead, pieces, out_ref = refs[:ahead_count], refs[ahead_count:-1], refs[-1]
    tok_count, model_width = out_ref.shape
    step = min(model_width, 512)
    spare = jnp.zeros((SLOTS - MOST, step), jnp.float32)
    for start in range(0, model_width, step):
        cols = pl.ds(start, step)
        rows = []
        for piece in pieces:
            rows += [piece[:, cols].astype(jnp.float32), spare]
        rows = jnp.concatenate(rows, axis=0).astype(jnp.bfloat16)
        product = jnp.dot(mix_ref[...], rows, preferred_element_type=jnp.float32)
        total = product[-tok_count:]
        for part in range(TERMS - 2, -1, -1):
            total = product[part * tok_count : (part + 1) * tok_count] + total
        for ref in ahead:
            total = total + ref[:, cols]
        out_ref[:, cols] = total.astype(out_ref.dtype)


def combine(mix, pieces, ahead, dtype):
    tok_count = mix.shape[0] // TERMS
    model_width = pieces[0].shape[1]
    return pl.pallas_call(
        functools.partial(combine_kernel, len(ahead)),
        in_specs=[WHOLE] * (1 + len(ahead) + len(pieces)),
        out_specs=WHOLE,
        out_shape=jax.ShapeDtypeStruct((tok_count, model_width), dtype),
        compiler_params=pltpu.CompilerParams(vmem_limit_bytes=24 * MIB),
        name="combine",
    )(mix, *ahead, *pieces)


def per_device(
    tokens, norm_gain, router_weight, routes, key_weight, value_weight, query_weight, output_weight
):
    tok_count, model_width = tokens.shape
    ctx_count = lax.axis_size("ctx")
    exp_count = lax.axis_size("exp")
    quarter_count = ctx_count // EXPERTS
    head_width = query_weight.shape[2]
    ranks = list(range(0, ctx_count, 2)) + list(range(1, ctx_count, 2))[::-1]
    forward = [(ranks[p], ranks[(p + 1) % ctx_count]) for p in range(ctx_count)]
    backward = [(b, a) for a, b in forward]
    sibling = [(e, 1 - e) for e in range(exp_count)]
    query_slab = query_weight[0]
    output_slab = output_weight[0]
    if quarter_count > 1:
        first = (lax.axis_index("ctx") % quarter_count) * head_width
        key_weight = lax.dynamic_slice_in_dim(key_weight, first, head_width, axis=1)
        value_weight = lax.dynamic_slice_in_dim(value_weight, first, head_width, axis=1)

    halves = norm_rows(tokens, norm_gain, routes)
    token_half = tok_count // 2
    steps = ctx_count // 2
    plan = [[0]] + [[-step, step] for step in range(1, steps)] + [[steps]]
    own, other, picked, queries, positions = [], [], [], [], []

    def send(parts):
        return [lax.ppermute(parts[0], "ctx", forward), lax.ppermute(parts[1], "ctx", backward)]

    def hand_over(panel):
        return lax.ppermute(panel, "exp", sibling)

    def tie(*arrays):
        return lax.optimization_barrier(arrays)

    blocks = halves
    lead = send([halves[0], halves[1]])
    rest = send([halves[1], halves[0]])
    for step in range(steps):
        keys, mark = project_keys(token_half, blocks, key_weight)
        following = [lead[0], rest[0], rest[1], lead[1]]
        if step == steps - 2:
            queries = project_queries(picked, query_slab, output_slab)
            picked = []
        if step < steps - 1:
            mark, *lead_next = tie(mark, *lead, *queries)
            queries = lead_next[2:]
            lead = send(lead_next[:2])
        panel, rows, position = project_values(token_half, blocks, plan[step], mark, keys, value_weight)
        if step < steps - 2:
            position, *rest_next = tie(position, *rest)
            rest = send(rest_next)
        own.append(panel)
        picked.append(rows)
        positions.append(position)
        if step < steps - 1:
            other.append(hand_over(panel))
        blocks = following
    queries = [*queries, *project_queries(picked, query_slab, output_slab)]
    own[-1], queries[-1], other[0], *blocks = tie(own[-1], queries[-1], other[0], *lead)
    other.append(hand_over(own[-1]))
    keys, mark = project_keys(token_half, blocks, key_weight)
    panel, rows, position = project_values(token_half, blocks, plan[-1], mark, keys, value_weight)
    own.append(panel)
    other.append(hand_over(panel))
    positions.append(position)
    queries = [*queries, *project_queries([rows], query_slab, output_slab)]
    held = arrange(ctx_count, plan, own, other, queries, positions)

    def swap(piece, k):
        return lax.ppermute(piece, "ctx", [(c, c ^ k) for c in range(ctx_count)])

    half, quarter = ctx_count // 2, ctx_count // 4
    far, mine = [], []
    for start, count in ((half, quarter), (half + quarter, quarter), (0, half)):
        pieces = attend((start // 2, count // 2), *held, output_slab)
        if start > 0:
            places, *pieces = tie(held[2], *pieces)
            held = [*held[:2], places]
            far.append([swap(piece, start + r) for r, piece in enumerate(pieces)])
        else:
            near = pieces
    *near, far[0][0] = tie(*near, far[0][0])
    near = [near[0]] + [swap(near[r], r) for r in range(1, half)]

    pieces = [*near, *far[0], *far[1]]
    early, late = piece_groups(ctx_count)
    early_mix, late_mix = gate_mix(quarter_count, halves, router_weight.T, ctx_count)
    ahead = combine(early_mix, [pieces[k] for k in early], [], jnp.float32)
    return combine(late_mix, [pieces[k] for k in late], [ahead], jnp.bfloat16)


def solution(mesh):
    in_specs = (
        P(("groups", "ctx", "exp"), None),
        P(),
        P(),
        P(("groups", "ctx", "exp"), None),
        P(),
        P(),
        P("ctx", None, None),
        P("ctx", None, None),
    )
    out_specs = P(("groups", "ctx", "exp"), None)
    return jax.shard_map(
        per_device, mesh=mesh, in_specs=in_specs, out_specs=out_specs, check_vma=False
    )
```

```python
import functools
import math

import jax
import jax.numpy as jnp
from jax import lax
from jax.experimental import pallas as pl
from jax.experimental.pallas import tpu as pltpu
from jax.sharding import PartitionSpec as P

HS = 128
EXPERTS = 8
MOST = 40
SLOTS = 48
MASKED = -1e30
LANES = 128
CODES = 16
TERMS = 2
MIB = 1 << 20
WHOLE = pl.BlockSpec(memory_space=pltpu.VMEM)


def ring_rank(place, count):
    place = lax.rem(place + 2 * count, count)
    return jnp.where(place < count // 2, 2 * place, 2 * (count - 1 - place) + 1)


def ring_place(rank, count):
    return jnp.where(rank % 2 == 0, rank // 2, count - 1 - rank // 2)


def ring_owner(offset):
    count = lax.axis_size("ctx")
    return ring_rank(ring_place(lax.axis_index("ctx"), count) + offset, count)


def norm_kernel(*refs):
    sources, top_ref, bottom_ref, *held, arrivals = refs[:3], *refs[3:]
    copies = [
        pltpu.make_async_copy(source, target, arrivals.at[i])
        for i, (source, target) in enumerate(zip(sources, held))
    ]
    for copy in copies:
        copy.start()
    for copy in copies:
        copy.wait()
    tokens_ref, gain_ref, routes_ref = held
    floats = tokens_ref[...].astype(jnp.float32)
    count, width = floats.shape
    factor = lax.rsqrt(jnp.mean(floats * floats, axis=1, keepdims=True) + 1e-06)
    normed = (floats * factor * gain_ref[...]).astype(jnp.bfloat16)
    expert = lax.broadcasted_iota(jnp.int32, (CODES, count), 0)
    named = (expert == routes_ref[0:1, :]) | (expert == routes_ref[1:2, :])
    before = lax.broadcasted_iota(jnp.int32, (count, count), 0) < lax.broadcasted_iota(
        jnp.int32, (count, count), 1
    )
    rank = jnp.dot(
        named.astype(jnp.bfloat16),
        before.astype(jnp.bfloat16),
        preferred_element_type=jnp.float32,
    )
    codes = jnp.where(named, rank, -1.0).astype(jnp.bfloat16)
    half = count // 2
    for ref, first in ((top_ref, 0), (bottom_ref, half)):
        for c in range(width // LANES):
            ref[pl.ds(c * half, half), :] = normed[
                first : first + half, c * LANES : (c + 1) * LANES
            ]
        ref[pl.ds(width // LANES * half, CODES), :] = codes


def message_rows(ref, half):
    tiles = (ref.shape[0] - CODES) // half
    return jnp.concatenate([ref[pl.ds(c * half, half), :] for c in range(tiles)], axis=1)


def message_codes(ref):
    return ref[pl.ds(ref.shape[0] - CODES, CODES), :].astype(jnp.float32)


def norm_rows(tokens, norm_gain, routes):
    count, width = tokens.shape
    half = jax.ShapeDtypeStruct((width // LANES * (count // 2) + CODES, LANES), jnp.bfloat16)
    operands = (tokens, norm_gain.reshape(1, -1), routes.T)
    return pl.pallas_call(
        norm_kernel,
        in_specs=[pl.BlockSpec(memory_space=pltpu.HBM)] * 3,
        out_specs=[WHOLE] * 2,
        out_shape=[half, half],
        scratch_shapes=[pltpu.VMEM(x.shape, x.dtype) for x in operands]
        + [pltpu.SemaphoreType.DMA((3,))],
        compiler_params=pltpu.CompilerParams(vmem_limit_bytes=60 * MIB),
        name="norm_rows",
    )(*operands)


def column_parts(ref):
    step = min(ref.shape[1], 256)
    return [pl.ds(start, step) for start in range(0, ref.shape[1], step)]


def keys_kernel(half, count, *refs):
    blocks = refs[:count]
    weight_ref, panel_ref, mark_ref = refs[count:]
    rows = jnp.concatenate([message_rows(block, half) for block in blocks], axis=0)
    for cols in column_parts(weight_ref):
        product = jnp.dot(rows, weight_ref[:, cols], preferred_element_type=jnp.float32)
        panel_ref[:, cols] = product.astype(jnp.bfloat16)
    mark_ref[...] = product[:8, :LANES]


def project_keys(half, blocks, key_weight):
    row_count = half * len(blocks)
    width = key_weight.shape[1]
    return pl.pallas_call(
        functools.partial(keys_kernel, half, len(blocks)),
        in_specs=[WHOLE] * (len(blocks) + 1),
        out_specs=[WHOLE] * 2,
        out_shape=[
            jax.ShapeDtypeStruct((row_count, width), jnp.bfloat16),
            jax.ShapeDtypeStruct((8, LANES), jnp.float32),
        ],
        compiler_params=pltpu.CompilerParams(vmem_limit_bytes=12 * MIB),
        name="project_keys",
    )(*blocks, key_weight)


def values_kernel(half, offsets, count, experts, mark_ref, keys_ref, *refs):
    blocks = refs[:count]
    value_ref, panel_ref, picked_ref, pos_ref = refs[count:]
    rows = jnp.concatenate([message_rows(block, half) for block in blocks], axis=0)
    tok_count = 2 * half
    expert = lax.axis_index("ctx") // (lax.axis_size("ctx") // experts)
    number = lax.broadcasted_iota(jnp.int32, (tok_count, LANES), 0).astype(jnp.bfloat16)
    for g, offset in enumerate(offsets):
        part = slice(g * tok_count, (g + 1) * tok_count)
        codes = message_codes(blocks[2 * g])
        mine = lax.broadcasted_iota(jnp.int32, codes.shape, 0) == expert
        slot = jnp.sum(jnp.where(mine, codes, 0.0), axis=0, keepdims=True)
        order = lax.broadcasted_iota(jnp.int32, (SLOTS, tok_count), 0).astype(jnp.float32)
        chosen = (order == slot).astype(jnp.bfloat16)
        picked_ref[g] = jnp.dot(
            chosen, rows[part], preferred_element_type=jnp.float32
        ).astype(jnp.bfloat16)
        start = (ring_owner(offset) * lax.axis_size("exp") + lax.axis_index("exp")) * tok_count
        pos_ref[g] = jnp.dot(
            chosen, number, preferred_element_type=jnp.float32
        ) + start.astype(jnp.float32)
    panel_ref[0] = keys_ref[...]
    for cols in column_parts(value_ref):
        panel_ref[1, :, cols] = jnp.dot(
            rows, value_ref[:, cols], preferred_element_type=jnp.float32
        ).astype(jnp.bfloat16)


def project_values(half, blocks, offsets, mark, keys, value_weight):
    row_count = half * len(blocks)
    model_width, width = value_weight.shape
    owners = len(offsets)
    return pl.pallas_call(
        functools.partial(values_kernel, half, offsets, len(blocks), EXPERTS),
        in_specs=[WHOLE] * (len(blocks) + 3),
        out_specs=[WHOLE] * 3,
        out_shape=[
            jax.ShapeDtypeStruct((2, row_count, width), jnp.bfloat16),
            jax.ShapeDtypeStruct((owners, SLOTS, model_width), jnp.bfloat16),
            jax.ShapeDtypeStruct((owners, SLOTS, LANES), jnp.float32),
        ],
        compiler_params=pltpu.CompilerParams(vmem_limit_bytes=12 * MIB),
        name="project_values",
    )(mark, keys, *blocks, value_weight)


def queries_kernel(*refs):
    count = len(refs) // 2 - 1
    picked, weight_ref, outs = refs[:count], refs[count], refs[count + 2 :]
    rows = jnp.concatenate([ref[g] for ref in picked for g in range(ref.shape[0])], axis=0)
    places = [(ref, g) for ref in outs for g in range(ref.shape[0])]
    for cols in column_parts(weight_ref):
        product = jnp.dot(rows, weight_ref[:, cols], preferred_element_type=jnp.float32)
        for i, (ref, g) in enumerate(places):
            ref[g, :, cols] = product[i * SLOTS : (i + 1) * SLOTS].astype(jnp.bfloat16)


def project_queries(picked, query_slab, next_slab):
    model_width, width = query_slab.shape
    owners = sum(rows.shape[0] for rows in picked)
    held = 4 * model_width * width + owners * SLOTS * (4 * model_width + 4 * width)
    return pl.pallas_call(
        queries_kernel,
        in_specs=[WHOLE] * (len(picked) + 2),
        out_specs=[WHOLE] * len(picked),
        out_shape=[
            jax.ShapeDtypeStruct((rows.shape[0], SLOTS, width), jnp.bfloat16) for rows in picked
        ],
        compiler_params=pltpu.CompilerParams(vmem_limit_bytes=held + 6 * MIB),
        name="project_queries",
    )(*picked, query_slab, next_slab)


def arrange_kernel(plan, *refs):
    count = len(plan)
    own_refs, other_refs, query_refs, pos_refs = (refs[k * count : (k + 1) * count] for k in range(4))
    panel_ref, queries_ref, places_ref = refs[4 * count :]
    exp_count = 2
    side = lax.axis_index("exp")
    tok_count = panel_ref.shape[2]
    for offsets, own_ref, other_ref, query_ref, pos_ref in zip(
        plan, own_refs, other_refs, query_refs, pos_refs
    ):
        for g, offset in enumerate(offsets):
            owner = ring_owner(offset)
            part = pl.ds(g * tok_count, tok_count)
            for which in range(2):
                panel_ref[which, owner * exp_count + side] = own_ref[which, part]
                panel_ref[which, owner * exp_count + 1 - side] = other_ref[which, part]
            queries_ref[owner] = query_ref[g].astype(jnp.float32)[:MOST]
            places_ref[owner] = pos_ref[g, :MOST]


def arrange(owners, plan, own, other, queries, positions):
    width = own[0].shape[2]
    tok_count = own[0].shape[1] // len(plan[0])
    shapes = [
        jax.ShapeDtypeStruct((2, 2 * owners, tok_count, width), jnp.bfloat16),
        jax.ShapeDtypeStruct((owners, MOST, width), jnp.float32),
        jax.ShapeDtypeStruct((owners, MOST, LANES), jnp.float32),
    ]
    operands = (*own, *other, *queries, *positions)
    return pl.pallas_call(
        functools.partial(arrange_kernel, plan),
        in_specs=[WHOLE] * len(operands),
        out_specs=[WHOLE] * 3,
        out_shape=shapes,
        compiler_params=pltpu.CompilerParams(
            vmem_limit_bytes=8 * MIB
        ),
        name="arrange",
    )(*operands)


def attend_kernel(lots, heads, panel_ref, queries_ref, places_ref, weight_ref, *refs):
    outs, (attended, scores, weights) = refs[:-3], refs[-3:]
    first, count = lots
    blocks, tok_count, width = panel_ref.shape[1:]
    rate = math.log2(math.e) / math.sqrt(HS)
    rank = lax.axis_index("ctx")
    tiles = blocks // 4
    tile = 2 * MOST
    parts = 4
    span = blocks * tok_count // parts
    per_span = blocks // parts
    passes = width // (heads * HS)

    def serve(part_id, number, lot, lanes):
        reach = (part_id + 1) * span
        pair = pl.ds(2 * number, 2)
        spots = places_ref[pair].reshape(tile, LANES)
        for h in range(heads):
            held = queries_ref[pair, :, lanes[h]].reshape(tile, HS).astype(jnp.bfloat16)
            for j in range(part_id + 1):
                key_part = panel_ref[0, per_span * j : per_span * (j + 1), :, lanes[h]]
                scores[h, :, pl.ds(j * span, span)] = lax.dot_general(
                    held,
                    key_part.reshape(span, HS),
                    (((1,), (1,)), ((), ())),
                    preferred_element_type=jnp.float32,
                )
        for h in range(heads):
            for sub in range(0, tile, 16):
                rows = pl.ds(sub, 16)
                part = scores[h, rows, pl.ds(0, reach)]
                last = part[:, reach - span :]
                key_index = lax.broadcasted_iota(jnp.int32, last.shape, 1) + (reach - span)
                spot = spots[sub : sub + 16, 0:1]
                last = jnp.where(key_index.astype(jnp.float32) <= spot, last, MASKED)
                if part_id > 0:
                    part = jnp.concatenate([part[:, : reach - span], last], axis=1)
                else:
                    part = last
                peak = jnp.max(part, axis=1, keepdims=True)
                raised = jnp.exp2((part - peak) * rate)
                total = jnp.sum(raised, axis=1, keepdims=True)
                weights[h, rows, pl.ds(0, reach)] = (raised * (1.0 / total)).astype(jnp.bfloat16)
        for h in range(heads):
            total = None
            for j in range(part_id + 1):
                value_part = panel_ref[1, per_span * j : per_span * (j + 1), :, lanes[h]]
                product = jnp.dot(
                    weights[h, :, pl.ds(j * span, span)],
                    value_part.reshape(span, HS),
                    preferred_element_type=jnp.float32,
                )
                total = product if total is None else total + product
            spare = jnp.zeros((SLOTS - MOST, HS), jnp.float32)
            for side in range(2):
                rows = jnp.concatenate([total[side * MOST : (side + 1) * MOST], spare], axis=0)
                attended[2 * lot + (side ^ (rank % 2)), :, lanes[h]] = rows.astype(jnp.bfloat16)

    def one(at, carry):
        lot, now = at // passes, at % passes
        number = (rank // 2) ^ (first + lot)
        lanes = [pl.ds(pl.multiple_of((now * heads + h) * HS, HS), HS) for h in range(heads)]
        for part_id in range(parts):
            pl.when(number // (tiles // parts) == part_id)(
                functools.partial(serve, part_id, number, lot, lanes)
            )
        return carry

    lax.fori_loop(0, count * passes, one, 0)
    rows = attended[...].reshape(2 * count * SLOTS, width)
    for cols in column_parts(weight_ref):
        product = jnp.dot(rows, weight_ref[:, cols], preferred_element_type=jnp.float32)
        for k, out_ref in enumerate(outs):
            out_ref[:, cols] = product[k * SLOTS : k * SLOTS + MOST].astype(jnp.bfloat16)


def attend(lots, panel, queries, places, output_slab):
    first, count = lots
    _, blocks, tok_count, width = panel.shape
    length = blocks * tok_count
    heads = min(8 if first == blocks // 8 else 4, width // HS) if blocks <= 16 else 1
    model_width = output_slab.shape[1]
    held = heads * 2 * SLOTS * length * 6 + 2 * length * width * 2 + width * model_width * 2
    held += 2 * count * SLOTS * (model_width * 8 + width * 2)
    return pl.pallas_call(
        functools.partial(attend_kernel, lots, heads),
        in_specs=[WHOLE] * 4,
        out_specs=[WHOLE] * (2 * count),
        out_shape=[jax.ShapeDtypeStruct((MOST, model_width), jnp.bfloat16)] * (2 * count),
        scratch_shapes=[
            pltpu.VMEM((2 * count, SLOTS, width), jnp.bfloat16),
            pltpu.VMEM((heads, 2 * MOST, length), jnp.float32),
            pltpu.VMEM((heads, 2 * MOST, length), jnp.bfloat16),
        ],
        compiler_params=pltpu.CompilerParams(vmem_limit_bytes=held * 9 // 8 + 4 * MIB),
        cost_estimate=pl.CostEstimate(
            flops=count * 2 * SLOTS * width * (4 * length + 2 * model_width),
            bytes_accessed=4 * length * width,
            transcendentals=count * 2 * SLOTS * length * width // HS,
        ),
        name="attend",
    )(panel, queries, places, output_slab)


def piece_groups(count):
    return [0, *range(count // 2, count)], list(range(count // 2 - 1, 0, -1))


def mix_kernel(quarter_count, top_ref, bottom_ref, router_ref, *refs):
    *mix_refs, slots_ref, gates_ref = refs
    half = LANES // 2
    rows = jnp.concatenate([message_rows(ref, half) for ref in (top_ref, bottom_ref)], axis=0)
    rest, terms = router_ref[...], []
    for _ in range(3):
        terms.append(rest.astype(jnp.bfloat16).astype(jnp.float32))
        rest = rest - terms[-1]
    experts = rest.shape[0]
    router = jnp.concatenate([*terms, jnp.zeros_like(rest)], axis=0).astype(jnp.bfloat16)
    products = lax.dot_general(
        router, rows, (((1,), (1,)), ((), ())), preferred_element_type=jnp.float32
    )
    logits = products[:experts] + (
        products[experts : 2 * experts] + products[2 * experts : 3 * experts]
    )
    slots = message_codes(top_ref)[:experts]
    logits = jnp.where(slots >= 0, logits, -jnp.inf)
    raised = jnp.exp(logits - jnp.max(logits, axis=0, keepdims=True))
    slots_ref[...] = slots
    gates_ref[...] = raised / jnp.sum(raised, axis=0, keepdims=True)
    tok_count = slots.shape[1]
    order = lax.broadcasted_iota(jnp.int32, (SLOTS, tok_count), 0).astype(jnp.float32)
    for mix_ref, group in zip(mix_refs, piece_groups(sum(r.shape[1] for r in mix_refs) // SLOTS)):
        parts = []
        for k in group:
            expert = pl.ds((lax.axis_index("ctx") ^ k) // quarter_count, 1)
            parts.append(jnp.where(order == slots_ref[expert, :], gates_ref[expert, :], 0.0))
        total = jnp.concatenate(parts, axis=0).T
        for part in range(TERMS):
            term = total.astype(jnp.bfloat16)
            mix_ref[pl.ds(part * tok_count, tok_count), :] = term
            total = total - term.astype(jnp.float32)


def gate_mix(quarter_count, halves, router, count):
    tok_count = LANES
    held = pltpu.VMEM((router.shape[0], tok_count), jnp.float32)
    return pl.pallas_call(
        functools.partial(mix_kernel, quarter_count),
        in_specs=[WHOLE] * 3,
        out_specs=[WHOLE] * 2,
        out_shape=[
            jax.ShapeDtypeStruct((TERMS * tok_count, len(group) * SLOTS), jnp.bfloat16)
            for group in piece_groups(count)
        ],
        scratch_shapes=[held, held],
        compiler_params=pltpu.CompilerParams(vmem_limit_bytes=16 * MIB),
        name="gate_mix",
    )(*halves, router)


def combine_kernel(ahead_count, mix_ref, *refs):
    *refs, out_ref, held, sent = refs
    ahead, pieces = refs[:ahead_count], refs[ahead_count:]
    tok_count, model_width = out_ref.shape
    copies = []
    step = min(model_width, 512)
    spare = jnp.zeros((SLOTS - MOST, step), jnp.float32)
    for start in range(0, model_width, step):
        cols = pl.ds(start, step)
        rows = []
        for piece in pieces:
            rows += [piece[:, cols].astype(jnp.float32), spare]
        rows = jnp.concatenate(rows, axis=0).astype(jnp.bfloat16)
        product = jnp.dot(mix_ref[...], rows, preferred_element_type=jnp.float32)
        total = product[-tok_count:]
        for part in range(TERMS - 2, -1, -1):
            total = product[part * tok_count : (part + 1) * tok_count] + total
        for ref in ahead:
            total = total + ref[:, cols]
        held[:, cols] = total.astype(held.dtype)
        copies.append(
            pltpu.make_async_copy(held.at[:, cols], out_ref.at[:, cols], sent.at[len(copies)])
        )
        copies[-1].start()
    for copy in copies:
        copy.wait()


def combine(mix, pieces, ahead, dtype):
    tok_count = mix.shape[0] // TERMS
    model_width = pieces[0].shape[1]
    return pl.pallas_call(
        functools.partial(combine_kernel, len(ahead)),
        in_specs=[WHOLE] * (1 + len(ahead) + len(pieces)),
        out_specs=pl.BlockSpec(memory_space=pl.ANY),
        out_shape=jax.ShapeDtypeStruct((tok_count, model_width), dtype),
        scratch_shapes=[
            pltpu.VMEM((tok_count, model_width), dtype),
            pltpu.SemaphoreType.DMA((-(-model_width // 512),)),
        ],
        compiler_params=pltpu.CompilerParams(vmem_limit_bytes=24 * MIB),
        name="combine",
    )(mix, *ahead, *pieces)


def per_device(
    tokens, norm_gain, router_weight, routes, key_weight, value_weight, query_weight, output_weight
):
    tok_count, model_width = tokens.shape
    ctx_count = lax.axis_size("ctx")
    exp_count = lax.axis_size("exp")
    quarter_count = ctx_count // EXPERTS
    head_width = query_weight.shape[2]
    ranks = list(range(0, ctx_count, 2)) + list(range(1, ctx_count, 2))[::-1]
    forward = [(ranks[p], ranks[(p + 1) % ctx_count]) for p in range(ctx_count)]
    backward = [(b, a) for a, b in forward]
    sibling = [(e, 1 - e) for e in range(exp_count)]
    query_slab = query_weight[0]
    output_slab = output_weight[0]
    if quarter_count > 1:
        first = (lax.axis_index("ctx") % quarter_count) * head_width
        key_weight = lax.dynamic_slice_in_dim(key_weight, first, head_width, axis=1)
        value_weight = lax.dynamic_slice_in_dim(value_weight, first, head_width, axis=1)

    halves = norm_rows(tokens, norm_gain, routes)
    token_half = tok_count // 2
    steps = ctx_count // 2
    plan = [[0]] + [[-step, step] for step in range(1, steps)] + [[steps]]
    own, other, picked, queries, positions = [], [], [], [], []

    def send(parts):
        return [lax.ppermute(parts[0], "ctx", forward), lax.ppermute(parts[1], "ctx", backward)]

    def hand_over(panel):
        return lax.ppermute(panel, "exp", sibling)

    def tie(*arrays):
        return lax.optimization_barrier(arrays)

    blocks = halves
    lead = send([halves[0], halves[1]])
    rest = send([halves[1], halves[0]])
    for step in range(steps):
        keys, mark = project_keys(token_half, blocks, key_weight)
        following = [lead[0], rest[0], rest[1], lead[1]]
        if step == steps - 2:
            queries = project_queries(picked, query_slab, output_slab)
            picked = []
        if step < steps - 1:
            mark, *lead_next = tie(mark, *lead, *queries)
            queries = lead_next[2:]
            lead = send(lead_next[:2])
        panel, rows, position = project_values(token_half, blocks, plan[step], mark, keys, value_weight)
        if step < steps - 2:
            position, *rest_next = tie(position, *rest)
            rest = send(rest_next)
        own.append(panel)
        picked.append(rows)
        positions.append(position)
        if step < steps - 1:
            other.append(hand_over(panel))
        blocks = following
    queries = [*queries, *project_queries(picked, query_slab, output_slab)]
    own[-1], queries[-1], other[0], *blocks = tie(own[-1], queries[-1], other[0], *lead)
    other.append(hand_over(own[-1]))
    keys, mark = project_keys(token_half, blocks, key_weight)
    panel, rows, position = project_values(token_half, blocks, plan[-1], mark, keys, value_weight)
    own.append(panel)
    other.append(hand_over(panel))
    positions.append(position)
    queries = [*queries, *project_queries([rows], query_slab, output_slab)]
    held = arrange(ctx_count, plan, own, other, queries, positions)

    def swap(piece, k):
        return lax.ppermute(piece, "ctx", [(c, c ^ k) for c in range(ctx_count)])

    half, quarter = ctx_count // 2, ctx_count // 4
    far, mine = [], []
    for start, count in ((half, quarter), (half + quarter, quarter), (0, half)):
        pieces = attend((start // 2, count // 2), *held, output_slab)
        if start > 0:
            places, *pieces = tie(held[2], *pieces)
            held = [*held[:2], places]
            far.append([swap(piece, start + r) for r, piece in enumerate(pieces)])
        else:
            near = pieces
    *near, far[0][0] = tie(*near, far[0][0])
    near = [near[0]] + [swap(near[r], r) for r in range(1, half)]

    pieces = [*near, *far[0], *far[1]]
    early, late = piece_groups(ctx_count)
    early_mix, late_mix = gate_mix(quarter_count, halves, router_weight.T, ctx_count)
    ahead = combine(early_mix, [pieces[k] for k in early], [], jnp.float32)
    return combine(late_mix, [pieces[k] for k in late], [ahead], jnp.bfloat16)


def solution(mesh):
    in_specs = (
        P(("groups", "ctx", "exp"), None),
        P(),
        P(),
        P(("groups", "ctx", "exp"), None),
        P(),
        P(),
        P("ctx", None, None),
        P("ctx", None, None),
    )
    out_specs = P(("groups", "ctx", "exp"), None)
    return jax.shard_map(
        per_device, mesh=mesh, in_specs=in_specs, out_specs=out_specs, check_vma=False
    )
```

```python
import functools
import math

import jax
import jax.numpy as jnp
from jax import lax
from jax.experimental import pallas as pl
from jax.experimental.pallas import tpu as pltpu
from jax.sharding import PartitionSpec as P

HS = 128
EXPERTS = 8
MOST = 40
SLOTS = 48
MASKED = -1e30
LANES = 128
CODES = 16
TERMS = 2
MIB = 1 << 20
WHOLE = pl.BlockSpec(memory_space=pltpu.VMEM)


def ring_rank(place, count):
    place = lax.rem(place + 2 * count, count)
    return jnp.where(place < count // 2, 2 * place, 2 * (count - 1 - place) + 1)


def ring_place(rank, count):
    return jnp.where(rank % 2 == 0, rank // 2, count - 1 - rank // 2)


def ring_owner(offset):
    count = lax.axis_size("ctx")
    return ring_rank(ring_place(lax.axis_index("ctx"), count) + offset, count)


def norm_kernel(*refs):
    sources, top_ref, bottom_ref, *held, arrivals = refs[:3], *refs[3:]
    copies = [
        pltpu.make_async_copy(source, target, arrivals.at[i])
        for i, (source, target) in enumerate(zip(sources, held))
    ]
    for copy in copies:
        copy.start()
    for copy in copies:
        copy.wait()
    tokens_ref, gain_ref, routes_ref = held
    floats = tokens_ref[...].astype(jnp.float32)
    count, width = floats.shape
    factor = lax.rsqrt(jnp.mean(floats * floats, axis=1, keepdims=True) + 1e-06)
    normed = (floats * factor * gain_ref[...]).astype(jnp.bfloat16)
    expert = lax.broadcasted_iota(jnp.int32, (CODES, count), 0)
    named = (expert == routes_ref[0:1, :]) | (expert == routes_ref[1:2, :])
    before = lax.broadcasted_iota(jnp.int32, (count, count), 0) < lax.broadcasted_iota(
        jnp.int32, (count, count), 1
    )
    rank = jnp.dot(
        named.astype(jnp.bfloat16),
        before.astype(jnp.bfloat16),
        preferred_element_type=jnp.float32,
    )
    codes = jnp.where(named, rank, -1.0).astype(jnp.bfloat16)
    half = count // 2
    for ref, first in ((top_ref, 0), (bottom_ref, half)):
        for c in range(width // LANES):
            ref[pl.ds(c * half, half), :] = normed[
                first : first + half, c * LANES : (c + 1) * LANES
            ]
        ref[pl.ds(width // LANES * half, CODES), :] = codes


def message_rows(ref, half):
    tiles = (ref.shape[0] - CODES) // half
    return jnp.concatenate([ref[pl.ds(c * half, half), :] for c in range(tiles)], axis=1)


def message_codes(ref):
    return ref[pl.ds(ref.shape[0] - CODES, CODES), :].astype(jnp.float32)


def norm_rows(tokens, norm_gain, routes):
    count, width = tokens.shape
    half = jax.ShapeDtypeStruct((width // LANES * (count // 2) + CODES, LANES), jnp.bfloat16)
    operands = (tokens, norm_gain.reshape(1, -1), routes.T)
    return pl.pallas_call(
        norm_kernel,
        in_specs=[pl.BlockSpec(memory_space=pltpu.HBM)] * 3,
        out_specs=[WHOLE] * 2,
        out_shape=[half, half],
        scratch_shapes=[pltpu.VMEM(x.shape, x.dtype) for x in operands]
        + [pltpu.SemaphoreType.DMA((3,))],
        compiler_params=pltpu.CompilerParams(vmem_limit_bytes=60 * MIB),
        name="norm_rows",
    )(*operands)


def column_parts(ref):
    step = min(ref.shape[1], 256)
    return [pl.ds(start, step) for start in range(0, ref.shape[1], step)]


def keys_kernel(half, count, *refs):
    blocks = refs[:count]
    weight_ref, panel_ref, mark_ref = refs[count:]
    rows = jnp.concatenate([message_rows(block, half) for block in blocks], axis=0)
    for cols in column_parts(weight_ref):
        product = jnp.dot(rows, weight_ref[:, cols], preferred_element_type=jnp.float32)
        panel_ref[:, cols] = product.astype(jnp.bfloat16)
    mark_ref[...] = product[:8, :LANES]


def project_keys(half, blocks, key_weight):
    row_count = half * len(blocks)
    width = key_weight.shape[1]
    return pl.pallas_call(
        functools.partial(keys_kernel, half, len(blocks)),
        in_specs=[WHOLE] * (len(blocks) + 1),
        out_specs=[WHOLE] * 2,
        out_shape=[
            jax.ShapeDtypeStruct((row_count, width), jnp.bfloat16),
            jax.ShapeDtypeStruct((8, LANES), jnp.float32),
        ],
        compiler_params=pltpu.CompilerParams(vmem_limit_bytes=12 * MIB),
        name="project_keys",
    )(*blocks, key_weight)


def values_kernel(half, offsets, count, experts, mark_ref, keys_ref, *refs):
    blocks = refs[:count]
    value_ref, panel_ref, picked_ref, pos_ref = refs[count:]
    rows = jnp.concatenate([message_rows(block, half) for block in blocks], axis=0)
    tok_count = 2 * half
    expert = lax.axis_index("ctx") // (lax.axis_size("ctx") // experts)
    number = lax.broadcasted_iota(jnp.int32, (tok_count, LANES), 0).astype(jnp.bfloat16)
    for g, offset in enumerate(offsets):
        part = slice(g * tok_count, (g + 1) * tok_count)
        codes = message_codes(blocks[2 * g])
        mine = lax.broadcasted_iota(jnp.int32, codes.shape, 0) == expert
        slot = jnp.sum(jnp.where(mine, codes, 0.0), axis=0, keepdims=True)
        order = lax.broadcasted_iota(jnp.int32, (SLOTS, tok_count), 0).astype(jnp.float32)
        chosen = (order == slot).astype(jnp.bfloat16)
        picked_ref[g] = jnp.dot(
            chosen, rows[part], preferred_element_type=jnp.float32
        ).astype(jnp.bfloat16)
        start = (ring_owner(offset) * lax.axis_size("exp") + lax.axis_index("exp")) * tok_count
        pos_ref[g] = jnp.dot(
            chosen, number, preferred_element_type=jnp.float32
        ) + start.astype(jnp.float32)
    panel_ref[0] = keys_ref[...]
    for cols in column_parts(value_ref):
        panel_ref[1, :, cols] = jnp.dot(
            rows, value_ref[:, cols], preferred_element_type=jnp.float32
        ).astype(jnp.bfloat16)


def project_values(half, blocks, offsets, mark, keys, value_weight):
    row_count = half * len(blocks)
    model_width, width = value_weight.shape
    owners = len(offsets)
    return pl.pallas_call(
        functools.partial(values_kernel, half, offsets, len(blocks), EXPERTS),
        in_specs=[WHOLE] * (len(blocks) + 3),
        out_specs=[WHOLE] * 3,
        out_shape=[
            jax.ShapeDtypeStruct((2, row_count, width), jnp.bfloat16),
            jax.ShapeDtypeStruct((owners, SLOTS, model_width), jnp.bfloat16),
            jax.ShapeDtypeStruct((owners, SLOTS, LANES), jnp.float32),
        ],
        compiler_params=pltpu.CompilerParams(vmem_limit_bytes=12 * MIB),
        name="project_values",
    )(mark, keys, *blocks, value_weight)


def queries_kernel(*refs):
    count = len(refs) // 2 - 1
    picked, weight_ref, outs = refs[:count], refs[count], refs[count + 2 :]
    rows = jnp.concatenate([ref[g] for ref in picked for g in range(ref.shape[0])], axis=0)
    places = [(ref, g) for ref in outs for g in range(ref.shape[0])]
    for cols in column_parts(weight_ref):
        product = jnp.dot(rows, weight_ref[:, cols], preferred_element_type=jnp.float32)
        for i, (ref, g) in enumerate(places):
            ref[g, :, cols] = product[i * SLOTS : (i + 1) * SLOTS].astype(jnp.bfloat16)


def project_queries(picked, query_slab, next_slab):
    model_width, width = query_slab.shape
    owners = sum(rows.shape[0] for rows in picked)
    held = 4 * model_width * width + owners * SLOTS * (4 * model_width + 4 * width)
    return pl.pallas_call(
        queries_kernel,
        in_specs=[WHOLE] * (len(picked) + 2),
        out_specs=[WHOLE] * len(picked),
        out_shape=[
            jax.ShapeDtypeStruct((rows.shape[0], SLOTS, width), jnp.bfloat16) for rows in picked
        ],
        compiler_params=pltpu.CompilerParams(vmem_limit_bytes=held + 6 * MIB),
        name="project_queries",
    )(*picked, query_slab, next_slab)


def arrange_kernel(plan, *refs):
    count = len(plan)
    own_refs, other_refs, query_refs, pos_refs = (refs[k * count : (k + 1) * count] for k in range(4))
    panel_ref, queries_ref, places_ref = refs[4 * count :]
    exp_count = 2
    side = lax.axis_index("exp")
    tok_count = panel_ref.shape[2]
    for offsets, own_ref, other_ref, query_ref, pos_ref in zip(
        plan, own_refs, other_refs, query_refs, pos_refs
    ):
        for g, offset in enumerate(offsets):
            owner = ring_owner(offset)
            part = pl.ds(g * tok_count, tok_count)
            for which in range(2):
                panel_ref[which, owner * exp_count + side] = own_ref[which, part]
                panel_ref[which, owner * exp_count + 1 - side] = other_ref[which, part]
            queries_ref[owner] = query_ref[g].astype(jnp.float32)[:MOST]
            places_ref[owner] = pos_ref[g, :MOST]


def arrange(owners, plan, own, other, queries, positions):
    width = own[0].shape[2]
    tok_count = own[0].shape[1] // len(plan[0])
    shapes = [
        jax.ShapeDtypeStruct((2, 2 * owners, tok_count, width), jnp.bfloat16),
        jax.ShapeDtypeStruct((owners, MOST, width), jnp.float32),
        jax.ShapeDtypeStruct((owners, MOST, LANES), jnp.float32),
    ]
    operands = (*own, *other, *queries, *positions)
    return pl.pallas_call(
        functools.partial(arrange_kernel, plan),
        in_specs=[WHOLE] * len(operands),
        out_specs=[WHOLE] * 3,
        out_shape=shapes,
        compiler_params=pltpu.CompilerParams(
            vmem_limit_bytes=8 * MIB
        ),
        name="arrange",
    )(*operands)


def attend_kernel(lots, heads, panel_ref, queries_ref, places_ref, weight_ref, *refs):
    outs, (attended, scores, weights) = refs[:-3], refs[-3:]
    first, count = lots
    blocks, tok_count, width = panel_ref.shape[1:]
    rate = math.log2(math.e) / math.sqrt(HS)
    rank = lax.axis_index("ctx")
    tiles = blocks // 4
    tile = 2 * MOST
    parts = 4
    span = blocks * tok_count // parts
    per_span = blocks // parts
    passes = width // (heads * HS)

    def serve(part_id, number, lot, lanes):
        reach = (part_id + 1) * span
        pair = pl.ds(2 * number, 2)
        spots = places_ref[pair].reshape(tile, LANES)
        for h in range(heads):
            held = queries_ref[pair, :, lanes[h]].reshape(tile, HS).astype(jnp.bfloat16)
            for j in range(part_id + 1):
                key_part = panel_ref[0, per_span * j : per_span * (j + 1), :, lanes[h]]
                scores[h, :, pl.ds(j * span, span)] = lax.dot_general(
                    held,
                    key_part.reshape(span, HS),
                    (((1,), (1,)), ((), ())),
                    preferred_element_type=jnp.float32,
                )
        for h in range(heads):
            for sub in range(0, tile, 16):
                rows = pl.ds(sub, 16)
                part = scores[h, rows, pl.ds(0, reach)]
                last = part[:, reach - span :]
                key_index = lax.broadcasted_iota(jnp.int32, last.shape, 1) + (reach - span)
                spot = spots[sub : sub + 16, 0:1]
                last = jnp.where(key_index.astype(jnp.float32) <= spot, last, MASKED)
                if part_id > 0:
                    part = jnp.concatenate([part[:, : reach - span], last], axis=1)
                else:
                    part = last
                peak = jnp.max(part, axis=1, keepdims=True)
                raised = jnp.exp2((part - peak) * rate)
                total = jnp.sum(raised, axis=1, keepdims=True)
                weights[h, rows, pl.ds(0, reach)] = (raised * (1.0 / total)).astype(jnp.bfloat16)
        for h in range(heads):
            total = None
            for j in range(part_id + 1):
                value_part = panel_ref[1, per_span * j : per_span * (j + 1), :, lanes[h]]
                product = jnp.dot(
                    weights[h, :, pl.ds(j * span, span)],
                    value_part.reshape(span, HS),
                    preferred_element_type=jnp.float32,
                )
                total = product if total is None else total + product
            spare = jnp.zeros((SLOTS - MOST, HS), jnp.float32)
            for side in range(2):
                rows = jnp.concatenate([total[side * MOST : (side + 1) * MOST], spare], axis=0)
                attended[2 * lot + (side ^ (rank % 2)), :, lanes[h]] = rows.astype(jnp.bfloat16)

    def one(at, carry):
        lot, now = at // passes, at % passes
        number = (rank // 2) ^ (first + lot)
        lanes = [pl.ds(pl.multiple_of((now * heads + h) * HS, HS), HS) for h in range(heads)]
        for part_id in range(parts):
            pl.when(number // (tiles // parts) == part_id)(
                functools.partial(serve, part_id, number, lot, lanes)
            )
        return carry

    lax.fori_loop(0, count * passes, one, 0)
    rows = attended[...].reshape(2 * count * SLOTS, width)
    for cols in column_parts(weight_ref):
        product = jnp.dot(rows, weight_ref[:, cols], preferred_element_type=jnp.float32)
        for k, out_ref in enumerate(outs):
            out_ref[:, cols] = product[k * SLOTS : k * SLOTS + MOST].astype(jnp.bfloat16)


def attend(lots, panel, queries, places, output_slab):
    first, count = lots
    _, blocks, tok_count, width = panel.shape
    length = blocks * tok_count
    heads = min(8 if first == blocks // 8 else 4, width // HS) if blocks <= 16 else 1
    model_width = output_slab.shape[1]
    held = heads * 2 * SLOTS * length * 6 + 2 * length * width * 2 + width * model_width * 2
    held += 2 * count * SLOTS * (model_width * 8 + width * 2)
    return pl.pallas_call(
        functools.partial(attend_kernel, lots, heads),
        in_specs=[WHOLE] * 4,
        out_specs=[WHOLE] * (2 * count),
        out_shape=[jax.ShapeDtypeStruct((MOST, model_width), jnp.bfloat16)] * (2 * count),
        scratch_shapes=[
            pltpu.VMEM((2 * count, SLOTS, width), jnp.bfloat16),
            pltpu.VMEM((heads, 2 * MOST, length), jnp.float32),
            pltpu.VMEM((heads, 2 * MOST, length), jnp.bfloat16),
        ],
        compiler_params=pltpu.CompilerParams(vmem_limit_bytes=held * 9 // 8 + 4 * MIB),
        cost_estimate=pl.CostEstimate(
            flops=count * 2 * SLOTS * width * (4 * length + 2 * model_width),
            bytes_accessed=4 * length * width,
            transcendentals=count * 2 * SLOTS * length * width // HS,
        ),
        name="attend",
    )(panel, queries, places, output_slab)


def piece_groups(count):
    return [0, *range(count // 2, count)], list(range(count // 2 - 1, 0, -1))


def mix_kernel(quarter_count, top_ref, bottom_ref, router_ref, *refs):
    *mix_refs, slots_ref, gates_ref = refs
    half = LANES // 2
    rows = jnp.concatenate([message_rows(ref, half) for ref in (top_ref, bottom_ref)], axis=0)
    rest, terms = router_ref[...], []
    for _ in range(3):
        terms.append(rest.astype(jnp.bfloat16).astype(jnp.float32))
        rest = rest - terms[-1]
    experts = rest.shape[0]
    router = jnp.concatenate([*terms, jnp.zeros_like(rest)], axis=0).astype(jnp.bfloat16)
    products = lax.dot_general(
        router, rows, (((1,), (1,)), ((), ())), preferred_element_type=jnp.float32
    )
    logits = products[:experts] + (
        products[experts : 2 * experts] + products[2 * experts : 3 * experts]
    )
    slots = message_codes(top_ref)[:experts]
    logits = jnp.where(slots >= 0, logits, -jnp.inf)
    raised = jnp.exp(logits - jnp.max(logits, axis=0, keepdims=True))
    slots_ref[...] = slots
    gates_ref[...] = raised / jnp.sum(raised, axis=0, keepdims=True)
    tok_count = slots.shape[1]
    order = lax.broadcasted_iota(jnp.int32, (SLOTS, tok_count), 0).astype(jnp.float32)
    for mix_ref, group in zip(mix_refs, piece_groups(sum(r.shape[1] for r in mix_refs) // SLOTS)):
        parts = []
        for k in group:
            expert = pl.ds((lax.axis_index("ctx") ^ k) // quarter_count, 1)
            parts.append(jnp.where(order == slots_ref[expert, :], gates_ref[expert, :], 0.0))
        total = jnp.concatenate(parts, axis=0).T
        for part in range(TERMS):
            term = total.astype(jnp.bfloat16)
            mix_ref[pl.ds(part * tok_count, tok_count), :] = term
            total = total - term.astype(jnp.float32)


def gate_mix(quarter_count, halves, router, count):
    tok_count = LANES
    held = pltpu.VMEM((router.shape[0], tok_count), jnp.float32)
    return pl.pallas_call(
        functools.partial(mix_kernel, quarter_count),
        in_specs=[WHOLE] * 3,
        out_specs=[WHOLE] * 2,
        out_shape=[
            jax.ShapeDtypeStruct((TERMS * tok_count, len(group) * SLOTS), jnp.bfloat16)
            for group in piece_groups(count)
        ],
        scratch_shapes=[held, held],
        compiler_params=pltpu.CompilerParams(vmem_limit_bytes=16 * MIB),
        name="gate_mix",
    )(*halves, router)


def combine_kernel(ahead_count, mix_ref, *refs):
    if ahead_count > 0:
        *refs, out_ref, held, sent = refs
    else:
        *refs, held = refs
        out_ref = held
    ahead, pieces = refs[:ahead_count], refs[ahead_count:]
    tok_count, model_width = out_ref.shape
    copies = []
    step = min(model_width, 512)
    spare = jnp.zeros((SLOTS - MOST, step), jnp.float32)
    for start in range(0, model_width, step):
        cols = pl.ds(start, step)
        rows = []
        for piece in pieces:
            rows += [piece[:, cols].astype(jnp.float32), spare]
        rows = jnp.concatenate(rows, axis=0).astype(jnp.bfloat16)
        product = jnp.dot(mix_ref[...], rows, preferred_element_type=jnp.float32)
        total = product[-tok_count:]
        for part in range(TERMS - 2, -1, -1):
            total = product[part * tok_count : (part + 1) * tok_count] + total
        for ref in ahead:
            total = total + ref[:, cols]
        held[:, cols] = total.astype(held.dtype)
        if ahead_count > 0:
            copies.append(
                pltpu.make_async_copy(held.at[:, cols], out_ref.at[:, cols], sent.at[len(copies)])
            )
            copies[-1].start()
    for copy in copies:
        copy.wait()


def combine(mix, pieces, ahead, dtype):
    tok_count = mix.shape[0] // TERMS
    model_width = pieces[0].shape[1]
    scratch = [
        pltpu.VMEM((tok_count, model_width), dtype),
        pltpu.SemaphoreType.DMA((-(-model_width // 512),)),
    ]
    return pl.pallas_call(
        functools.partial(combine_kernel, len(ahead)),
        in_specs=[WHOLE] * (1 + len(ahead) + len(pieces)),
        out_specs=pl.BlockSpec(memory_space=pl.ANY) if ahead else WHOLE,
        out_shape=jax.ShapeDtypeStruct((tok_count, model_width), dtype),
        scratch_shapes=scratch if ahead else [],
        compiler_params=pltpu.CompilerParams(vmem_limit_bytes=24 * MIB),
        name="combine",
    )(mix, *ahead, *pieces)


def per_device(
    tokens, norm_gain, router_weight, routes, key_weight, value_weight, query_weight, output_weight
):
    tok_count, model_width = tokens.shape
    ctx_count = lax.axis_size("ctx")
    exp_count = lax.axis_size("exp")
    quarter_count = ctx_count // EXPERTS
    head_width = query_weight.shape[2]
    ranks = list(range(0, ctx_count, 2)) + list(range(1, ctx_count, 2))[::-1]
    forward = [(ranks[p], ranks[(p + 1) % ctx_count]) for p in range(ctx_count)]
    backward = [(b, a) for a, b in forward]
    sibling = [(e, 1 - e) for e in range(exp_count)]
    query_slab = query_weight[0]
    output_slab = output_weight[0]
    if quarter_count > 1:
        first = (lax.axis_index("ctx") % quarter_count) * head_width
        key_weight = lax.dynamic_slice_in_dim(key_weight, first, head_width, axis=1)
        value_weight = lax.dynamic_slice_in_dim(value_weight, first, head_width, axis=1)

    halves = norm_rows(tokens, norm_gain, routes)
    token_half = tok_count // 2
    steps = ctx_count // 2
    plan = [[0]] + [[-step, step] for step in range(1, steps)] + [[steps]]
    own, other, picked, queries, positions = [], [], [], [], []

    def send(parts):
        return [lax.ppermute(parts[0], "ctx", forward), lax.ppermute(parts[1], "ctx", backward)]

    def hand_over(panel):
        return lax.ppermute(panel, "exp", sibling)

    def tie(*arrays):
        return lax.optimization_barrier(arrays)

    blocks = halves
    lead = send([halves[0], halves[1]])
    rest = send([halves[1], halves[0]])
    for step in range(steps):
        keys, mark = project_keys(token_half, blocks, key_weight)
        following = [lead[0], rest[0], rest[1], lead[1]]
        if step == steps - 2:
            queries = project_queries(picked, query_slab, output_slab)
            picked = []
        if step < steps - 1:
            mark, *lead_next = tie(mark, *lead, *queries)
            queries = lead_next[2:]
            lead = send(lead_next[:2])
        panel, rows, position = project_values(token_half, blocks, plan[step], mark, keys, value_weight)
        if step < steps - 2:
            position, *rest_next = tie(position, *rest)
            rest = send(rest_next)
        own.append(panel)
        picked.append(rows)
        positions.append(position)
        if step < steps - 1:
            other.append(hand_over(panel))
        blocks = following
    queries = [*queries, *project_queries(picked, query_slab, output_slab)]
    own[-1], queries[-1], other[0], *blocks = tie(own[-1], queries[-1], other[0], *lead)
    other.append(hand_over(own[-1]))
    keys, mark = project_keys(token_half, blocks, key_weight)
    panel, rows, position = project_values(token_half, blocks, plan[-1], mark, keys, value_weight)
    own.append(panel)
    other.append(hand_over(panel))
    positions.append(position)
    queries = [*queries, *project_queries([rows], query_slab, output_slab)]
    held = arrange(ctx_count, plan, own, other, queries, positions)

    def swap(piece, k):
        return lax.ppermute(piece, "ctx", [(c, c ^ k) for c in range(ctx_count)])

    half, quarter = ctx_count // 2, ctx_count // 4
    far, mine = [], []
    for start, count in ((half, quarter), (half + quarter, quarter), (0, half)):
        pieces = attend((start // 2, count // 2), *held, output_slab)
        if start > 0:
            places, *pieces = tie(held[2], *pieces)
            held = [*held[:2], places]
            if far:
                pieces[-1], far[0][0] = tie(pieces[-1], far[0][0])
            far.append([swap(piece, start + r) for r, piece in enumerate(pieces)])
        else:
            near = pieces
    *near, far[0][0] = tie(*near, far[0][0])
    near = [near[0]] + [swap(near[r], r) for r in range(1, half)]

    pieces = [*near, *far[0], *far[1]]
    early, late = piece_groups(ctx_count)
    early_mix, late_mix = gate_mix(quarter_count, halves, router_weight.T, ctx_count)
    ahead = combine(early_mix, [pieces[k] for k in early], [], jnp.float32)
    return combine(late_mix, [pieces[k] for k in late], [ahead], jnp.bfloat16)


def solution(mesh):
    in_specs = (
        P(("groups", "ctx", "exp"), None),
        P(),
        P(),
        P(("groups", "ctx", "exp"), None),
        P(),
        P(),
        P("ctx", None, None),
        P("ctx", None, None),
    )
    out_specs = P(("groups", "ctx", "exp"), None)
    return jax.shard_map(
        per_device, mesh=mesh, in_specs=in_specs, out_specs=out_specs, check_vma=False
    )
```

```python
import functools
import math

import jax
import jax.numpy as jnp
from jax import lax
from jax.experimental import pallas as pl
from jax.experimental.pallas import tpu as pltpu
from jax.sharding import PartitionSpec as P

HS = 128
EXPERTS = 8
MOST = 40
SLOTS = 48
MASKED = -1e30
LANES = 128
CODES = 16
TERMS = 2
MIB = 1 << 20
WHOLE = pl.BlockSpec(memory_space=pltpu.VMEM)


def ring_rank(place, count):
    place = lax.rem(place + 2 * count, count)
    return jnp.where(place < count // 2, 2 * place, 2 * (count - 1 - place) + 1)


def ring_place(rank, count):
    return jnp.where(rank % 2 == 0, rank // 2, count - 1 - rank // 2)


def ring_owner(offset):
    count = lax.axis_size("ctx")
    return ring_rank(ring_place(lax.axis_index("ctx"), count) + offset, count)


def norm_kernel(*refs):
    sources, top_ref, bottom_ref, *held, arrivals = refs[:3], *refs[3:]
    copies = [
        pltpu.make_async_copy(source, target, arrivals.at[i])
        for i, (source, target) in enumerate(zip(sources, held))
    ]
    for copy in copies:
        copy.start()
    for copy in copies:
        copy.wait()
    tokens_ref, gain_ref, routes_ref = held
    floats = tokens_ref[...].astype(jnp.float32)
    count, width = floats.shape
    factor = lax.rsqrt(jnp.mean(floats * floats, axis=1, keepdims=True) + 1e-06)
    normed = (floats * factor * gain_ref[...]).astype(jnp.bfloat16)
    expert = lax.broadcasted_iota(jnp.int32, (CODES, count), 0)
    named = (expert == routes_ref[0:1, :]) | (expert == routes_ref[1:2, :])
    before = lax.broadcasted_iota(jnp.int32, (count, count), 0) < lax.broadcasted_iota(
        jnp.int32, (count, count), 1
    )
    rank = jnp.dot(
        named.astype(jnp.bfloat16),
        before.astype(jnp.bfloat16),
        preferred_element_type=jnp.float32,
    )
    codes = jnp.where(named, rank, -1.0).astype(jnp.bfloat16)
    half = count // 2
    for ref, first in ((top_ref, 0), (bottom_ref, half)):
        for c in range(width // LANES):
            ref[pl.ds(c * half, half), :] = normed[
                first : first + half, c * LANES : (c + 1) * LANES
            ]
        ref[pl.ds(width // LANES * half, CODES), :] = codes


def message_rows(ref, half):
    tiles = (ref.shape[0] - CODES) // half
    return jnp.concatenate([ref[pl.ds(c * half, half), :] for c in range(tiles)], axis=1)


def message_codes(ref):
    return ref[pl.ds(ref.shape[0] - CODES, CODES), :].astype(jnp.float32)


def norm_rows(tokens, norm_gain, routes):
    count, width = tokens.shape
    half = jax.ShapeDtypeStruct((width // LANES * (count // 2) + CODES, LANES), jnp.bfloat16)
    operands = (tokens, norm_gain.reshape(1, -1), routes.T)
    return pl.pallas_call(
        norm_kernel,
        in_specs=[pl.BlockSpec(memory_space=pltpu.HBM)] * 3,
        out_specs=[WHOLE] * 2,
        out_shape=[half, half],
        scratch_shapes=[pltpu.VMEM(x.shape, x.dtype) for x in operands]
        + [pltpu.SemaphoreType.DMA((3,))],
        compiler_params=pltpu.CompilerParams(vmem_limit_bytes=60 * MIB),
        name="norm_rows",
    )(*operands)


def column_parts(ref):
    step = min(ref.shape[1], 256)
    return [pl.ds(start, step) for start in range(0, ref.shape[1], step)]


def keys_kernel(half, count, *refs):
    blocks = refs[:count]
    weight_ref, panel_ref, mark_ref = refs[count:]
    rows = jnp.concatenate([message_rows(block, half) for block in blocks], axis=0)
    for cols in column_parts(weight_ref):
        product = jnp.dot(rows, weight_ref[:, cols], preferred_element_type=jnp.float32)
        panel_ref[:, cols] = product.astype(jnp.bfloat16)
    mark_ref[...] = product[:8, :LANES]


def project_keys(half, blocks, key_weight):
    row_count = half * len(blocks)
    width = key_weight.shape[1]
    return pl.pallas_call(
        functools.partial(keys_kernel, half, len(blocks)),
        in_specs=[WHOLE] * (len(blocks) + 1),
        out_specs=[WHOLE] * 2,
        out_shape=[
            jax.ShapeDtypeStruct((row_count, width), jnp.bfloat16),
            jax.ShapeDtypeStruct((8, LANES), jnp.float32),
        ],
        compiler_params=pltpu.CompilerParams(vmem_limit_bytes=12 * MIB),
        name="project_keys",
    )(*blocks, key_weight)


def values_kernel(half, offsets, count, experts, mark_ref, keys_ref, *refs):
    blocks = refs[:count]
    value_ref, panel_ref, picked_ref, pos_ref = refs[count:]
    rows = jnp.concatenate([message_rows(block, half) for block in blocks], axis=0)
    tok_count = 2 * half
    expert = lax.axis_index("ctx") // (lax.axis_size("ctx") // experts)
    number = lax.broadcasted_iota(jnp.int32, (tok_count, LANES), 0).astype(jnp.bfloat16)
    for g, offset in enumerate(offsets):
        part = slice(g * tok_count, (g + 1) * tok_count)
        codes = message_codes(blocks[2 * g])
        mine = lax.broadcasted_iota(jnp.int32, codes.shape, 0) == expert
        slot = jnp.sum(jnp.where(mine, codes, 0.0), axis=0, keepdims=True)
        order = lax.broadcasted_iota(jnp.int32, (SLOTS, tok_count), 0).astype(jnp.float32)
        chosen = (order == slot).astype(jnp.bfloat16)
        picked_ref[g] = jnp.dot(
            chosen, rows[part], preferred_element_type=jnp.float32
        ).astype(jnp.bfloat16)
        start = (ring_owner(offset) * lax.axis_size("exp") + lax.axis_index("exp")) * tok_count
        pos_ref[g] = jnp.dot(
            chosen, number, preferred_element_type=jnp.float32
        ) + start.astype(jnp.float32)
    panel_ref[0] = keys_ref[...]
    for cols in column_parts(value_ref):
        panel_ref[1, :, cols] = jnp.dot(
            rows, value_ref[:, cols], preferred_element_type=jnp.float32
        ).astype(jnp.bfloat16)


def project_values(half, blocks, offsets, mark, keys, value_weight):
    row_count = half * len(blocks)
    model_width, width = value_weight.shape
    owners = len(offsets)
    return pl.pallas_call(
        functools.partial(values_kernel, half, offsets, len(blocks), EXPERTS),
        in_specs=[WHOLE] * (len(blocks) + 3),
        out_specs=[WHOLE] * 3,
        out_shape=[
            jax.ShapeDtypeStruct((2, row_count, width), jnp.bfloat16),
            jax.ShapeDtypeStruct((owners, SLOTS, model_width), jnp.bfloat16),
            jax.ShapeDtypeStruct((owners, SLOTS, LANES), jnp.float32),
        ],
        compiler_params=pltpu.CompilerParams(vmem_limit_bytes=12 * MIB),
        name="project_values",
    )(mark, keys, *blocks, value_weight)


def queries_kernel(*refs):
    count = len(refs) // 2 - 1
    picked, weight_ref, outs = refs[:count], refs[count], refs[count + 2 :]
    rows = jnp.concatenate([ref[g] for ref in picked for g in range(ref.shape[0])], axis=0)
    places = [(ref, g) for ref in outs for g in range(ref.shape[0])]
    for cols in column_parts(weight_ref):
        product = jnp.dot(rows, weight_ref[:, cols], preferred_element_type=jnp.float32)
        for i, (ref, g) in enumerate(places):
            ref[g, :, cols] = product[i * SLOTS : (i + 1) * SLOTS].astype(jnp.bfloat16)


def project_queries(picked, query_slab, next_slab):
    model_width, width = query_slab.shape
    owners = sum(rows.shape[0] for rows in picked)
    held = 4 * model_width * width + owners * SLOTS * (4 * model_width + 4 * width)
    return pl.pallas_call(
        queries_kernel,
        in_specs=[WHOLE] * (len(picked) + 2),
        out_specs=[WHOLE] * len(picked),
        out_shape=[
            jax.ShapeDtypeStruct((rows.shape[0], SLOTS, width), jnp.bfloat16) for rows in picked
        ],
        compiler_params=pltpu.CompilerParams(vmem_limit_bytes=held + 6 * MIB),
        name="project_queries",
    )(*picked, query_slab, next_slab)


def arrange_other(panel_ref, offsets, other_ref):
    tok_count = panel_ref.shape[2]
    for g, offset in enumerate(offsets):
        place = ring_owner(offset) * 2 + 1 - lax.axis_index("exp")
        for which in range(2):
            panel_ref[which, place] = other_ref[which, pl.ds(g * tok_count, tok_count)]


def arrange_kernel(plan, *refs):
    count = len(plan)
    own_refs, query_refs, pos_refs = (refs[k * count : (k + 1) * count] for k in range(3))
    other_refs = refs[3 * count : -3]
    panel_ref, queries_ref, places_ref = refs[-3:]
    tok_count = panel_ref.shape[2]
    for offsets, own_ref, query_ref, pos_ref in zip(plan, own_refs, query_refs, pos_refs):
        for g, offset in enumerate(offsets):
            owner = ring_owner(offset)
            for which in range(2):
                panel_ref[which, owner * 2 + lax.axis_index("exp")] = own_ref[
                    which, pl.ds(g * tok_count, tok_count)
                ]
            queries_ref[owner] = query_ref[g].astype(jnp.float32)[:MOST]
            places_ref[owner] = pos_ref[g, :MOST]
    for offsets, other_ref in zip(plan, other_refs):
        arrange_other(panel_ref, offsets, other_ref)


def arrange(owners, plan, own, other, queries, positions):
    width = own[0].shape[2]
    tok_count = own[0].shape[1] // len(plan[0])
    shapes = [
        jax.ShapeDtypeStruct((2, 2 * owners, tok_count, width), jnp.bfloat16),
        jax.ShapeDtypeStruct((owners, MOST, width), jnp.float32),
        jax.ShapeDtypeStruct((owners, MOST, LANES), jnp.float32),
    ]
    operands = (*own, *queries, *positions, *other[:-1])
    panel, queries, places = pl.pallas_call(
        functools.partial(arrange_kernel, plan),
        in_specs=[WHOLE] * len(operands),
        out_specs=[WHOLE] * 3,
        out_shape=shapes,
        compiler_params=pltpu.CompilerParams(vmem_limit_bytes=8 * MIB),
        name="arrange",
    )(*operands)

    def last_kernel(held_ref, other_ref, panel_ref):
        arrange_other(panel_ref, plan[-1], other_ref)

    panel = pl.pallas_call(
        last_kernel,
        in_specs=[WHOLE] * 2,
        out_specs=WHOLE,
        out_shape=shapes[0],
        input_output_aliases={0: 0},
        compiler_params=pltpu.CompilerParams(vmem_limit_bytes=8 * MIB),
        name="arrange_last",
    )(panel, other[-1])
    return panel, queries, places


def attend_kernel(lots, heads, panel_ref, queries_ref, places_ref, weight_ref, *refs):
    outs, (attended, scores, weights) = refs[:-3], refs[-3:]
    first, count = lots
    blocks, tok_count, width = panel_ref.shape[1:]
    rate = math.log2(math.e) / math.sqrt(HS)
    rank = lax.axis_index("ctx")
    tiles = blocks // 4
    tile = 2 * MOST
    parts = 4
    span = blocks * tok_count // parts
    per_span = blocks // parts
    passes = width // (heads * HS)

    def serve(part_id, number, lot, lanes):
        reach = (part_id + 1) * span
        pair = pl.ds(2 * number, 2)
        spots = places_ref[pair].reshape(tile, LANES)
        for h in range(heads):
            held = queries_ref[pair, :, lanes[h]].reshape(tile, HS).astype(jnp.bfloat16)
            for j in range(part_id + 1):
                key_part = panel_ref[0, per_span * j : per_span * (j + 1), :, lanes[h]]
                scores[h, :, pl.ds(j * span, span)] = lax.dot_general(
                    held,
                    key_part.reshape(span, HS),
                    (((1,), (1,)), ((), ())),
                    preferred_element_type=jnp.float32,
                )
        for h in range(heads):
            for sub in range(0, tile, 16):
                rows = pl.ds(sub, 16)
                part = scores[h, rows, pl.ds(0, reach)]
                last = part[:, reach - span :]
                key_index = lax.broadcasted_iota(jnp.int32, last.shape, 1) + (reach - span)
                spot = spots[sub : sub + 16, 0:1]
                last = jnp.where(key_index.astype(jnp.float32) <= spot, last, MASKED)
                if part_id > 0:
                    part = jnp.concatenate([part[:, : reach - span], last], axis=1)
                else:
                    part = last
                peak = jnp.max(part, axis=1, keepdims=True)
                raised = jnp.exp2((part - peak) * rate)
                total = jnp.sum(raised, axis=1, keepdims=True)
                weights[h, rows, pl.ds(0, reach)] = (raised * (1.0 / total)).astype(jnp.bfloat16)
        for h in range(heads):
            total = None
            for j in range(part_id + 1):
                value_part = panel_ref[1, per_span * j : per_span * (j + 1), :, lanes[h]]
                product = jnp.dot(
                    weights[h, :, pl.ds(j * span, span)],
                    value_part.reshape(span, HS),
                    preferred_element_type=jnp.float32,
                )
                total = product if total is None else total + product
            spare = jnp.zeros((SLOTS - MOST, HS), jnp.float32)
            for side in range(2):
                rows = jnp.concatenate([total[side * MOST : (side + 1) * MOST], spare], axis=0)
                attended[2 * lot + (side ^ (rank % 2)), :, lanes[h]] = rows.astype(jnp.bfloat16)

    def one(at, carry):
        lot, now = at // passes, at % passes
        number = (rank // 2) ^ (first + lot)
        lanes = [pl.ds(pl.multiple_of((now * heads + h) * HS, HS), HS) for h in range(heads)]
        for part_id in range(parts):
            pl.when(number // (tiles // parts) == part_id)(
                functools.partial(serve, part_id, number, lot, lanes)
            )
        return carry

    lax.fori_loop(0, count * passes, one, 0)
    rows = attended[...].reshape(2 * count * SLOTS, width)
    for cols in column_parts(weight_ref):
        product = jnp.dot(rows, weight_ref[:, cols], preferred_element_type=jnp.float32)
        for k, out_ref in enumerate(outs):
            out_ref[:, cols] = product[k * SLOTS : k * SLOTS + MOST].astype(jnp.bfloat16)


def attend(lots, panel, queries, places, output_slab):
    first, count = lots
    _, blocks, tok_count, width = panel.shape
    length = blocks * tok_count
    heads = min(8 if first == blocks // 8 else 4, width // HS) if blocks <= 16 else 1
    model_width = output_slab.shape[1]
    held = heads * 2 * SLOTS * length * 6 + 2 * length * width * 2 + width * model_width * 2
    held += 2 * count * SLOTS * (model_width * 8 + width * 2)
    return pl.pallas_call(
        functools.partial(attend_kernel, lots, heads),
        in_specs=[WHOLE] * 4,
        out_specs=[WHOLE] * (2 * count),
        out_shape=[jax.ShapeDtypeStruct((MOST, model_width), jnp.bfloat16)] * (2 * count),
        scratch_shapes=[
            pltpu.VMEM((2 * count, SLOTS, width), jnp.bfloat16),
            pltpu.VMEM((heads, 2 * MOST, length), jnp.float32),
            pltpu.VMEM((heads, 2 * MOST, length), jnp.bfloat16),
        ],
        compiler_params=pltpu.CompilerParams(vmem_limit_bytes=held * 9 // 8 + 4 * MIB),
        cost_estimate=pl.CostEstimate(
            flops=count * 1 * SLOTS * width * (4 * length + 2 * model_width),
            bytes_accessed=4 * length * width,
            transcendentals=count * 2 * SLOTS * length * width // HS,
        ),
        name="attend",
    )(panel, queries, places, output_slab)


def piece_groups(count):
    return [0, *range(count // 2, count)], list(range(count // 2 - 1, 0, -1))


def mix_kernel(quarter_count, top_ref, bottom_ref, router_ref, *refs):
    *mix_refs, slots_ref, gates_ref = refs
    half = LANES // 2
    rows = jnp.concatenate([message_rows(ref, half) for ref in (top_ref, bottom_ref)], axis=0)
    rest, terms = router_ref[...], []
    for _ in range(3):
        terms.append(rest.astype(jnp.bfloat16).astype(jnp.float32))
        rest = rest - terms[-1]
    experts = rest.shape[0]
    router = jnp.concatenate([*terms, jnp.zeros_like(rest)], axis=0).astype(jnp.bfloat16)
    products = lax.dot_general(
        router, rows, (((1,), (1,)), ((), ())), preferred_element_type=jnp.float32
    )
    logits = products[:experts] + (
        products[experts : 2 * experts] + products[2 * experts : 3 * experts]
    )
    slots = message_codes(top_ref)[:experts]
    logits = jnp.where(slots >= 0, logits, -jnp.inf)
    raised = jnp.exp(logits - jnp.max(logits, axis=0, keepdims=True))
    slots_ref[...] = slots
    gates_ref[...] = raised / jnp.sum(raised, axis=0, keepdims=True)
    tok_count = slots.shape[1]
    order = lax.broadcasted_iota(jnp.int32, (SLOTS, tok_count), 0).astype(jnp.float32)
    for mix_ref, group in zip(mix_refs, piece_groups(sum(r.shape[1] for r in mix_refs) // SLOTS)):
        parts = []
        for k in group:
            expert = pl.ds((lax.axis_index("ctx") ^ k) // quarter_count, 1)
            parts.append(jnp.where(order == slots_ref[expert, :], gates_ref[expert, :], 0.0))
        total = jnp.concatenate(parts, axis=0).T
        for part in range(TERMS):
            term = total.astype(jnp.bfloat16)
            mix_ref[pl.ds(part * tok_count, tok_count), :] = term
            total = total - term.astype(jnp.float32)


def gate_mix(quarter_count, halves, router, count):
    tok_count = LANES
    held = pltpu.VMEM((router.shape[0], tok_count), jnp.float32)
    return pl.pallas_call(
        functools.partial(mix_kernel, quarter_count),
        in_specs=[WHOLE] * 3,
        out_specs=[WHOLE] * 2,
        out_shape=[
            jax.ShapeDtypeStruct((TERMS * tok_count, len(group) * SLOTS), jnp.bfloat16)
            for group in piece_groups(count)
        ],
        scratch_shapes=[held, held],
        compiler_params=pltpu.CompilerParams(vmem_limit_bytes=16 * MIB),
        name="gate_mix",
    )(*halves, router)


def combine_kernel(ahead_count, mix_ref, *refs):
    if ahead_count > 0:
        *refs, out_ref, held, sent = refs
    else:
        *refs, held = refs
        out_ref = held
    ahead, pieces = refs[:ahead_count], refs[ahead_count:]
    tok_count, model_width = out_ref.shape
    copies = []
    step = min(model_width, 512)
    spare = jnp.zeros((SLOTS - MOST, step), jnp.float32)
    for start in range(0, model_width, step):
        cols = pl.ds(start, step)
        rows = []
        for piece in pieces:
            rows += [piece[:, cols].astype(jnp.float32), spare]
        rows = jnp.concatenate(rows, axis=0).astype(jnp.bfloat16)
        product = jnp.dot(mix_ref[...], rows, preferred_element_type=jnp.float32)
        total = product[-tok_count:]
        for part in range(TERMS - 2, -1, -1):
            total = product[part * tok_count : (part + 1) * tok_count] + total
        for ref in ahead:
            total = total + ref[:, cols]
        held[:, cols] = total.astype(held.dtype)
        if ahead_count > 0:
            copies.append(
                pltpu.make_async_copy(held.at[:, cols], out_ref.at[:, cols], sent.at[len(copies)])
            )
            copies[-1].start()
    for copy in copies:
        copy.wait()


def combine(mix, pieces, ahead, dtype):
    tok_count = mix.shape[0] // TERMS
    model_width = pieces[0].shape[1]
    scratch = [
        pltpu.VMEM((tok_count, model_width), dtype),
        pltpu.SemaphoreType.DMA((-(-model_width // 512),)),
    ]
    return pl.pallas_call(
        functools.partial(combine_kernel, len(ahead)),
        in_specs=[WHOLE] * (1 + len(ahead) + len(pieces)),
        out_specs=pl.BlockSpec(memory_space=pl.ANY) if ahead else WHOLE,
        out_shape=jax.ShapeDtypeStruct((tok_count, model_width), dtype),
        scratch_shapes=scratch if ahead else [],
        compiler_params=pltpu.CompilerParams(vmem_limit_bytes=24 * MIB),
        name="combine",
    )(mix, *ahead, *pieces)


def per_device(
    tokens, norm_gain, router_weight, routes, key_weight, value_weight, query_weight, output_weight
):
    tok_count, model_width = tokens.shape
    ctx_count = lax.axis_size("ctx")
    exp_count = lax.axis_size("exp")
    quarter_count = ctx_count // EXPERTS
    head_width = query_weight.shape[2]
    ranks = list(range(0, ctx_count, 2)) + list(range(1, ctx_count, 2))[::-1]
    forward = [(ranks[p], ranks[(p + 1) % ctx_count]) for p in range(ctx_count)]
    backward = [(b, a) for a, b in forward]
    sibling = [(e, 1 - e) for e in range(exp_count)]
    query_slab = query_weight[0]
    output_slab = output_weight[0]
    if quarter_count > 1:
        first = (lax.axis_index("ctx") % quarter_count) * head_width
        key_weight = lax.dynamic_slice_in_dim(key_weight, first, head_width, axis=1)
        value_weight = lax.dynamic_slice_in_dim(value_weight, first, head_width, axis=1)

    halves = norm_rows(tokens, norm_gain, routes)
    token_half = tok_count // 2
    steps = ctx_count // 2
    plan = [[0]] + [[-step, step] for step in range(1, steps)] + [[steps]]
    own, other, picked, queries, positions = [], [], [], [], []

    def send(parts):
        return [lax.ppermute(parts[0], "ctx", forward), lax.ppermute(parts[1], "ctx", backward)]

    def hand_over(panel):
        return lax.ppermute(panel, "exp", sibling)

    def tie(*arrays):
        return lax.optimization_barrier(arrays)

    blocks = halves
    lead = send([halves[0], halves[1]])
    rest = send([halves[1], halves[0]])
    for step in range(steps):
        keys, mark = project_keys(token_half, blocks, key_weight)
        following = [lead[0], rest[0], rest[1], lead[1]]
        if step == steps - 2:
            queries = project_queries(picked, query_slab, output_slab)
            picked = []
        if step < steps - 1:
            mark, *lead_next = tie(mark, *lead, *queries)
            queries = lead_next[2:]
            lead = send(lead_next[:2])
        panel, rows, position = project_values(token_half, blocks, plan[step], mark, keys, value_weight)
        if step < steps - 2:
            position, *rest_next = tie(position, *rest)
            rest = send(rest_next)
        own.append(panel)
        picked.append(rows)
        positions.append(position)
        if step < steps - 1:
            other.append(hand_over(panel))
        blocks = following
    queries = [*queries, *project_queries(picked, query_slab, output_slab)]
    own[-1], queries[-1], other[0], *blocks = tie(own[-1], queries[-1], other[0], *lead)
    other.append(hand_over(own[-1]))
    keys, mark = project_keys(token_half, blocks, key_weight)
    panel, rows, position = project_values(token_half, blocks, plan[-1], mark, keys, value_weight)
    own.append(panel)
    other.append(hand_over(panel))
    positions.append(position)
    queries = [*queries, *project_queries([rows], query_slab, output_slab)]
    held = arrange(ctx_count, plan, own, other, queries, positions)

    def swap(piece, k):
        return lax.ppermute(piece, "ctx", [(c, c ^ k) for c in range(ctx_count)])

    half, quarter = ctx_count // 2, ctx_count // 4
    far, mine = [], []
    for start, count in ((half, quarter), (half + quarter, quarter), (0, half)):
        pieces = attend((start // 2, count // 2), *held, output_slab)
        if start > 0:
            places, *pieces = tie(held[2], *pieces)
            held = [*held[:2], places]
            far.append([swap(piece, start + r) for r, piece in enumerate(pieces)])
        else:
            near = pieces
    *near, far[0][0] = tie(*near, far[0][0])
    near = [near[0]] + [swap(near[r], r) for r in range(1, half)]

    pieces = [*near, *far[0], *far[1]]
    early, late = piece_groups(ctx_count)
    early_mix, late_mix = gate_mix(quarter_count, halves, router_weight.T, ctx_count)
    ahead = combine(early_mix, [pieces[k] for k in early], [], jnp.float32)
    return combine(late_mix, [pieces[k] for k in late], [ahead], jnp.bfloat16)


def solution(mesh):
    in_specs = (
        P(("groups", "ctx", "exp"), None),
        P(),
        P(),
        P(("groups", "ctx", "exp"), None),
        P(),
        P(),
        P("ctx", None, None),
        P("ctx", None, None),
    )
    out_specs = P(("groups", "ctx", "exp"), None)
    return jax.shard_map(
        per_device, mesh=mesh, in_specs=in_specs, out_specs=out_specs, check_vma=False
    )
```

```python
import functools
import math

import jax
import jax.numpy as jnp
from jax import lax
from jax.experimental import pallas as pl
from jax.experimental.pallas import tpu as pltpu
from jax.sharding import PartitionSpec as P

HS = 128
EXPERTS = 8
MOST = 40
SLOTS = 48
MASKED = -1e30
LANES = 128
CODES = 16
TERMS = 2
MIB = 1 << 20
WHOLE = pl.BlockSpec(memory_space=pltpu.VMEM)


def ring_rank(place, count):
    place = lax.rem(place + 2 * count, count)
    return jnp.where(place < count // 2, 2 * place, 2 * (count - 1 - place) + 1)


def ring_place(rank, count):
    return jnp.where(rank % 2 == 0, rank // 2, count - 1 - rank // 2)


def ring_owner(offset):
    count = lax.axis_size("ctx")
    return ring_rank(ring_place(lax.axis_index("ctx"), count) + offset, count)


def norm_kernel(*refs):
    sources, top_ref, bottom_ref, *held, arrivals = refs[:3], *refs[3:]
    copies = [
        pltpu.make_async_copy(source, target, arrivals.at[i])
        for i, (source, target) in enumerate(zip(sources, held))
    ]
    for copy in copies:
        copy.start()
    for copy in copies:
        copy.wait()
    tokens_ref, gain_ref, routes_ref = held
    floats = tokens_ref[...].astype(jnp.float32)
    count, width = floats.shape
    factor = lax.rsqrt(jnp.mean(floats * floats, axis=1, keepdims=True) + 1e-06)
    normed = (floats * factor * gain_ref[...]).astype(jnp.bfloat16)
    expert = lax.broadcasted_iota(jnp.int32, (CODES, count), 0)
    named = (expert == routes_ref[0:1, :]) | (expert == routes_ref[1:2, :])
    before = lax.broadcasted_iota(jnp.int32, (count, count), 0) < lax.broadcasted_iota(
        jnp.int32, (count, count), 1
    )
    rank = jnp.dot(
        named.astype(jnp.bfloat16),
        before.astype(jnp.bfloat16),
        preferred_element_type=jnp.float32,
    )
    codes = jnp.where(named, rank, -1.0).astype(jnp.bfloat16)
    half = count // 2
    for ref, first in ((top_ref, 0), (bottom_ref, half)):
        for c in range(width // LANES):
            ref[pl.ds(c * half, half), :] = normed[
                first : first + half, c * LANES : (c + 1) * LANES
            ]
        ref[pl.ds(width // LANES * half, CODES), :] = codes


def message_rows(ref, half):
    tiles = (ref.shape[0] - CODES) // half
    return jnp.concatenate([ref[pl.ds(c * half, half), :] for c in range(tiles)], axis=1)


def message_codes(ref):
    return ref[pl.ds(ref.shape[0] - CODES, CODES), :].astype(jnp.float32)


def norm_rows(tokens, norm_gain, routes):
    count, width = tokens.shape
    half = jax.ShapeDtypeStruct((width // LANES * (count // 2) + CODES, LANES), jnp.bfloat16)
    operands = (tokens, norm_gain.reshape(1, -1), routes.T)
    return pl.pallas_call(
        norm_kernel,
        in_specs=[pl.BlockSpec(memory_space=pltpu.HBM)] * 3,
        out_specs=[WHOLE] * 2,
        out_shape=[half, half],
        scratch_shapes=[pltpu.VMEM(x.shape, x.dtype) for x in operands]
        + [pltpu.SemaphoreType.DMA((3,))],
        compiler_params=pltpu.CompilerParams(vmem_limit_bytes=60 * MIB),
        name="norm_rows",
    )(*operands)


def column_parts(ref):
    step = min(ref.shape[1], 256)
    return [pl.ds(start, step) for start in range(0, ref.shape[1], step)]


def keys_kernel(half, count, *refs):
    blocks = refs[:count]
    weight_ref, panel_ref, mark_ref = refs[count:]
    rows = jnp.concatenate([message_rows(block, half) for block in blocks], axis=0)
    for cols in column_parts(weight_ref):
        product = jnp.dot(rows, weight_ref[:, cols], preferred_element_type=jnp.float32)
        panel_ref[:, cols] = product.astype(jnp.bfloat16)
    mark_ref[...] = product[:8, :LANES]


def project_keys(half, blocks, key_weight):
    row_count = half * len(blocks)
    width = key_weight.shape[1]
    return pl.pallas_call(
        functools.partial(keys_kernel, half, len(blocks)),
        in_specs=[WHOLE] * (len(blocks) + 1),
        out_specs=[WHOLE] * 2,
        out_shape=[
            jax.ShapeDtypeStruct((row_count, width), jnp.bfloat16),
            jax.ShapeDtypeStruct((8, LANES), jnp.float32),
        ],
        compiler_params=pltpu.CompilerParams(vmem_limit_bytes=12 * MIB),
        name="project_keys",
    )(*blocks, key_weight)


def values_kernel(half, offsets, count, experts, mark_ref, keys_ref, *refs):
    blocks = refs[:count]
    value_ref, panel_ref, picked_ref, pos_ref = refs[count:]
    rows = jnp.concatenate([message_rows(block, half) for block in blocks], axis=0)
    tok_count = 2 * half
    expert = lax.axis_index("ctx") // (lax.axis_size("ctx") // experts)
    number = lax.broadcasted_iota(jnp.int32, (tok_count, LANES), 0).astype(jnp.bfloat16)
    for g, offset in enumerate(offsets):
        part = slice(g * tok_count, (g + 1) * tok_count)
        codes = message_codes(blocks[2 * g])
        mine = lax.broadcasted_iota(jnp.int32, codes.shape, 0) == expert
        slot = jnp.sum(jnp.where(mine, codes, 0.0), axis=0, keepdims=True)
        order = lax.broadcasted_iota(jnp.int32, (SLOTS, tok_count), 0).astype(jnp.float32)
        chosen = (order == slot).astype(jnp.bfloat16)
        picked_ref[g] = jnp.dot(
            chosen, rows[part], preferred_element_type=jnp.float32
        ).astype(jnp.bfloat16)
        start = (ring_owner(offset) * lax.axis_size("exp") + lax.axis_index("exp")) * tok_count
        pos_ref[g] = jnp.dot(
            chosen, number, preferred_element_type=jnp.float32
        ) + start.astype(jnp.float32)
    panel_ref[0] = keys_ref[...]
    for cols in column_parts(value_ref):
        panel_ref[1, :, cols] = jnp.dot(
            rows, value_ref[:, cols], preferred_element_type=jnp.float32
        ).astype(jnp.bfloat16)


def project_values(half, blocks, offsets, mark, keys, value_weight):
    row_count = half * len(blocks)
    model_width, width = value_weight.shape
    owners = len(offsets)
    return pl.pallas_call(
        functools.partial(values_kernel, half, offsets, len(blocks), EXPERTS),
        in_specs=[WHOLE] * (len(blocks) + 3),
        out_specs=[WHOLE] * 3,
        out_shape=[
            jax.ShapeDtypeStruct((2, row_count, width), jnp.bfloat16),
            jax.ShapeDtypeStruct((owners, SLOTS, model_width), jnp.bfloat16),
            jax.ShapeDtypeStruct((owners, SLOTS, LANES), jnp.float32),
        ],
        compiler_params=pltpu.CompilerParams(vmem_limit_bytes=12 * MIB),
        name="project_values",
    )(mark, keys, *blocks, value_weight)


def queries_kernel(*refs):
    count = len(refs) // 2 - 1
    picked, weight_ref, outs = refs[:count], refs[count], refs[count + 2 :]
    rows = jnp.concatenate([ref[g] for ref in picked for g in range(ref.shape[0])], axis=0)
    places = [(ref, g) for ref in outs for g in range(ref.shape[0])]
    for cols in column_parts(weight_ref):
        product = jnp.dot(rows, weight_ref[:, cols], preferred_element_type=jnp.float32)
        for i, (ref, g) in enumerate(places):
            ref[g, :, cols] = product[i * SLOTS : (i + 1) * SLOTS].astype(jnp.bfloat16)


def project_queries(picked, query_slab, next_slab):
    model_width, width = query_slab.shape
    owners = sum(rows.shape[0] for rows in picked)
    held = 4 * model_width * width + owners * SLOTS * (4 * model_width + 4 * width)
    return pl.pallas_call(
        queries_kernel,
        in_specs=[WHOLE] * (len(picked) + 2),
        out_specs=[WHOLE] * len(picked),
        out_shape=[
            jax.ShapeDtypeStruct((rows.shape[0], SLOTS, width), jnp.bfloat16) for rows in picked
        ],
        compiler_params=pltpu.CompilerParams(vmem_limit_bytes=held + 6 * MIB),
        name="project_queries",
    )(*picked, query_slab, next_slab)


def arrange_other(panel_ref, offsets, other_ref):
    tok_count = panel_ref.shape[2]
    for g, offset in enumerate(offsets):
        place = ring_owner(offset) * 2 + 1 - lax.axis_index("exp")
        for which in range(2):
            panel_ref[which, place] = other_ref[which, pl.ds(g * tok_count, tok_count)]


def arrange_kernel(plan, *refs):
    count = len(plan)
    own_refs, query_refs, pos_refs = (refs[k * count : (k + 1) * count] for k in range(3))
    other_refs = refs[3 * count : -3]
    panel_ref, queries_ref, places_ref = refs[-3:]
    tok_count = panel_ref.shape[2]
    for offsets, own_ref, query_ref, pos_ref in zip(plan, own_refs, query_refs, pos_refs):
        for g, offset in enumerate(offsets):
            owner = ring_owner(offset)
            for which in range(2):
                panel_ref[which, owner * 2 + lax.axis_index("exp")] = own_ref[
                    which, pl.ds(g * tok_count, tok_count)
                ]
            queries_ref[owner] = query_ref[g].astype(jnp.float32)[:MOST]
            places_ref[owner] = pos_ref[g, :MOST]
    for offsets, other_ref in zip(plan, other_refs):
        arrange_other(panel_ref, offsets, other_ref)


def arrange(owners, plan, own, other, queries, positions):
    width = own[0].shape[2]
    tok_count = own[0].shape[1] // len(plan[0])
    shapes = [
        jax.ShapeDtypeStruct((2, 2 * owners, tok_count, width), jnp.bfloat16),
        jax.ShapeDtypeStruct((owners, MOST, width), jnp.float32),
        jax.ShapeDtypeStruct((owners, MOST, LANES), jnp.float32),
    ]
    operands = (*own, *queries, *positions, *other[:-1])
    panel, queries, places = pl.pallas_call(
        functools.partial(arrange_kernel, plan),
        in_specs=[WHOLE] * len(operands),
        out_specs=[WHOLE] * 3,
        out_shape=shapes,
        compiler_params=pltpu.CompilerParams(vmem_limit_bytes=8 * MIB),
        name="arrange",
    )(*operands)

    def last_kernel(held_ref, other_ref, panel_ref):
        arrange_other(panel_ref, plan[-1], other_ref)

    panel = pl.pallas_call(
        last_kernel,
        in_specs=[WHOLE] * 2,
        out_specs=WHOLE,
        out_shape=shapes[0],
        input_output_aliases={0: 0},
        compiler_params=pltpu.CompilerParams(vmem_limit_bytes=8 * MIB),
        name="arrange_last",
    )(panel, other[-1])
    return panel, queries, places


def attend_kernel(lots, heads, panel_ref, queries_ref, places_ref, weight_ref, *refs):
    outs, (attended, scores, weights) = refs[:-3], refs[-3:]
    first, count = lots
    blocks, tok_count, width = panel_ref.shape[1:]
    rate = math.log2(math.e) / math.sqrt(HS)
    rank = lax.axis_index("ctx")
    tiles = blocks // 4
    tile = 2 * MOST
    parts = 4
    span = blocks * tok_count // parts
    per_span = blocks // parts
    passes = width // (heads * HS)

    def serve(part_id, number, lot, lanes):
        reach = (part_id + 1) * span
        pair = pl.ds(2 * number, 2)
        spots = places_ref[pair].reshape(tile, LANES)
        for h in range(heads):
            held = queries_ref[pair, :, lanes[h]].reshape(tile, HS).astype(jnp.bfloat16)
            for j in range(part_id + 1):
                key_part = panel_ref[0, per_span * j : per_span * (j + 1), :, lanes[h]]
                scores[h, :, pl.ds(j * span, span)] = lax.dot_general(
                    held,
                    key_part.reshape(span, HS),
                    (((1,), (1,)), ((), ())),
                    preferred_element_type=jnp.float32,
                )
        for h in range(heads):
            for sub in range(0, tile, 16):
                rows = pl.ds(sub, 16)
                part = scores[h, rows, pl.ds(0, reach)]
                last = part[:, reach - span :]
                key_index = lax.broadcasted_iota(jnp.int32, last.shape, 1) + (reach - span)
                spot = spots[sub : sub + 16, 0:1]
                last = jnp.where(key_index.astype(jnp.float32) <= spot, last, MASKED)
                if part_id > 0:
                    part = jnp.concatenate([part[:, : reach - span], last], axis=1)
                else:
                    part = last
                peak = jnp.max(part, axis=1, keepdims=True)
                raised = jnp.exp2((part - peak) * rate)
                total = jnp.sum(raised, axis=1, keepdims=True)
                weights[h, rows, pl.ds(0, reach)] = (raised * (1.0 / total)).astype(jnp.bfloat16)
        for h in range(heads):
            total = None
            for j in range(part_id + 1):
                value_part = panel_ref[1, per_span * j : per_span * (j + 1), :, lanes[h]]
                product = jnp.dot(
                    weights[h, :, pl.ds(j * span, span)],
                    value_part.reshape(span, HS),
                    preferred_element_type=jnp.float32,
                )
                total = product if total is None else total + product
            spare = jnp.zeros((SLOTS - MOST, HS), jnp.float32)
            for side in range(2):
                rows = jnp.concatenate([total[side * MOST : (side + 1) * MOST], spare], axis=0)
                attended[2 * lot + (side ^ (rank % 2)), :, lanes[h]] = rows.astype(jnp.bfloat16)

    def one(at, carry):
        lot, now = at // passes, at % passes
        number = (rank // 2) ^ (first + lot)
        lanes = [pl.ds(pl.multiple_of((now * heads + h) * HS, HS), HS) for h in range(heads)]
        for part_id in range(parts):
            pl.when(number // (tiles // parts) == part_id)(
                functools.partial(serve, part_id, number, lot, lanes)
            )
        return carry

    lax.fori_loop(0, count * passes, one, 0)
    rows = attended[...].reshape(2 * count * SLOTS, width)
    for cols in column_parts(weight_ref):
        product = jnp.dot(rows, weight_ref[:, cols], preferred_element_type=jnp.float32)
        for k, out_ref in enumerate(outs):
            out_ref[:, cols] = product[k * SLOTS : k * SLOTS + MOST].astype(jnp.bfloat16)


def attend(lots, panel, queries, places, output_slab):
    first, count = lots
    _, blocks, tok_count, width = panel.shape
    length = blocks * tok_count
    heads = min(8 if first == blocks // 8 else 4, width // HS) if blocks <= 16 else 1
    model_width = output_slab.shape[1]
    held = heads * 2 * SLOTS * length * 6 + 2 * length * width * 2 + width * model_width * 2
    held += 2 * count * SLOTS * (model_width * 8 + width * 2)
    return pl.pallas_call(
        functools.partial(attend_kernel, lots, heads),
        in_specs=[WHOLE] * 4,
        out_specs=[WHOLE] * (2 * count),
        out_shape=[jax.ShapeDtypeStruct((MOST, model_width), jnp.bfloat16)] * (2 * count),
        scratch_shapes=[
            pltpu.VMEM((2 * count, SLOTS, width), jnp.bfloat16),
            pltpu.VMEM((heads, 2 * MOST, length), jnp.float32),
            pltpu.VMEM((heads, 2 * MOST, length), jnp.bfloat16),
        ],
        compiler_params=pltpu.CompilerParams(vmem_limit_bytes=held * 9 // 8 + 4 * MIB),
        cost_estimate=pl.CostEstimate(
            flops=count * 1 * SLOTS * width * (4 * length + 2 * model_width),
            bytes_accessed=4 * length * width,
            transcendentals=count * 2 * SLOTS * length * width // HS,
        ),
        name="attend",
    )(panel, queries, places, output_slab)


def piece_groups(count):
    return [0, *range(count // 2, count)], list(range(count // 2 - 1, 0, -1))


def mix_kernel(quarter_count, top_ref, bottom_ref, router_ref, *refs):
    *mix_refs, slots_ref, gates_ref = refs
    half = LANES // 2
    rows = jnp.concatenate([message_rows(ref, half) for ref in (top_ref, bottom_ref)], axis=0)
    rest, terms = router_ref[...], []
    for _ in range(3):
        terms.append(rest.astype(jnp.bfloat16).astype(jnp.float32))
        rest = rest - terms[-1]
    experts = rest.shape[0]
    router = jnp.concatenate([*terms, jnp.zeros_like(rest)], axis=0).astype(jnp.bfloat16)
    products = lax.dot_general(
        router, rows, (((1,), (1,)), ((), ())), preferred_element_type=jnp.float32
    )
    logits = products[:experts] + (
        products[experts : 2 * experts] + products[2 * experts : 3 * experts]
    )
    slots = message_codes(top_ref)[:experts]
    logits = jnp.where(slots >= 0, logits, -jnp.inf)
    raised = jnp.exp(logits - jnp.max(logits, axis=0, keepdims=True))
    slots_ref[...] = slots
    gates_ref[...] = raised / jnp.sum(raised, axis=0, keepdims=True)
    tok_count = slots.shape[1]
    order = lax.broadcasted_iota(jnp.int32, (SLOTS, tok_count), 0).astype(jnp.float32)
    for mix_ref, group in zip(mix_refs, piece_groups(sum(r.shape[1] for r in mix_refs) // SLOTS)):
        parts = []
        for k in group:
            expert = pl.ds((lax.axis_index("ctx") ^ k) // quarter_count, 1)
            parts.append(jnp.where(order == slots_ref[expert, :], gates_ref[expert, :], 0.0))
        total = jnp.concatenate(parts, axis=0).T
        for part in range(TERMS):
            term = total.astype(jnp.bfloat16)
            mix_ref[pl.ds(part * tok_count, tok_count), :] = term
            total = total - term.astype(jnp.float32)


def gate_mix(quarter_count, halves, router, count):
    tok_count = LANES
    held = pltpu.VMEM((router.shape[0], tok_count), jnp.float32)
    return pl.pallas_call(
        functools.partial(mix_kernel, quarter_count),
        in_specs=[WHOLE] * 3,
        out_specs=[WHOLE] * 2,
        out_shape=[
            jax.ShapeDtypeStruct((TERMS * tok_count, len(group) * SLOTS), jnp.bfloat16)
            for group in piece_groups(count)
        ],
        scratch_shapes=[held, held],
        compiler_params=pltpu.CompilerParams(vmem_limit_bytes=16 * MIB),
        name="gate_mix",
    )(*halves, router)


def combine_kernel(ahead_count, mix_ref, *refs):
    if ahead_count > 0:
        *refs, out_ref, held, sent = refs
    else:
        *refs, held = refs
        out_ref = held
    ahead, pieces = refs[:ahead_count], refs[ahead_count:]
    tok_count, model_width = out_ref.shape
    copies = []
    step = min(model_width, 512)
    spare = jnp.zeros((SLOTS - MOST, step), jnp.float32)
    for start in range(0, model_width, step):
        cols = pl.ds(start, step)
        rows = []
        for piece in pieces:
            rows += [piece[:, cols].astype(jnp.float32), spare]
        rows = jnp.concatenate(rows, axis=0).astype(jnp.bfloat16)
        product = jnp.dot(mix_ref[...], rows, preferred_element_type=jnp.float32)
        total = product[-tok_count:]
        for part in range(TERMS - 2, -1, -1):
            total = product[part * tok_count : (part + 1) * tok_count] + total
        for ref in ahead:
            total = total + ref[:, cols]
        held[:, cols] = total.astype(held.dtype)
        if ahead_count > 0:
            copies.append(
                pltpu.make_async_copy(held.at[:, cols], out_ref.at[:, cols], sent.at[len(copies)])
            )
            copies[-1].start()
    for copy in copies:
        copy.wait()


def combine(mix, pieces, ahead, dtype):
    tok_count = mix.shape[0] // TERMS
    model_width = pieces[0].shape[1]
    scratch = [
        pltpu.VMEM((tok_count, model_width), dtype),
        pltpu.SemaphoreType.DMA((-(-model_width // 512),)),
    ]
    return pl.pallas_call(
        functools.partial(combine_kernel, len(ahead)),
        in_specs=[WHOLE] * (1 + len(ahead) + len(pieces)),
        out_specs=pl.BlockSpec(memory_space=pl.ANY) if ahead else WHOLE,
        out_shape=jax.ShapeDtypeStruct((tok_count, model_width), dtype),
        scratch_shapes=scratch if ahead else [],
        compiler_params=pltpu.CompilerParams(vmem_limit_bytes=24 * MIB),
        name="combine",
    )(mix, *ahead, *pieces)


def per_device(
    tokens, norm_gain, router_weight, routes, key_weight, value_weight, query_weight, output_weight
):
    tok_count, model_width = tokens.shape
    ctx_count = lax.axis_size("ctx")
    exp_count = lax.axis_size("exp")
    quarter_count = ctx_count // EXPERTS
    head_width = query_weight.shape[2]
    ranks = list(range(0, ctx_count, 2)) + list(range(1, ctx_count, 2))[::-1]
    forward = [(ranks[p], ranks[(p + 1) % ctx_count]) for p in range(ctx_count)]
    backward = [(b, a) for a, b in forward]
    sibling = [(e, 1 - e) for e in range(exp_count)]
    query_slab = query_weight[0]
    output_slab = output_weight[0]
    if quarter_count > 1:
        first = (lax.axis_index("ctx") % quarter_count) * head_width
        key_weight = lax.dynamic_slice_in_dim(key_weight, first, head_width, axis=1)
        value_weight = lax.dynamic_slice_in_dim(value_weight, first, head_width, axis=1)

    halves = norm_rows(tokens, norm_gain, routes)
    token_half = tok_count // 2
    steps = ctx_count // 2
    plan = [[0]] + [[-step, step] for step in range(1, steps)] + [[steps]]
    own, other, picked, queries, positions = [], [], [], [], []

    def send(parts):
        return [lax.ppermute(parts[0], "ctx", forward), lax.ppermute(parts[1], "ctx", backward)]

    def hand_over(panel):
        return lax.ppermute(panel, "exp", sibling)

    def tie(*arrays):
        return lax.optimization_barrier(arrays)

    blocks = halves
    lead = send([halves[0], halves[1]])
    rest = send([halves[1], halves[0]])
    for step in range(steps):
        keys, mark = project_keys(token_half, blocks, key_weight)
        following = [lead[0], rest[0], rest[1], lead[1]]
        if step == steps - 2:
            queries = project_queries(picked, query_slab, output_slab)
            picked = []
        if step < steps - 1:
            mark, *lead_next = tie(mark, *lead, *queries)
            queries = lead_next[2:]
            lead = send(lead_next[:2])
        panel, rows, position = project_values(token_half, blocks, plan[step], mark, keys, value_weight)
        if step < steps - 2:
            position, *rest_next = tie(position, *rest)
            rest = send(rest_next)
        own.append(panel)
        picked.append(rows)
        positions.append(position)
        if step < steps - 1:
            other.append(hand_over(panel))
        blocks = following
    queries = [*queries, *project_queries(picked, query_slab, output_slab)]
    own[-1], queries[-1], other[0], *blocks = tie(own[-1], queries[-1], other[0], *lead)
    other.append(hand_over(own[-1]))
    keys, mark = project_keys(token_half, blocks, key_weight)
    panel, rows, position = project_values(token_half, blocks, plan[-1], mark, keys, value_weight)
    own.append(panel)
    other.append(hand_over(panel))
    positions.append(position)
    queries = [*queries, *project_queries([rows], query_slab, output_slab)]
    held = arrange(ctx_count, plan, own, other, queries, positions)

    def swap(piece, k):
        return lax.ppermute(piece, "ctx", [(c, c ^ k) for c in range(ctx_count)])

    half, quarter = ctx_count // 2, ctx_count // 4
    far, mine = [], []
    for start, count in ((half, quarter), (half + quarter, quarter), (0, half)):
        pieces = attend((start // 2, count // 2), *held, output_slab)
        if start > 0:
            places, *pieces = tie(held[2], *pieces)
            held = [*held[:2], places]
            far.append([swap(piece, start + r) for r, piece in enumerate(pieces)])
        else:
            near = pieces
    near = list(near)
    *near[:-1], far[0][0] = tie(*near[:-1], far[0][0])
    near = [near[0]] + [swap(near[r], r) for r in range(1, half)]

    pieces = [*near, *far[0], *far[1]]
    early, late = piece_groups(ctx_count)
    early_mix, late_mix = gate_mix(quarter_count, halves, router_weight.T, ctx_count)
    ahead = combine(early_mix, [pieces[k] for k in early], [], jnp.float32)
    return combine(late_mix, [pieces[k] for k in late], [ahead], jnp.bfloat16)


def solution(mesh):
    in_specs = (
        P(("groups", "ctx", "exp"), None),
        P(),
        P(),
        P(("groups", "ctx", "exp"), None),
        P(),
        P(),
        P("ctx", None, None),
        P("ctx", None, None),
    )
    out_specs = P(("groups", "ctx", "exp"), None)
    return jax.shard_map(
        per_device, mesh=mesh, in_specs=in_specs, out_specs=out_specs, check_vma=False
    )
```

```python
import functools
import math

import jax
import jax.numpy as jnp
from jax import lax
from jax.experimental import pallas as pl
from jax.experimental.pallas import tpu as pltpu
from jax.sharding import PartitionSpec as P

HS = 128
EXPERTS = 8
MOST = 40
SLOTS = 48
MASKED = -1e30
LANES = 128
CODES = 16
TERMS = 2
PART = 256
MIB = 1 << 20
WHOLE = pl.BlockSpec(memory_space=pltpu.VMEM)


def ring_rank(place, count):
    place = lax.rem(place + 2 * count, count)
    return jnp.where(place < count // 2, 2 * place, 2 * (count - 1 - place) + 1)


def ring_place(rank, count):
    return jnp.where(rank % 2 == 0, rank // 2, count - 1 - rank // 2)


def ring_owner(offset):
    count = lax.axis_size("ctx")
    return ring_rank(ring_place(lax.axis_index("ctx"), count) + offset, count)


def norm_kernel(*refs):
    sources, top_ref, bottom_ref, *held, arrivals = refs[:3], *refs[3:]
    copies = [
        pltpu.make_async_copy(source, target, arrivals.at[i])
        for i, (source, target) in enumerate(zip(sources, held))
    ]
    for copy in copies:
        copy.start()
    for copy in copies:
        copy.wait()
    tokens_ref, gain_ref, routes_ref = held
    floats = tokens_ref[...].astype(jnp.float32)
    count, width = floats.shape
    factor = lax.rsqrt(jnp.mean(floats * floats, axis=1, keepdims=True) + 1e-06)
    normed = (floats * factor * gain_ref[...]).astype(jnp.bfloat16)
    expert = lax.broadcasted_iota(jnp.int32, (CODES, count), 0)
    named = (expert == routes_ref[0:1, :]) | (expert == routes_ref[1:2, :])
    before = lax.broadcasted_iota(jnp.int32, (count, count), 0) < lax.broadcasted_iota(
        jnp.int32, (count, count), 1
    )
    rank = jnp.dot(
        named.astype(jnp.bfloat16),
        before.astype(jnp.bfloat16),
        preferred_element_type=jnp.float32,
    )
    codes = jnp.where(named, rank, -1.0).astype(jnp.bfloat16)
    half = count // 2
    for ref, first in ((top_ref, 0), (bottom_ref, half)):
        for c in range(width // LANES):
            ref[pl.ds(c * half, half), :] = normed[
                first : first + half, c * LANES : (c + 1) * LANES
            ]
        ref[pl.ds(width // LANES * half, CODES), :] = codes


def message_rows(ref, half):
    tiles = (ref.shape[0] - CODES) // half
    return jnp.concatenate([ref[pl.ds(c * half, half), :] for c in range(tiles)], axis=1)


def message_codes(ref):
    return ref[pl.ds(ref.shape[0] - CODES, CODES), :].astype(jnp.float32)


def norm_rows(tokens, norm_gain, routes):
    count, width = tokens.shape
    half = jax.ShapeDtypeStruct((width // LANES * (count // 2) + CODES, LANES), jnp.bfloat16)
    operands = (tokens, norm_gain.reshape(1, -1), routes.T)
    return pl.pallas_call(
        norm_kernel,
        in_specs=[pl.BlockSpec(memory_space=pltpu.HBM)] * 3,
        out_specs=[WHOLE] * 2,
        out_shape=[half, half],
        scratch_shapes=[pltpu.VMEM(x.shape, x.dtype) for x in operands]
        + [pltpu.SemaphoreType.DMA((3,))],
        compiler_params=pltpu.CompilerParams(vmem_limit_bytes=60 * MIB),
        name="norm_rows",
    )(*operands)


def column_parts(ref):
    step = min(ref.shape[1], 256)
    return [pl.ds(start, step) for start in range(0, ref.shape[1], step)]


def keys_kernel(half, count, *refs):
    blocks = refs[:count]
    weight_ref, panel_ref, mark_ref = refs[count:]
    rows = jnp.concatenate([message_rows(block, half) for block in blocks], axis=0)
    for cols in column_parts(weight_ref):
        product = jnp.dot(rows, weight_ref[:, cols], preferred_element_type=jnp.float32)
        panel_ref[:, cols] = product.astype(jnp.bfloat16)
    mark_ref[...] = product[:8, :LANES]


def project_keys(half, blocks, key_weight):
    row_count = half * len(blocks)
    width = key_weight.shape[1]
    return pl.pallas_call(
        functools.partial(keys_kernel, half, len(blocks)),
        in_specs=[WHOLE] * (len(blocks) + 1),
        out_specs=[WHOLE] * 2,
        out_shape=[
            jax.ShapeDtypeStruct((row_count, width), jnp.bfloat16),
            jax.ShapeDtypeStruct((8, LANES), jnp.float32),
        ],
        compiler_params=pltpu.CompilerParams(vmem_limit_bytes=12 * MIB),
        name="project_keys",
    )(*blocks, key_weight)


def values_kernel(half, offsets, count, experts, mark_ref, keys_ref, *refs):
    blocks = refs[:count]
    value_ref, panel_ref, picked_ref, pos_ref = refs[count:]
    rows = jnp.concatenate([message_rows(block, half) for block in blocks], axis=0)
    tok_count = 2 * half
    expert = lax.axis_index("ctx") // (lax.axis_size("ctx") // experts)
    number = lax.broadcasted_iota(jnp.int32, (tok_count, LANES), 0).astype(jnp.bfloat16)
    for g, offset in enumerate(offsets):
        part = slice(g * tok_count, (g + 1) * tok_count)
        codes = message_codes(blocks[2 * g])
        mine = lax.broadcasted_iota(jnp.int32, codes.shape, 0) == expert
        slot = jnp.sum(jnp.where(mine, codes, 0.0), axis=0, keepdims=True)
        order = lax.broadcasted_iota(jnp.int32, (SLOTS, tok_count), 0).astype(jnp.float32)
        chosen = (order == slot).astype(jnp.bfloat16)
        picked_ref[g] = jnp.dot(
            chosen, rows[part], preferred_element_type=jnp.float32
        ).astype(jnp.bfloat16)
        start = (ring_owner(offset) * lax.axis_size("exp") + lax.axis_index("exp")) * tok_count
        pos_ref[g] = jnp.dot(
            chosen, number, preferred_element_type=jnp.float32
        ) + start.astype(jnp.float32)
    panel_ref[0] = keys_ref[...]
    for cols in column_parts(value_ref):
        panel_ref[1, :, cols] = jnp.dot(
            rows, value_ref[:, cols], preferred_element_type=jnp.float32
        ).astype(jnp.bfloat16)


def project_values(half, blocks, offsets, mark, keys, value_weight):
    row_count = half * len(blocks)
    model_width, width = value_weight.shape
    owners = len(offsets)
    return pl.pallas_call(
        functools.partial(values_kernel, half, offsets, len(blocks), EXPERTS),
        in_specs=[WHOLE] * (len(blocks) + 3),
        out_specs=[WHOLE] * 3,
        out_shape=[
            jax.ShapeDtypeStruct((2, row_count, width), jnp.bfloat16),
            jax.ShapeDtypeStruct((owners, SLOTS, model_width), jnp.bfloat16),
            jax.ShapeDtypeStruct((owners, SLOTS, LANES), jnp.float32),
        ],
        compiler_params=pltpu.CompilerParams(vmem_limit_bytes=12 * MIB),
        name="project_values",
    )(mark, keys, *blocks, value_weight)


def queries_kernel(*refs):
    count = len(refs) // 2 - 1
    picked, weight_ref, outs = refs[:count], refs[count], refs[count + 2 :]
    rows = jnp.concatenate([ref[g] for ref in picked for g in range(ref.shape[0])], axis=0)
    places = [(ref, g) for ref in outs for g in range(ref.shape[0])]
    for cols in column_parts(weight_ref):
        product = jnp.dot(rows, weight_ref[:, cols], preferred_element_type=jnp.float32)
        for i, (ref, g) in enumerate(places):
            ref[g, :, cols] = product[i * SLOTS : (i + 1) * SLOTS].astype(jnp.bfloat16)


def project_queries(picked, query_slab, next_slab):
    model_width, width = query_slab.shape
    owners = sum(rows.shape[0] for rows in picked)
    held = 4 * model_width * width + owners * SLOTS * (4 * model_width + 4 * width)
    return pl.pallas_call(
        queries_kernel,
        in_specs=[WHOLE] * (len(picked) + 2),
        out_specs=[WHOLE] * len(picked),
        out_shape=[
            jax.ShapeDtypeStruct((rows.shape[0], SLOTS, width), jnp.bfloat16) for rows in picked
        ],
        compiler_params=pltpu.CompilerParams(vmem_limit_bytes=held + 6 * MIB),
        name="project_queries",
    )(*picked, query_slab, next_slab)


def arrange_other(panel_ref, offsets, other_ref):
    tok_count = panel_ref.shape[2]
    for g, offset in enumerate(offsets):
        place = ring_owner(offset) * 2 + 1 - lax.axis_index("exp")
        for which in range(2):
            panel_ref[which, place] = other_ref[which, pl.ds(g * tok_count, tok_count)]


def arrange_kernel(plan, *refs):
    count = len(plan)
    own_refs, query_refs, pos_refs = (refs[k * count : (k + 1) * count] for k in range(3))
    other_refs = refs[3 * count : -3]
    panel_ref, queries_ref, places_ref = refs[-3:]
    tok_count = panel_ref.shape[2]
    for offsets, own_ref, query_ref, pos_ref in zip(plan, own_refs, query_refs, pos_refs):
        for g, offset in enumerate(offsets):
            owner = ring_owner(offset)
            for which in range(2):
                panel_ref[which, owner * 2 + lax.axis_index("exp")] = own_ref[
                    which, pl.ds(g * tok_count, tok_count)
                ]
            queries_ref[owner] = query_ref[g].astype(jnp.float32)[:MOST]
            places_ref[owner] = pos_ref[g, :MOST]
    for offsets, other_ref in zip(plan, other_refs):
        arrange_other(panel_ref, offsets, other_ref)


def arrange(owners, plan, own, other, queries, positions):
    width = own[0].shape[2]
    tok_count = own[0].shape[1] // len(plan[0])
    shapes = [
        jax.ShapeDtypeStruct((2, 2 * owners, tok_count, width), jnp.bfloat16),
        jax.ShapeDtypeStruct((owners, MOST, width), jnp.float32),
        jax.ShapeDtypeStruct((owners, MOST, LANES), jnp.float32),
    ]
    operands = (*own, *queries, *positions, *other[:-1])
    panel, queries, places = pl.pallas_call(
        functools.partial(arrange_kernel, plan),
        in_specs=[WHOLE] * len(operands),
        out_specs=[WHOLE] * 3,
        out_shape=shapes,
        compiler_params=pltpu.CompilerParams(vmem_limit_bytes=8 * MIB),
        name="arrange",
    )(*operands)

    def last_kernel(held_ref, other_ref, panel_ref):
        arrange_other(panel_ref, plan[-1], other_ref)

    panel = pl.pallas_call(
        last_kernel,
        in_specs=[WHOLE] * 2,
        out_specs=WHOLE,
        out_shape=shapes[0],
        input_output_aliases={0: 0},
        compiler_params=pltpu.CompilerParams(vmem_limit_bytes=8 * MIB),
        name="arrange_last",
    )(panel, other[-1])
    return panel, queries, places


def attend_kernel(lots, heads, panel_ref, queries_ref, places_ref, weight_ref, *refs):
    outs, (attended, scores, weights) = refs[:-3], refs[-3:]
    first, count = lots
    blocks, tok_count, width = panel_ref.shape[1:]
    rate = math.log2(math.e) / math.sqrt(HS)
    rank = lax.axis_index("ctx")
    tiles = blocks // 4
    tile = 2 * MOST
    parts = 4
    span = blocks * tok_count // parts
    per_span = blocks // parts
    passes = width // (heads * HS)

    def serve(part_id, number, lot, lanes):
        reach = (part_id + 1) * span
        pair = pl.ds(2 * number, 2)
        spots = places_ref[pair].reshape(tile, LANES)
        for h in range(heads):
            held = queries_ref[pair, :, lanes[h]].reshape(tile, HS).astype(jnp.bfloat16)
            for j in range(part_id + 1):
                key_part = panel_ref[0, per_span * j : per_span * (j + 1), :, lanes[h]]
                scores[h, :, pl.ds(j * span, span)] = lax.dot_general(
                    held,
                    key_part.reshape(span, HS),
                    (((1,), (1,)), ((), ())),
                    preferred_element_type=jnp.float32,
                )
        for h in range(heads):
            for sub in range(0, tile, 16):
                rows = pl.ds(sub, 16)
                part = scores[h, rows, pl.ds(0, reach)]
                last = part[:, reach - span :]
                key_index = lax.broadcasted_iota(jnp.int32, last.shape, 1) + (reach - span)
                spot = spots[sub : sub + 16, 0:1]
                last = jnp.where(key_index.astype(jnp.float32) <= spot, last, MASKED)
                if part_id > 0:
                    part = jnp.concatenate([part[:, : reach - span], last], axis=1)
                else:
                    part = last
                peak = jnp.max(part, axis=1, keepdims=True)
                raised = jnp.exp2((part - peak) * rate)
                total = jnp.sum(raised, axis=1, keepdims=True)
                weights[h, rows, pl.ds(0, reach)] = (raised * (1.0 / total)).astype(jnp.bfloat16)
        for h in range(heads):
            total = None
            for j in range(part_id + 1):
                value_part = panel_ref[1, per_span * j : per_span * (j + 1), :, lanes[h]]
                product = jnp.dot(
                    weights[h, :, pl.ds(j * span, span)],
                    value_part.reshape(span, HS),
                    preferred_element_type=jnp.float32,
                )
                total = product if total is None else total + product
            spare = jnp.zeros((SLOTS - MOST, HS), jnp.float32)
            for side in range(2):
                rows = jnp.concatenate([total[side * MOST : (side + 1) * MOST], spare], axis=0)
                attended[2 * lot + (side ^ (rank % 2)), :, lanes[h]] = rows.astype(jnp.bfloat16)

    def one(at, carry):
        lot, now = at // passes, at % passes
        number = (rank // 2) ^ (first + lot)
        lanes = [pl.ds(pl.multiple_of((now * heads + h) * HS, HS), HS) for h in range(heads)]
        for part_id in range(parts):
            pl.when(number // (tiles // parts) == part_id)(
                functools.partial(serve, part_id, number, lot, lanes)
            )
        return carry

    lax.fori_loop(0, count * passes, one, 0)
    rows = attended[...].reshape(2 * count * SLOTS, width)
    for cols in column_parts(weight_ref):
        product = jnp.dot(rows, weight_ref[:, cols], preferred_element_type=jnp.float32)
        for k, out_ref in enumerate(outs):
            out_ref[:, cols] = product[k * SLOTS : k * SLOTS + MOST].astype(jnp.bfloat16)


def attend(lots, panel, queries, places, output_slab):
    first, count = lots
    _, blocks, tok_count, width = panel.shape
    length = blocks * tok_count
    heads = min(8 if first == blocks // 8 else 4, width // HS) if blocks <= 16 else 1
    model_width = output_slab.shape[1]
    held = heads * 2 * SLOTS * length * 6 + 2 * length * width * 2 + width * model_width * 2
    held += 2 * count * SLOTS * (model_width * 8 + width * 2)
    return pl.pallas_call(
        functools.partial(attend_kernel, lots, heads),
        in_specs=[WHOLE] * 4,
        out_specs=[WHOLE] * (2 * count),
        out_shape=[jax.ShapeDtypeStruct((MOST, model_width), jnp.bfloat16)] * (2 * count),
        scratch_shapes=[
            pltpu.VMEM((2 * count, SLOTS, width), jnp.bfloat16),
            pltpu.VMEM((heads, 2 * MOST, length), jnp.float32),
            pltpu.VMEM((heads, 2 * MOST, length), jnp.bfloat16),
        ],
        compiler_params=pltpu.CompilerParams(vmem_limit_bytes=held * 9 // 8 + 4 * MIB),
        cost_estimate=pl.CostEstimate(
            flops=count * 1 * SLOTS * width * (4 * length + 2 * model_width),
            bytes_accessed=4 * length * width,
            transcendentals=count * 2 * SLOTS * length * width // HS,
        ),
        name="attend",
    )(panel, queries, places, output_slab)


def piece_groups(count):
    return [0, *range(count // 2, count)], list(range(count // 2 - 1, 0, -1))


def mix_kernel(quarter_count, top_ref, bottom_ref, router_ref, *refs):
    *mix_refs, slots_ref, gates_ref = refs
    half = LANES // 2
    rows = jnp.concatenate([message_rows(ref, half) for ref in (top_ref, bottom_ref)], axis=0)
    rest, terms = router_ref[...], []
    for _ in range(3):
        terms.append(rest.astype(jnp.bfloat16).astype(jnp.float32))
        rest = rest - terms[-1]
    experts = rest.shape[0]
    router = jnp.concatenate([*terms, jnp.zeros_like(rest)], axis=0).astype(jnp.bfloat16)
    products = lax.dot_general(
        router, rows, (((1,), (1,)), ((), ())), preferred_element_type=jnp.float32
    )
    logits = products[:experts] + (
        products[experts : 2 * experts] + products[2 * experts : 3 * experts]
    )
    slots = message_codes(top_ref)[:experts]
    logits = jnp.where(slots >= 0, logits, -jnp.inf)
    raised = jnp.exp(logits - jnp.max(logits, axis=0, keepdims=True))
    slots_ref[...] = slots
    gates_ref[...] = raised / jnp.sum(raised, axis=0, keepdims=True)
    tok_count = slots.shape[1]
    order = lax.broadcasted_iota(jnp.int32, (SLOTS, tok_count), 0).astype(jnp.float32)
    for mix_ref, group in zip(mix_refs, piece_groups(sum(r.shape[1] for r in mix_refs) // SLOTS)):
        parts = []
        for k in group:
            expert = pl.ds((lax.axis_index("ctx") ^ k) // quarter_count, 1)
            parts.append(jnp.where(order == slots_ref[expert, :], gates_ref[expert, :], 0.0))
        total = jnp.concatenate(parts, axis=0).T
        for part in range(TERMS):
            term = total.astype(jnp.bfloat16)
            mix_ref[pl.ds(part * tok_count, tok_count), :] = term
            total = total - term.astype(jnp.float32)


def gate_mix(quarter_count, halves, router, count):
    tok_count = LANES
    held = pltpu.VMEM((router.shape[0], tok_count), jnp.float32)
    return pl.pallas_call(
        functools.partial(mix_kernel, quarter_count),
        in_specs=[WHOLE] * 3,
        out_specs=[WHOLE] * 2,
        out_shape=[
            jax.ShapeDtypeStruct((TERMS * tok_count, len(group) * SLOTS), jnp.bfloat16)
            for group in piece_groups(count)
        ],
        scratch_shapes=[held, held],
        compiler_params=pltpu.CompilerParams(vmem_limit_bytes=16 * MIB),
        name="gate_mix",
    )(*halves, router)


def combine_kernel(ahead_count, mix_ref, *refs):
    if ahead_count > 0:
        *refs, out_ref, held, sent = refs
    else:
        *refs, held = refs
        out_ref = held
    ahead, pieces = refs[:ahead_count], refs[ahead_count:]
    tok_count, model_width = out_ref.shape
    copies = []
    step = min(model_width, PART)
    spare = jnp.zeros((SLOTS - MOST, step), jnp.float32)
    for start in range(0, model_width, step):
        cols = pl.ds(start, step)
        rows = []
        for piece in pieces:
            rows += [piece[:, cols].astype(jnp.float32), spare]
        rows = jnp.concatenate(rows, axis=0).astype(jnp.bfloat16)
        product = jnp.dot(mix_ref[...], rows, preferred_element_type=jnp.float32)
        total = product[-tok_count:]
        for part in range(TERMS - 2, -1, -1):
            total = product[part * tok_count : (part + 1) * tok_count] + total
        for ref in ahead:
            total = total + ref[:, cols]
        held[:, cols] = total.astype(held.dtype)
        if ahead_count > 0:
            copies.append(
                pltpu.make_async_copy(held.at[:, cols], out_ref.at[:, cols], sent.at[len(copies)])
            )
            copies[-1].start()
    for copy in copies:
        copy.wait()


def combine(mix, pieces, ahead, dtype):
    tok_count = mix.shape[0] // TERMS
    model_width = pieces[0].shape[1]
    scratch = [
        pltpu.VMEM((tok_count, model_width), dtype),
        pltpu.SemaphoreType.DMA((-(-model_width // PART),)),
    ]
    return pl.pallas_call(
        functools.partial(combine_kernel, len(ahead)),
        in_specs=[WHOLE] * (1 + len(ahead) + len(pieces)),
        out_specs=pl.BlockSpec(memory_space=pl.ANY) if ahead else WHOLE,
        out_shape=jax.ShapeDtypeStruct((tok_count, model_width), dtype),
        scratch_shapes=scratch if ahead else [],
        compiler_params=pltpu.CompilerParams(vmem_limit_bytes=24 * MIB),
        name="combine",
    )(mix, *ahead, *pieces)


def per_device(
    tokens, norm_gain, router_weight, routes, key_weight, value_weight, query_weight, output_weight
):
    tok_count, model_width = tokens.shape
    ctx_count = lax.axis_size("ctx")
    exp_count = lax.axis_size("exp")
    quarter_count = ctx_count // EXPERTS
    head_width = query_weight.shape[2]
    ranks = list(range(0, ctx_count, 2)) + list(range(1, ctx_count, 2))[::-1]
    forward = [(ranks[p], ranks[(p + 1) % ctx_count]) for p in range(ctx_count)]
    backward = [(b, a) for a, b in forward]
    sibling = [(e, 1 - e) for e in range(exp_count)]
    query_slab = query_weight[0]
    output_slab = output_weight[0]
    if quarter_count > 1:
        first = (lax.axis_index("ctx") % quarter_count) * head_width
        key_weight = lax.dynamic_slice_in_dim(key_weight, first, head_width, axis=1)
        value_weight = lax.dynamic_slice_in_dim(value_weight, first, head_width, axis=1)

    halves = norm_rows(tokens, norm_gain, routes)
    token_half = tok_count // 2
    steps = ctx_count // 2
    plan = [[0]] + [[-step, step] for step in range(1, steps)] + [[steps]]
    own, other, picked, queries, positions = [], [], [], [], []

    def send(parts):
        return [lax.ppermute(parts[0], "ctx", forward), lax.ppermute(parts[1], "ctx", backward)]

    def hand_over(panel):
        return lax.ppermute(panel, "exp", sibling)

    def tie(*arrays):
        return lax.optimization_barrier(arrays)

    blocks = halves
    lead = send([halves[0], halves[1]])
    rest = send([halves[1], halves[0]])
    for step in range(steps):
        keys, mark = project_keys(token_half, blocks, key_weight)
        following = [lead[0], rest[0], rest[1], lead[1]]
        if step == steps - 2:
            queries = project_queries(picked, query_slab, output_slab)
            picked = []
        if step < steps - 1:
            mark, *lead_next = tie(mark, *lead, *queries)
            queries = lead_next[2:]
            lead = send(lead_next[:2])
        panel, rows, position = project_values(token_half, blocks, plan[step], mark, keys, value_weight)
        if step < steps - 2:
            position, *rest_next = tie(position, *rest)
            rest = send(rest_next)
        own.append(panel)
        picked.append(rows)
        positions.append(position)
        if step < steps - 1:
            other.append(hand_over(panel))
        blocks = following
    queries = [*queries, *project_queries(picked, query_slab, output_slab)]
    own[-1], queries[-1], other[0], *blocks = tie(own[-1], queries[-1], other[0], *lead)
    other.append(hand_over(own[-1]))
    keys, mark = project_keys(token_half, blocks, key_weight)
    panel, rows, position = project_values(token_half, blocks, plan[-1], mark, keys, value_weight)
    own.append(panel)
    other.append(hand_over(panel))
    positions.append(position)
    queries = [*queries, *project_queries([rows], query_slab, output_slab)]
    held = arrange(ctx_count, plan, own, other, queries, positions)

    def swap(piece, k):
        return lax.ppermute(piece, "ctx", [(c, c ^ k) for c in range(ctx_count)])

    half, quarter = ctx_count // 2, ctx_count // 4
    far, mine = [], []
    for start, count in ((half, quarter), (half + quarter, quarter), (0, half)):
        pieces = attend((start // 2, count // 2), *held, output_slab)
        if start > 0:
            places, *pieces = tie(held[2], *pieces)
            held = [*held[:2], places]
            far.append([swap(piece, start + r) for r, piece in enumerate(pieces)])
        else:
            near = pieces
    near = list(near)
    *near[:-1], far[0][0] = tie(*near[:-1], far[0][0])
    near = [near[0]] + [swap(near[r], r) for r in range(1, half)]

    pieces = [*near, *far[0], *far[1]]
    early, late = piece_groups(ctx_count)
    early_mix, late_mix = gate_mix(quarter_count, halves, router_weight.T, ctx_count)
    ahead = combine(early_mix, [pieces[k] for k in early], [], jnp.float32)
    return combine(late_mix, [pieces[k] for k in late], [ahead], jnp.bfloat16)


def solution(mesh):
    in_specs = (
        P(("groups", "ctx", "exp"), None),
        P(),
        P(),
        P(("groups", "ctx", "exp"), None),
        P(),
        P(),
        P("ctx", None, None),
        P("ctx", None, None),
    )
    out_specs = P(("groups", "ctx", "exp"), None)
    return jax.shard_map(
        per_device, mesh=mesh, in_specs=in_specs, out_specs=out_specs, check_vma=False
    )
```
